256 devices in a mesh: lat: 4 (over y_lo, core), lon: 64 (over x, z, y_hi).
Axes of the slice: x: 4, y: 4 (y_hi: 2, y_lo: 2; y = y_hi * 2 + y_lo), z: 8, core: 2. Of those that a mesh axis runs over, the one named last changes fastest.
Arguments:
- activation: float32 [64, 768, 640], P('lat', 'lon'), may hold values from -6 to 6
- cotangent: float32 [64, 768, 640], P('lat', 'lon'), may hold values from -6 to 6
- weight_in: float32 [1280, 640], replicated, may hold values from -0.25 to 0.25
- weight_out: float32 [1280, 640], replicated, may hold values from -0.15625 to 0.15625
- kernels: float32 [3, 64, 7, 768], P(None, 'lat'), may hold values from -0.21875 to 0.21875
- mixing: float32 [640, 3], P('lon'), may hold values from -3.5 to 3.5
Outputs:
- field_grad: float32 [64, 768, 640], P('lat', 'lon')
- grad_in: float32 [1280, 640], P('lon', 'lat')
- grad_out: float32 [1280, 640], P('lon', 'lat')
The draws below stay inside these ranges and needn't reach their ends.
All inputs are finite; a program needn't handle non-finite values.
Results may differ from the reference program's by a relative error of at most 0.0001.
Values sent between devices are 32-bit elements; how exact they have to be, the bound alone decides.
No kernel may reach another device: no remote copies, remote signals or barrier semaphores. Data moves between devices by JAX's collectives and lax.ppermute only.
A program may use at most 128 MiB of HBM per device.

```python
import math
import jax
import jax.numpy as jnp
from jax import lax

D = 640
H = 1280
NLON = 768
KLAT = 7
BASIS = 3
NLAT = 64


def shard_levels(own_key, shape, shards, smallest, high):
    def one(axis_at, parts):
        heights = jax.random.uniform(jax.random.fold_in(jax.random.fold_in(own_key, 6), axis_at), (parts,), jnp.float32, smallest / len(shards), high / len(shards))
        return jnp.repeat(jnp.exp(heights), shape[axis_at] // parts).reshape((-1,) + (1,) * (len(shape) - axis_at - 1))

    factor_of = one(*shards[0])
    for cut in shards[1:]:
        factor_of = factor_of * one(*cut)
    return factor_of


def gaussian(rng, shape, spread, bound, cuts=(), kind=jnp.bfloat16):
    entries = spread * jax.random.normal(rng, shape, jnp.float32)
    if cuts:
        entries = entries * shard_levels(rng, shape, cuts, -0.22, 0.18)
    return jnp.clip(entries, -bound, bound).astype(kind)


def setup_inputs(seed: int = 0) -> dict:
    splits = jax.random.split(jax.random.key(seed), 7)
    return {
        "activation": gaussian(splits[0], (NLAT, NLON, D), 1.0, 6.0, ((0, 4), (1, 64)), jnp.float32),
        "cotangent": gaussian(splits[1], (NLAT, NLON, D), 1.0, 6.0, ((0, 4), (1, 64)), jnp.float32),
        "weight_in": gaussian(splits[2], (H, D), D ** -0.5, 0.25, (), jnp.float32),
        "weight_out": gaussian(splits[3], (H, D), H ** -0.5, 0.15625, (), jnp.float32),
        "kernels": gaussian(splits[4], (BASIS, NLAT, KLAT, NLON), 0.0137, 0.21875, ((1, 4),), jnp.float32),
        "mixing": gaussian(splits[5], (D, BASIS), BASIS ** -0.5, 3.5, ((0, 64),), jnp.float32),
    }


def gelu_parts(preact):
    normal_cdf = 0.5 * (1.0 + jax.scipy.special.erf(preact / math.sqrt(2.0)))
    density = jnp.exp(-0.5 * preact * preact) / math.sqrt(2.0 * math.pi)
    return (preact * normal_cdf, normal_cdf + preact * density)

def reference(activation, cotangent, weight_in, weight_out, kernels, mixing):
    high = lax.Precision.HIGHEST

    def latitude(carry, pieces):
        act_row, cot_row = pieces
        preact = jnp.dot(act_row, weight_in.T, precision=high, preferred_element_type=jnp.float32)
        hidden, slope = gelu_parts(preact)
        hidden_grad = jnp.dot(cot_row, weight_out.T, precision=high, preferred_element_type=jnp.float32) * slope
        unit_row = cot_row + jnp.dot(hidden_grad, weight_in, precision=high, preferred_element_type=jnp.float32)
        acc_in = carry[0] + jnp.dot(hidden_grad.T, act_row, precision=high, preferred_element_type=jnp.float32)
        acc_out = carry[1] + jnp.dot(hidden.T, cot_row, precision=high, preferred_element_type=jnp.float32)
        return ((acc_in, acc_out), unit_row)
    zeros = jnp.zeros(weight_in.shape, jnp.float32)
    (grad_in, grad_out), unit_grad = lax.scan(latitude, (zeros, zeros), (activation, cotangent))
    spectrum = jnp.fft.rfft(unit_grad, axis=1)
    spec_real = jnp.pad(spectrum.real, ((3, 3), (0, 0), (0, 0)))
    spec_imag = jnp.pad(spectrum.imag, ((3, 3), (0, 0), (0, 0)))
    kernel_spec = jnp.fft.rfft(kernels, axis=-1)
    kernel_real = kernel_spec.real
    kernel_imag = kernel_spec.imag
    total_real = jnp.zeros(spectrum.shape, spec_real.dtype)
    total_imag = jnp.zeros(spectrum.shape, spec_real.dtype)
    for offset in range(KLAT):
        part_real = jnp.einsum('cb,bjf->jfc', mixing, kernel_real[:, :, offset], precision=high)
        part_imag = jnp.einsum('cb,bjf->jfc', mixing, kernel_imag[:, :, offset], precision=high)
        shifted_real = spec_real[6 - offset:6 - offset + NLAT]
        shifted_imag = spec_imag[6 - offset:6 - offset + NLAT]
        total_real = total_real + part_real * shifted_real + part_imag * shifted_imag
        total_imag = total_imag + part_real * shifted_imag - part_imag * shifted_real
    field_grad = jnp.fft.irfft(total_real + 1j * total_imag, n=NLON, axis=1)
    return (field_grad.astype(activation.dtype), grad_in, grad_out)
```

```python
import functools
import math

import jax
import jax.numpy as jnp
import ml_dtypes
import numpy as np
from jax import lax
from jax.experimental import pallas as pl
from jax.experimental.pallas import tpu as pltpu
from jax.sharding import Mesh
from jax.sharding import PartitionSpec as P

AXES = ("yl", "co", "x", "z", "yh")
LAT = ("yl", "co")
LON = ("x", "z", "yh")
F32 = jnp.float32
BF16 = jnp.bfloat16
SHARDS = 64
COLS = 12
ROWS = 16
OWN = 10
CIRCLE = 768
HALF = 384
TAPS = 7
BASIS = 3
MIB = 1 << 20


def split(value):
    top = value.astype(BF16)
    return top, (value - top.astype(F32)).astype(BF16)


def dot3(left, right, dims):
    (a, b), (c, d) = left, right
    numbers = (dims, ((), ()))
    one = functools.partial(lax.dot_general, dimension_numbers=numbers, preferred_element_type=F32)
    return one(a, c) + (one(a, d) + one(b, c))


def whole(n):
    return [pl.BlockSpec(memory_space=pltpu.VMEM)] * n


def params(mib):
    return pltpu.CompilerParams(vmem_limit_bytes=mib * MIB)


def cost(flops, moved):
    return pl.CostEstimate(flops=flops, bytes_accessed=moved, transcendentals=0)


def table(order):
    angle = 2.0 * np.pi / CIRCLE * (order[:, None] * np.arange(HALF)[None, :] % CIRCLE)
    nyquist = np.where(order % 2 == 0, 1.0, -1.0)
    real, imag = np.cos(angle), -np.sin(angle)
    imag[:, 0] = nyquist
    return np.concatenate([real, imag], axis=1)


def parts(matrix):
    exact = matrix.astype(np.float32)
    top = exact.astype(ml_dtypes.bfloat16)
    return top, (exact - top.astype(np.float32)).astype(ml_dtypes.bfloat16)


def forward_table(order):
    return parts(table(order))


def backward_table(order):
    weight = np.full((2, HALF), 2.0 / CIRCLE)
    weight[:, 0] = 1.0 / CIRCLE
    return parts(table(order) * weight.reshape(1, -1))


def shard_order():
    return (np.arange(COLS)[:, None] + COLS * np.arange(SHARDS)[None, :]).reshape(-1)


def pack(unit, out_ref):
    def piece(l, r):
        return unit[ROWS * l : ROWS * (l + 1), SHARDS * r : SHARDS * (r + 1)]

    for l in range(COLS):
        out_ref[:, l, :] = jnp.concatenate([piece(l, r) for r in range(8)], axis=0).T
    for q in range(3):
        chunk = [piece(3 * g + q, r) for g in range(4) for r in (8, 9)]
        out_ref[:, 12 + q, :] = jnp.concatenate(chunk, axis=0).T
    out_ref[:, 15, :] = jnp.zeros((SHARDS, 128), F32)


def mlp_kernel(act_ref, cot_ref, in_ref, out_ref, block_ref, hidden_ref, grad_ref, unit_ref):
    step = pl.program_id(0)
    act, cot = split(act_ref[...]), split(cot_ref[...])
    w_in, w_out = split(in_ref[...]), split(out_ref[...])
    preact = dot3(act, w_in, ((1,), (1,)))
    cdf = 0.5 * (1.0 + lax.erf(preact * (1.0 / math.sqrt(2.0))))
    density = jnp.exp(-0.5 * preact * preact) * (1.0 / math.sqrt(2.0 * math.pi))
    hidden_ref[...] = preact * cdf
    grad = dot3(cot, w_out, ((1,), (1,))) * (cdf + preact * density)
    grad_ref[...] = grad
    term = dot3(split(grad), w_in, ((1,), (0,)))

    @pl.when(step == 0)
    def _():
        unit_ref[...] = cot_ref[...] + term

    @pl.when(step > 0)
    def _():
        unit_ref[...] += term

    @pl.when(step == pl.num_programs(0) - 1)
    def _():
        pack(unit_ref[...], block_ref)


def mlp(act, cot, weight_in, weight_out):
    points, width = act.shape
    units = weight_in.shape[0]
    tile = 256
    full = lambda shape: pl.BlockSpec(shape, lambda i: (0,) * len(shape))
    return pl.pallas_call(
        mlp_kernel,
        grid=(units // tile,),
        in_specs=[
            full((points, width)),
            full((points, width)),
            pl.BlockSpec((tile, width), lambda i: (i, 0)),
            pl.BlockSpec((tile, width), lambda i: (i, 0)),
        ],
        out_specs=[
            full((SHARDS, 16, 128)),
            pl.BlockSpec((points, tile), lambda i: (0, i)),
            pl.BlockSpec((points, tile), lambda i: (0, i)),
        ],
        out_shape=[
            jax.ShapeDtypeStruct((SHARDS, 16, 128), F32),
            jax.ShapeDtypeStruct((points, units), F32),
            jax.ShapeDtypeStruct((points, units), F32),
        ],
        scratch_shapes=[pltpu.VMEM((points, width), F32)],
        compiler_params=params(32),
        cost_estimate=cost(18 * points * width * units, 10_000_000),
        name="mlp",
    )(act, cot, weight_in, weight_out)


def pick(field, core):
    even = jnp.concatenate([field[:, 0:160], field[:, 320:480]], axis=1)
    odd = jnp.concatenate([field[:, 160:320], field[:, 480:640]], axis=1)
    return split(jnp.where(core == 0, even, odd))


def weight_kernel(core_ref, grad_ref, hidden_ref, act_ref, cot_ref, *rest):
    out_ref = rest[-1]
    core = core_ref[0]
    act, cot = pick(act_ref[...], core), pick(cot_ref[...], core)
    contract = ((0,), (0,))
    first = dot3(split(grad_ref[...]), act, contract)
    second = dot3(split(hidden_ref[...]), cot, contract)
    total = jnp.concatenate([first, second], axis=1)
    if len(rest) == 2:
        total += rest[0][...]
    out_ref[...] = total


def weight_part(core, grad, hidden, act, cot, arrived):
    points, units = grad.shape
    width = act.shape[1]
    tile = 256
    tall = pl.BlockSpec((points, tile), lambda i: (0, i))
    flat = pl.BlockSpec((points, width), lambda i: (0, 0))
    wide = pl.BlockSpec((tile, width), lambda i: (i, 0))
    return pl.pallas_call(
        weight_kernel,
        grid=(units // tile,),
        in_specs=[pl.BlockSpec(memory_space=pltpu.SMEM), tall, tall, flat, flat]
        + [wide] * len(arrived),
        out_specs=wide,
        out_shape=jax.ShapeDtypeStruct((units, width), F32),
        compiler_params=params(24),
        cost_estimate=cost(6 * points * width * units, 10_000_000),
        name="weights",
    )(core, grad, hidden, act, cot, *arrived)


def last_kernel(place_ref, total_ref, first_ref, second_ref):
    total = total_ref[...]
    upper, right = place_ref[0], place_ref[1]
    kept = jnp.where(right == 1, total[20:40], total[0:20])
    first_ref[...] = jnp.where(upper == 1, kept[:, 160:320], kept[:, 0:160])
    second_ref[...] = jnp.where(upper == 1, kept[:, 480:640], kept[:, 320:480])


def weight_gradients(grad, hidden, act, cot):
    core = lax.axis_index("co")
    other = weight_part((1 - core).reshape(1), grad, hidden, act, cot, ())
    arrived = lax.ppermute(other, "co", [(0, 1), (1, 0)])
    total = weight_part(core.reshape(1), grad, hidden, act, cot, (arrived,))
    total = lax.psum_scatter(total, ("x", "z"), scatter_dimension=0, tiled=True)
    total = lax.psum(total, ("yl", "yh"))
    place = jnp.stack([lax.axis_index("yl"), lax.axis_index("yh")])
    return pl.pallas_call(
        last_kernel,
        in_specs=[pl.BlockSpec(memory_space=pltpu.SMEM)] + whole(1),
        out_specs=whole(2),
        out_shape=[jax.ShapeDtypeStruct((20, 160), F32)] * 2,
        name="last",
    )(place, total)


def spectrum_kernel(block_ref, top_ref, low_ref, out_ref, first_ref, final_ref, flat_ref):
    for p in range(COLS // 2):
        pair = jnp.concatenate([block_ref[:, 2 * p, :], block_ref[:, 2 * p + 1, :]], axis=0)
        flat_ref[0:128, 128 * p : 128 * (p + 1)] = pair.T
    rest = [block_ref[:, 12 + q, :].T for q in range(3)]
    pieces = [rest[q][32 * g : 32 * (g + 1), :] for g in range(4) for q in range(3)]
    flat_ref[128:160, :] = jnp.concatenate(pieces, axis=1)
    result = dot3(split(flat_ref[...]), (top_ref[...], low_ref[...]), ((1,), (0,)))
    out_ref[...] = result
    for r in range(OWN):
        first_ref[3 * r : 3 * r + 3, :] = result[ROWS * r : ROWS * r + 3, :]
        final_ref[3 * r : 3 * r + 3, :] = result[ROWS * r + 13 : ROWS * r + 16, :]


def spectrum(block):
    top, low = forward_table(shard_order())
    rows = OWN * ROWS
    return pl.pallas_call(
        spectrum_kernel,
        in_specs=whole(3),
        out_specs=whole(3),
        out_shape=[
            jax.ShapeDtypeStruct((rows, CIRCLE), F32),
            jax.ShapeDtypeStruct((3 * OWN, CIRCLE), F32),
            jax.ShapeDtypeStruct((3 * OWN, CIRCLE), F32),
        ],
        scratch_shapes=[pltpu.VMEM((rows, CIRCLE), F32)],
        compiler_params=params(24),
        cost_estimate=cost(6 * rows * CIRCLE * CIRCLE, 4_000_000),
        name="spectrum",
    )(block, jnp.asarray(top), jnp.asarray(low))


def kernel_spectrum_kernel(kernel_ref, top_ref, low_ref, out_ref):
    out_ref[...] = dot3(split(kernel_ref[...]), (top_ref[...], low_ref[...]), ((1,), (0,)))


def kernel_spectrum(kernels):
    top, low = forward_table(np.arange(CIRCLE))
    rows = BASIS * TAPS * ROWS
    flat = kernels.transpose(0, 2, 1, 3).reshape(rows, CIRCLE)
    return pl.pallas_call(
        kernel_spectrum_kernel,
        in_specs=whole(3),
        out_specs=whole(1)[0],
        out_shape=jax.ShapeDtypeStruct((rows, CIRCLE), F32),
        compiler_params=params(24),
        cost_estimate=cost(6 * rows * CIRCLE * CIRCLE, 5_000_000),
        name="kernel_spectrum",
    )(flat, jnp.asarray(top), jnp.asarray(low))


def filter_kernel(
    mixing_ref, data_ref, before_ref, after_ref, kernel_ref, top_ref, low_ref, out_ref, rows_ref, sum_ref
):
    for r in range(OWN):
        rows_ref[r, 0:3, :] = before_ref[3 * r : 3 * r + 3, :]
        rows_ref[r, 3 : 3 + ROWS, :] = data_ref[ROWS * r : ROWS * (r + 1), :]
        rows_ref[r, 3 + ROWS : 6 + ROWS, :] = after_ref[3 * r : 3 * r + 3, :]
    lane = lax.broadcasted_iota(jnp.int32, (ROWS, HALF), 1)
    ends = lane == 0

    def channel(r, carry):
        real = jnp.zeros((ROWS, HALF), F32)
        imag = jnp.zeros((ROWS, HALF), F32)
        for k in range(TAPS):
            mixed_real = jnp.zeros((ROWS, HALF), F32)
            mixed_imag = jnp.zeros((ROWS, HALF), F32)
            for b in range(BASIS):
                weight = mixing_ref[r, b]
                at = ROWS * (TAPS * b + k)
                mixed_real += weight * kernel_ref[at : at + ROWS, 0:HALF]
                mixed_imag += weight * kernel_ref[at : at + ROWS, HALF:CIRCLE]
            own = jnp.where(ends, mixed_imag, mixed_real)
            cross = jnp.where(ends, 0.0, mixed_imag)
            data_real = rows_ref[r, 6 - k : 6 - k + ROWS, 0:HALF]
            data_imag = rows_ref[r, 6 - k : 6 - k + ROWS, HALF:CIRCLE]
            real += mixed_real * data_real + cross * data_imag
            imag += own * data_imag - cross * data_real
        sum_ref[r, :, 0:HALF] = real
        sum_ref[r, :, HALF:CIRCLE] = imag
        return carry

    lax.fori_loop(0, OWN, channel, 0)
    total = split(sum_ref[...].reshape(OWN * ROWS, CIRCLE))
    field = dot3((top_ref[...], low_ref[...]), total, ((1,), (1,)))
    for l in range(COLS):
        out_ref[:, l, :] = field[SHARDS * l : SHARDS * (l + 1), 0:128]
    for q in range(3):
        pieces = [
            field[SHARDS * (3 * g + q) : SHARDS * (3 * g + q + 1), 128:160] for g in range(4)
        ]
        out_ref[:, 12 + q, :] = jnp.concatenate(pieces, axis=1)
    out_ref[:, 15, :] = jnp.zeros((SHARDS, 128), F32)


def filtered(mixing, data, before, after, kernel):
    top, low = backward_table(shard_order())
    return pl.pallas_call(
        filter_kernel,
        in_specs=[pl.BlockSpec(memory_space=pltpu.SMEM)] + whole(6),
        out_specs=whole(1)[0],
        out_shape=jax.ShapeDtypeStruct((SHARDS, 16, 128), F32),
        scratch_shapes=[
            pltpu.VMEM((OWN, 24, CIRCLE), F32),
            pltpu.VMEM((OWN, ROWS, CIRCLE), F32),
        ],
        compiler_params=params(32),
        cost_estimate=cost(6 * OWN * ROWS * CIRCLE * CIRCLE, 5_000_000),
        name="filter",
    )(mixing, data, before, after, kernel, jnp.asarray(top), jnp.asarray(low))


def unpack_kernel(block_ref, out_ref):
    def put(l, r, pair):
        out_ref[ROWS * l : ROWS * (l + 1), SHARDS * r : SHARDS * (r + 2)] = jnp.concatenate(
            pair, axis=1
        )

    for l in range(COLS):
        turned = block_ref[:, l, :].T
        for r in range(0, 8, 2):
            put(l, r, [turned[ROWS * r : ROWS * (r + 1)], turned[ROWS * (r + 1) : ROWS * (r + 2)]])
    for q in range(3):
        turned = block_ref[:, 12 + q, :].T
        for g in range(4):
            at = 32 * g
            put(3 * g + q, 8, [turned[at : at + ROWS], turned[at + ROWS : at + 2 * ROWS]])


def unpack(block):
    return pl.pallas_call(
        unpack_kernel,
        in_specs=whole(1),
        out_specs=whole(1)[0],
        out_shape=jax.ShapeDtypeStruct((ROWS * COLS, SHARDS * OWN), F32),
        name="unpack",
    )(block)


def across(block):
    return lax.all_to_all(block, LON, split_axis=0, concat_axis=0, tiled=True)


def per_device(activation, cotangent, weight_in, weight_out, kernels, mixing):
    points = ROWS * COLS
    width = activation.shape[2]
    act = activation.transpose(1, 0, 2).reshape(points, width)
    cot = cotangent.transpose(1, 0, 2).reshape(points, width)
    every = lax.all_gather(mixing, LON, axis=0, tiled=True).reshape(OWN, SHARDS, BASIS)
    shard = lax.axis_index(LON)
    own_mixing = lax.dynamic_slice_in_dim(every, shard, 1, 1).reshape(OWN, BASIS)
    block, hidden, grad = mlp(act, cot, weight_in, weight_out)
    spread = across(block)
    grad_in, grad_out = weight_gradients(grad, hidden, act, cot)
    kernel = kernel_spectrum(kernels)
    data, first, final = spectrum(spread)
    forward = [(i, i + 1) for i in range(3)]
    backward = [(target, source) for source, target in forward]
    before = lax.ppermute(final, LAT, forward)
    after = lax.ppermute(first, LAT, backward)
    result = across(filtered(own_mixing, data, before, after, kernel))
    field = unpack(result).reshape(COLS, ROWS, width).transpose(1, 0, 2)
    return (field, grad_in, grad_out)


def solution(mesh):
    fine = Mesh(mesh.devices.reshape(2, 2, 4, 8, 2), AXES)
    placed = (
        P(LAT, LON, None),
        P(LAT, LON, None),
        P(),
        P(),
        P(None, LAT, None, None),
        P(LON, None),
    )
    return jax.shard_map(
        per_device,
        mesh=fine,
        in_specs=placed,
        out_specs=(P(LAT, LON, None), P(LON, LAT), P(LON, LAT)),
        check_vma=False,
    )
```

```python
import functools
import math

import jax
import jax.numpy as jnp
import ml_dtypes
import numpy as np
from jax import lax
from jax.experimental import pallas as pl
from jax.experimental.pallas import tpu as pltpu
from jax.sharding import Mesh
from jax.sharding import PartitionSpec as P

AXES = ("yl", "co", "x", "z", "yh")
LAT = ("yl", "co")
LON = ("x", "z", "yh")
F32 = jnp.float32
BF16 = jnp.bfloat16
SHARDS = 64
COLS = 12
ROWS = 16
OWN = 10
CIRCLE = 768
HALF = 384
TAPS = 7
BASIS = 3
MIB = 1 << 20


def split(value):
    top = value.astype(BF16)
    return top, (value - top.astype(F32)).astype(BF16)


def dot3(left, right, dims):
    (a, b), (c, d) = left, right
    numbers = (dims, ((), ()))
    one = functools.partial(lax.dot_general, dimension_numbers=numbers, preferred_element_type=F32)
    return one(a, c) + (one(a, d) + one(b, c))


def whole(n):
    return [pl.BlockSpec(memory_space=pltpu.VMEM)] * n


def params(mib):
    return pltpu.CompilerParams(vmem_limit_bytes=mib * MIB)


def cost(flops, moved):
    return pl.CostEstimate(flops=flops, bytes_accessed=moved, transcendentals=0)


def table(order):
    angle = 2.0 * np.pi / CIRCLE * (order[:, None] * np.arange(HALF)[None, :] % CIRCLE)
    nyquist = np.where(order % 2 == 0, 1.0, -1.0)
    real, imag = np.cos(angle), -np.sin(angle)
    imag[:, 0] = nyquist
    return np.concatenate([real, imag], axis=1)


def parts(matrix):
    exact = matrix.astype(np.float32)
    top = exact.astype(ml_dtypes.bfloat16)
    return top, (exact - top.astype(np.float32)).astype(ml_dtypes.bfloat16)


def forward_table(order):
    return parts(table(order))


def backward_table(order):
    weight = np.full((2, HALF), 2.0 / CIRCLE)
    weight[:, 0] = 1.0 / CIRCLE
    return parts(table(order) * weight.reshape(1, -1))


def shard_order():
    return (np.arange(COLS)[:, None] + COLS * np.arange(SHARDS)[None, :]).reshape(-1)


def pack(unit, mixing_ref, shard, out_ref):
    def piece(l, r):
        return unit[ROWS * l : ROWS * (l + 1), SHARDS * r : SHARDS * (r + 1)]

    for l in range(COLS):
        out_ref[:, l, :] = jnp.concatenate([piece(l, r) for r in range(8)], axis=0).T
    for q in range(3):
        chunk = [piece(3 * g + q, r) for g in range(4) for r in (8, 9)]
        out_ref[:, 12 + q, :] = jnp.concatenate(chunk, axis=0).T
    target = lax.broadcasted_iota(jnp.int32, (SHARDS, 128), 0)
    lane = lax.broadcasted_iota(jnp.int32, (SHARDS, 128), 1)
    weights = jnp.zeros((SHARDS, 128), F32)
    for i in range(OWN):
        channel = OWN * shard + i
        here = target == lax.rem(channel, SHARDS)
        first = BASIS * lax.div(channel, SHARDS)
        for b in range(BASIS):
            weights = jnp.where(here & (lane == first + b), mixing_ref[i, b], weights)
    out_ref[:, 15, :] = weights


def mlp_kernel(
    shard_ref, mixing_ref, act_ref, cot_ref, in_ref, out_ref, block_ref, hidden_ref, grad_ref, unit_ref
):
    step = pl.program_id(0)
    act, cot = split(act_ref[...]), split(cot_ref[...])
    w_in, w_out = split(in_ref[...]), split(out_ref[...])
    preact = dot3(act, w_in, ((1,), (1,)))
    cdf = 0.5 * (1.0 + lax.erf(preact * (1.0 / math.sqrt(2.0))))
    density = jnp.exp(-0.5 * preact * preact) * (1.0 / math.sqrt(2.0 * math.pi))
    hidden_ref[...] = preact * cdf
    grad = dot3(cot, w_out, ((1,), (1,))) * (cdf + preact * density)
    grad_ref[...] = grad
    term = dot3(split(grad), w_in, ((1,), (0,)))

    @pl.when(step == 0)
    def _():
        unit_ref[...] = cot_ref[...] + term

    @pl.when(step > 0)
    def _():
        unit_ref[...] += term

    @pl.when(step == pl.num_programs(0) - 1)
    def _():
        pack(unit_ref[...], mixing_ref, shard_ref[0], block_ref)


def mlp(shard, mixing, act, cot, weight_in, weight_out):
    points, width = act.shape
    units = weight_in.shape[0]
    tile = 256
    full = lambda shape: pl.BlockSpec(shape, lambda i: (0,) * len(shape))
    return pl.pallas_call(
        mlp_kernel,
        grid=(units // tile,),
        in_specs=[
            pl.BlockSpec(memory_space=pltpu.SMEM),
            pl.BlockSpec(memory_space=pltpu.SMEM),
            full((points, width)),
            full((points, width)),
            pl.BlockSpec((tile, width), lambda i: (i, 0)),
            pl.BlockSpec((tile, width), lambda i: (i, 0)),
        ],
        out_specs=[
            full((SHARDS, 16, 128)),
            pl.BlockSpec((points, tile), lambda i: (0, i)),
            pl.BlockSpec((points, tile), lambda i: (0, i)),
        ],
        out_shape=[
            jax.ShapeDtypeStruct((SHARDS, 16, 128), F32),
            jax.ShapeDtypeStruct((points, units), F32),
            jax.ShapeDtypeStruct((points, units), F32),
        ],
        scratch_shapes=[pltpu.VMEM((points, width), F32)],
        compiler_params=params(60),
        cost_estimate=cost(18 * points * width * units, 10_000_000),
        name="mlp",
    )(shard, mixing, act, cot, weight_in, weight_out)


def pick(field, core):
    even = jnp.concatenate([field[:, 0:160], field[:, 320:480]], axis=1)
    odd = jnp.concatenate([field[:, 160:320], field[:, 480:640]], axis=1)
    return split(jnp.where(core == 0, even, odd))


def weight_kernel(core_ref, grad_ref, hidden_ref, act_ref, cot_ref, *rest):
    out_ref = rest[-1]
    core = core_ref[0]
    act, cot = pick(act_ref[...], core), pick(cot_ref[...], core)
    contract = ((0,), (0,))
    first = dot3(split(grad_ref[...]), act, contract)
    second = dot3(split(hidden_ref[...]), cot, contract)
    total = jnp.concatenate([first, second], axis=1)
    if len(rest) == 2:
        total += rest[0][...]
    out_ref[...] = total


def weight_part(core, grad, hidden, act, cot, arrived):
    points, units = grad.shape
    width = act.shape[1]
    tile = 256
    tall = pl.BlockSpec((points, tile), lambda i: (0, i))
    flat = pl.BlockSpec((points, width), lambda i: (0, 0))
    wide = pl.BlockSpec((tile, width), lambda i: (i, 0))
    return pl.pallas_call(
        weight_kernel,
        grid=(units // tile,),
        in_specs=[pl.BlockSpec(memory_space=pltpu.SMEM), tall, tall, flat, flat]
        + [wide] * len(arrived),
        out_specs=wide,
        out_shape=jax.ShapeDtypeStruct((units, width), F32),
        compiler_params=params(24),
        cost_estimate=cost(6 * points * width * units, 10_000_000),
        name="weights",
    )(core, grad, hidden, act, cot, *arrived)


def quarter(total, upper, right):
    kept = jnp.where(right == 1, total[20:40], total[0:20])
    first = jnp.where(upper == 1, kept[:, 160:320], kept[:, 0:160])
    second = jnp.where(upper == 1, kept[:, 480:640], kept[:, 320:480])
    return first, second


def cut_kernel(place_ref, total_ref, *out_refs):
    total = total_ref[...]
    for m, out_ref in enumerate(out_refs):
        upper, right = place_ref[0], place_ref[1]
        upper = 1 - upper if m & 2 else upper
        right = 1 - right if m & 1 else right
        first, second = quarter(total, upper, right)
        out_ref[0:20, :] = first
        out_ref[24:44, :] = second


def sum_kernel(*refs):
    first_ref, second_ref = refs[4:]
    first_ref[...] = (refs[0][0:20] + refs[1][0:20]) + (refs[2][0:20] + refs[3][0:20])
    second_ref[...] = (refs[0][24:44] + refs[1][24:44]) + (refs[2][24:44] + refs[3][24:44])


def weight_sums(grad, hidden, act, cot):
    core = lax.axis_index("co")
    other = weight_part((1 - core).reshape(1), grad, hidden, act, cot, ())
    arrived = lax.ppermute(other, "co", [(0, 1), (1, 0)])
    total = weight_part(core.reshape(1), grad, hidden, act, cot, (arrived,))
    return lax.psum_scatter(total, "x", scatter_dimension=0, tiled=True)


def finish(total):
    total = lax.psum_scatter(total, "z", scatter_dimension=0, tiled=True)
    place = jnp.stack([lax.axis_index("yl"), lax.axis_index("yh")])
    pieces = pl.pallas_call(
        cut_kernel,
        in_specs=[pl.BlockSpec(memory_space=pltpu.SMEM)] + whole(1),
        out_specs=whole(4),
        out_shape=[jax.ShapeDtypeStruct((48, 160), F32)] * 4,
        name="cut",
    )(place, total)
    moved = [pieces[0]] + [
        lax.ppermute(pieces[m], ("yl", "yh"), [(i, i ^ m) for i in range(4)]) for m in (1, 2, 3)
    ]
    return pl.pallas_call(
        sum_kernel,
        in_specs=whole(4),
        out_specs=whole(2),
        out_shape=[jax.ShapeDtypeStruct((20, 160), F32)] * 2,
        name="last",
    )(*moved)


def spectrum_kernel(
    block_ref, top_ref, low_ref, out_ref, first_ref, final_ref, mixing_ref, flat_ref
):
    for p in range(COLS // 2):
        pair = jnp.concatenate([block_ref[:, 2 * p, :], block_ref[:, 2 * p + 1, :]], axis=0)
        flat_ref[0:128, 128 * p : 128 * (p + 1)] = pair.T
    rest = [block_ref[:, 12 + q, :].T for q in range(3)]
    pieces = [rest[q][32 * g : 32 * (g + 1), :] for g in range(4) for q in range(3)]
    flat_ref[128:160, :] = jnp.concatenate(pieces, axis=1)
    result = dot3(split(flat_ref[...]), (top_ref[...], low_ref[...]), ((1,), (0,)))
    out_ref[...] = result
    mixing_ref[...] = jnp.sum(block_ref[:, 15, :], axis=0, keepdims=True)
    for r in range(OWN):
        first_ref[3 * r : 3 * r + 3, :] = result[ROWS * r : ROWS * r + 3, :]
        final_ref[3 * r : 3 * r + 3, :] = result[ROWS * r + 13 : ROWS * r + 16, :]


def spectrum(block):
    top, low = forward_table(shard_order())
    rows = OWN * ROWS
    return pl.pallas_call(
        spectrum_kernel,
        in_specs=whole(3),
        out_specs=whole(4),
        out_shape=[
            jax.ShapeDtypeStruct((rows, CIRCLE), F32),
            jax.ShapeDtypeStruct((3 * OWN, CIRCLE), F32),
            jax.ShapeDtypeStruct((3 * OWN, CIRCLE), F32),
            jax.ShapeDtypeStruct((1, 128), F32),
        ],
        scratch_shapes=[pltpu.VMEM((rows, CIRCLE), F32)],
        compiler_params=params(24),
        cost_estimate=cost(6 * rows * CIRCLE * CIRCLE, 4_000_000),
        name="spectrum",
    )(block, jnp.asarray(top), jnp.asarray(low))


def kernel_spectrum_kernel(kernel_ref, top_ref, low_ref, out_ref):
    out_ref[...] = dot3(split(kernel_ref[...]), (top_ref[...], low_ref[...]), ((1,), (0,)))


def kernel_spectrum(kernels):
    top, low = forward_table(np.arange(CIRCLE))
    rows = BASIS * TAPS * ROWS
    flat = kernels.transpose(0, 2, 1, 3).reshape(rows, CIRCLE)
    return pl.pallas_call(
        kernel_spectrum_kernel,
        in_specs=whole(3),
        out_specs=whole(1)[0],
        out_shape=jax.ShapeDtypeStruct((rows, CIRCLE), F32),
        compiler_params=params(24),
        cost_estimate=cost(6 * rows * CIRCLE * CIRCLE, 5_000_000),
        name="kernel_spectrum",
    )(flat, jnp.asarray(top), jnp.asarray(low))


def filter_kernel(
    mixing_ref, data_ref, before_ref, after_ref, kernel_ref, top_ref, low_ref, out_ref, rows_ref, sum_ref
):
    for r in range(OWN):
        rows_ref[r, 0:3, :] = before_ref[3 * r : 3 * r + 3, :]
        rows_ref[r, 3 : 3 + ROWS, :] = data_ref[ROWS * r : ROWS * (r + 1), :]
        rows_ref[r, 3 + ROWS : 6 + ROWS, :] = after_ref[3 * r : 3 * r + 3, :]
    lane = lax.broadcasted_iota(jnp.int32, (ROWS, HALF), 1)
    ends = lane == 0

    def channel(r, carry):
        real = jnp.zeros((ROWS, HALF), F32)
        imag = jnp.zeros((ROWS, HALF), F32)
        for k in range(TAPS):
            mixed_real = jnp.zeros((ROWS, HALF), F32)
            mixed_imag = jnp.zeros((ROWS, HALF), F32)
            for b in range(BASIS):
                weight = mixing_ref[0, BASIS * r + b]
                at = ROWS * (TAPS * b + k)
                mixed_real += weight * kernel_ref[at : at + ROWS, 0:HALF]
                mixed_imag += weight * kernel_ref[at : at + ROWS, HALF:CIRCLE]
            own = jnp.where(ends, mixed_imag, mixed_real)
            cross = jnp.where(ends, 0.0, mixed_imag)
            data_real = rows_ref[r, 6 - k : 6 - k + ROWS, 0:HALF]
            data_imag = rows_ref[r, 6 - k : 6 - k + ROWS, HALF:CIRCLE]
            real += mixed_real * data_real + cross * data_imag
            imag += own * data_imag - cross * data_real
        sum_ref[r, :, 0:HALF] = real
        sum_ref[r, :, HALF:CIRCLE] = imag
        return carry

    lax.fori_loop(0, OWN, channel, 0)
    total = split(sum_ref[...].reshape(OWN * ROWS, CIRCLE))
    field = dot3((top_ref[...], low_ref[...]), total, ((1,), (1,)))
    for l in range(COLS):
        out_ref[:, l, :] = field[SHARDS * l : SHARDS * (l + 1), 0:128]
    for q in range(3):
        pieces = [
            field[SHARDS * (3 * g + q) : SHARDS * (3 * g + q + 1), 128:160] for g in range(4)
        ]
        out_ref[:, 12 + q, :] = jnp.concatenate(pieces, axis=1)
    out_ref[:, 15, :] = jnp.zeros((SHARDS, 128), F32)


def filtered(mixing, data, before, after, kernel):
    top, low = backward_table(shard_order())
    return pl.pallas_call(
        filter_kernel,
        in_specs=[pl.BlockSpec(memory_space=pltpu.SMEM)] + whole(6),
        out_specs=whole(1)[0],
        out_shape=jax.ShapeDtypeStruct((SHARDS, 16, 128), F32),
        scratch_shapes=[
            pltpu.VMEM((OWN, 24, CIRCLE), F32),
            pltpu.VMEM((OWN, ROWS, CIRCLE), F32),
        ],
        compiler_params=params(32),
        cost_estimate=cost(6 * OWN * ROWS * CIRCLE * CIRCLE, 5_000_000),
        name="filter",
    )(mixing, data, before, after, kernel, jnp.asarray(top), jnp.asarray(low))


def unpack_kernel(block_ref, out_ref):
    def put(l, r, pair):
        out_ref[ROWS * l : ROWS * (l + 1), SHARDS * r : SHARDS * (r + 2)] = jnp.concatenate(
            pair, axis=1
        )

    for l in range(COLS):
        turned = block_ref[:, l, :].T
        for r in range(0, 8, 2):
            put(l, r, [turned[ROWS * r : ROWS * (r + 1)], turned[ROWS * (r + 1) : ROWS * (r + 2)]])
    for q in range(3):
        turned = block_ref[:, 12 + q, :].T
        for g in range(4):
            at = 32 * g
            put(3 * g + q, 8, [turned[at : at + ROWS], turned[at + ROWS : at + 2 * ROWS]])


def unpack(block):
    return pl.pallas_call(
        unpack_kernel,
        in_specs=whole(1),
        out_specs=whole(1)[0],
        out_shape=jax.ShapeDtypeStruct((ROWS * COLS, SHARDS * OWN), F32),
        name="unpack",
    )(block)


def across(block):
    return lax.all_to_all(block, LON, split_axis=0, concat_axis=0, tiled=True)


def per_device(activation, cotangent, weight_in, weight_out, kernels, mixing):
    points = ROWS * COLS
    width = activation.shape[2]
    act = activation.transpose(1, 0, 2).reshape(points, width)
    cot = cotangent.transpose(1, 0, 2).reshape(points, width)
    shard = lax.axis_index(LON).reshape(1)
    block, hidden, grad = mlp(shard, mixing, act, cot, weight_in, weight_out)
    spread = across(block)
    total = weight_sums(grad, hidden, act, cot)
    kernel = kernel_spectrum(kernels)
    data, first, final, own_mixing = spectrum(spread)
    forward = [(i, i + 1) for i in range(3)]
    backward = [(target, source) for source, target in forward]
    before = lax.ppermute(final, LAT, forward)
    after = lax.ppermute(first, LAT, backward)
    sent = filtered(own_mixing, data, before, after, kernel)
    result = across(sent)
    total, _ = lax.optimization_barrier((total, sent))
    grad_in, grad_out = finish(total)
    field = unpack(result).reshape(COLS, ROWS, width).transpose(1, 0, 2)
    return (field, grad_in, grad_out)


def solution(mesh):
    fine = Mesh(mesh.devices.reshape(2, 2, 4, 8, 2), AXES)
    placed = (
        P(LAT, LON, None),
        P(LAT, LON, None),
        P(),
        P(),
        P(None, LAT, None, None),
        P(LON, None),
    )
    return jax.shard_map(
        per_device,
        mesh=fine,
        in_specs=placed,
        out_specs=(P(LAT, LON, None), P(LON, LAT), P(LON, LAT)),
        check_vma=False,
    )
```

```python
import functools
import math

import jax
import jax.numpy as jnp
import ml_dtypes
import numpy as np
from jax import lax
from jax.experimental import pallas as pl
from jax.experimental.pallas import tpu as pltpu
from jax.sharding import Mesh
from jax.sharding import PartitionSpec as P

AXES = ("yl", "co", "x", "z", "yh")
LAT = ("yl", "co")
LON = ("x", "z", "yh")
F32 = jnp.float32
BF16 = jnp.bfloat16
SHARDS = 64
COLS = 12
ROWS = 16
OWN = 10
CIRCLE = 768
HALF = 384
TAPS = 7
BASIS = 3
MIB = 1 << 20


def split(value):
    top = value.astype(BF16)
    return top, (value - top.astype(F32)).astype(BF16)


def dot3(left, right, dims):
    (a, b), (c, d) = left, right
    numbers = (dims, ((), ()))
    one = functools.partial(lax.dot_general, dimension_numbers=numbers, preferred_element_type=F32)
    return one(a, c) + (one(a, d) + one(b, c))


def whole(n):
    return [pl.BlockSpec(memory_space=pltpu.VMEM)] * n


def params(mib):
    return pltpu.CompilerParams(vmem_limit_bytes=mib * MIB)


def cost(flops, moved):
    return pl.CostEstimate(flops=flops, bytes_accessed=moved, transcendentals=0)


def table(order):
    angle = 2.0 * np.pi / CIRCLE * (order[:, None] * np.arange(HALF)[None, :] % CIRCLE)
    nyquist = np.where(order % 2 == 0, 1.0, -1.0)
    real, imag = np.cos(angle), -np.sin(angle)
    imag[:, 0] = nyquist
    return np.concatenate([real, imag], axis=1)


def parts(matrix):
    exact = matrix.astype(np.float32)
    top = exact.astype(ml_dtypes.bfloat16)
    return top, (exact - top.astype(np.float32)).astype(ml_dtypes.bfloat16)


def forward_table(order):
    return parts(table(order))


def backward_table(order):
    weight = np.full((2, HALF), 2.0 / CIRCLE)
    weight[:, 0] = 1.0 / CIRCLE
    return parts(table(order) * weight.reshape(1, -1))


def shard_order():
    return (np.arange(COLS)[:, None] + COLS * np.arange(SHARDS)[None, :]).reshape(-1)


def pack(unit, mixing_ref, shard, out_ref):
    def piece(l, r):
        return unit[ROWS * l : ROWS * (l + 1), SHARDS * r : SHARDS * (r + 1)]

    for l in range(COLS):
        out_ref[:, l, :] = jnp.concatenate([piece(l, r) for r in range(8)], axis=0).T
    for q in range(3):
        chunk = [piece(3 * g + q, r) for g in range(4) for r in (8, 9)]
        out_ref[:, 12 + q, :] = jnp.concatenate(chunk, axis=0).T
    target = lax.broadcasted_iota(jnp.int32, (SHARDS, 128), 0)
    lane = lax.broadcasted_iota(jnp.int32, (SHARDS, 128), 1)
    weights = jnp.zeros((SHARDS, 128), F32)
    for i in range(OWN):
        channel = OWN * shard + i
        here = target == lax.rem(channel, SHARDS)
        first = BASIS * lax.div(channel, SHARDS)
        for b in range(BASIS):
            weights = jnp.where(here & (lane == first + b), mixing_ref[i, b], weights)
    out_ref[:, 15, :] = weights


def mlp_kernel(
    place_ref,
    mixing_ref,
    act_ref,
    cot_ref,
    in_ref,
    out_ref,
    block_ref,
    own_ref,
    other_ref,
    unit_ref,
    act_top,
    act_low,
    cot_top,
    cot_low,
    act_cols_top,
    act_cols_low,
    cot_cols_top,
    cot_cols_low,
):
    step = pl.program_id(0)

    @pl.when(step == 0)
    def _():
        act, cot = act_ref[...], cot_ref[...]
        act_top[...], act_low[...] = split(act)
        cot_top[...], cot_low[...] = split(cot)
        even = [act[:, 0:160], act[:, 320:480]]
        odd = [act[:, 160:320], act[:, 480:640]]
        act_cols_top[...], act_cols_low[...] = split(jnp.concatenate(even + odd, axis=1))
        even = [cot[:, 0:160], cot[:, 320:480]]
        odd = [cot[:, 160:320], cot[:, 480:640]]
        cot_cols_top[...], cot_cols_low[...] = split(jnp.concatenate(odd + even, axis=1))

    w_in, w_out = split(in_ref[...]), split(out_ref[...])
    preact = dot3((act_top[...], act_low[...]), w_in, ((1,), (1,)))
    cdf = 0.5 * (1.0 + lax.erf(preact * (1.0 / math.sqrt(2.0))))
    density = jnp.exp(-0.5 * preact * preact) * (1.0 / math.sqrt(2.0 * math.pi))
    hidden = split(preact * cdf)
    slope = cdf + preact * density
    grad = split(dot3((cot_top[...], cot_low[...]), w_out, ((1,), (1,))) * slope)
    term = dot3(grad, w_in, ((1,), (0,)))

    @pl.when(step == 0)
    def _():
        unit_ref[...] = cot_ref[...] + term

    @pl.when(step > 0)
    def _():
        unit_ref[...] += term

    contract = ((0,), (0,))
    first = dot3(grad, (act_cols_top[...], act_cols_low[...]), contract)
    second = dot3(hidden, (cot_cols_top[...], cot_cols_low[...]), contract)
    left = lax.broadcasted_iota(jnp.int32, first.shape, 1) < 320
    mine = left == (place_ref[1] == 0)
    own_ref[...] = jnp.where(mine, first, second)
    other_ref[...] = jnp.where(mine, second, first)

    @pl.when(step == pl.num_programs(0) - 1)
    def _():
        pack(unit_ref[...], mixing_ref, place_ref[0], block_ref)


def mlp(place, mixing, act, cot, weight_in, weight_out):
    points, width = act.shape
    units = weight_in.shape[0]
    tile = 256
    full = lambda shape: pl.BlockSpec(shape, lambda i: (0,) * len(shape))
    rows = pl.BlockSpec((tile, width), lambda i: (i, 0))
    scalars = pl.BlockSpec(memory_space=pltpu.SMEM)
    return pl.pallas_call(
        mlp_kernel,
        grid=(units // tile,),
        in_specs=[scalars, scalars, full((points, width)), full((points, width)), rows, rows],
        out_specs=[full((SHARDS, 16, 128)), rows, rows],
        out_shape=[
            jax.ShapeDtypeStruct((SHARDS, 16, 128), F32),
            jax.ShapeDtypeStruct((units, width), F32),
            jax.ShapeDtypeStruct((units, width), F32),
        ],
        scratch_shapes=[pltpu.VMEM((points, width), F32)]
        + [pltpu.VMEM((points, width), BF16)] * 8,
        compiler_params=params(60),
        cost_estimate=cost(30 * points * width * units, 15_000_000),
        name="mlp",
    )(place, mixing, act, cot, weight_in, weight_out)


def choose(upper, right, rows, low, high):
    kept = jnp.where(right == 1, rows[high], rows[low])
    first = jnp.where(upper == 1, kept[:, 160:320], kept[:, 0:160])
    second = jnp.where(upper == 1, kept[:, 480:640], kept[:, 320:480])
    return [first, second]


def partner(place_ref, m):
    upper, right = place_ref[2], place_ref[3]
    return (1 - upper if m & 2 else upper), (1 - right if m & 1 else right)


def cut_kernel(place_ref, own_ref, arrived_ref, *out_refs):
    for m in range(4):
        start = pl.multiple_of(320 * lax.rem(place_ref[4] + m, 4), 8)
        rows = pl.ds(start, 160)
        out_refs[m][...] = own_ref[rows, :] + arrived_ref[rows, :]
    for x in range(4):
        at = 320 * x + 160
        total = own_ref[at : at + 160, :] + arrived_ref[at : at + 160, :]
        for m in range(4):
            upper, right = partner(place_ref, m)
            for z in range(4):
                low = slice(40 * z, 40 * z + 20)
                high = slice(40 * z + 20, 40 * z + 40)
                piece = jnp.concatenate(choose(upper, right, total, low, high), axis=1)
                row, col = 80 * (x % 2) + 20 * z, 320 * (x // 2)
                out_refs[4 + m][row : row + 20, col : col + 320] = piece


def swap_kernel(place_ref, *refs):
    ins, outs, kept_ref = refs[:8], refs[8:16], refs[16]
    along_x = (ins[0][...] + ins[1][...]) + (ins[2][...] + ins[3][...])
    along_y = (ins[4][...] + ins[5][...]) + (ins[6][...] + ins[7][...])
    for m in range(4):
        upper, right = partner(place_ref, m)
        for z in range(4):
            low = slice(40 * z, 40 * z + 20)
            high = slice(40 * z + 20, 40 * z + 40)
            piece = jnp.concatenate(choose(upper, right, along_x, low, high), axis=1)
            row, col = 20 * (z % 2), 320 * (z // 2)
            outs[m][row : row + 20, col : col + 320] = piece
    for x in range(4):
        row, col = 80 * (x % 2), 320 * (x // 2)
        part = along_y[row : row + 80, col : col + 320]
        kept_ref[x] = jnp.concatenate([part[0:40], part[40:80]], axis=1)
    for m in range(4):
        outs[4 + m][...] = kept_ref[lax.rem(place_ref[4] + m, 4)]


def stack_kernel(*refs):
    out_ref = refs[8]
    out_ref[...] = jnp.zeros(out_ref.shape, F32)
    for half in range(2):
        ins = refs[4 * half : 4 * half + 4]
        total = (ins[0][...] + ins[1][...]) + (ins[2][...] + ins[3][...])
        for z in range(4):
            row, col, at = 20 * (z % 2), 320 * (z // 2), 24 * (4 * half + z)
            out_ref[at : at + 20, 0:320] = total[row : row + 20, col : col + 320]


def last_kernel(place_ref, total_ref, first_ref, second_ref):
    total = total_ref[0:20, 0:320]
    even = place_ref[1] == 0
    first_ref[...] = jnp.where(even, total[:, 0:160], total[:, 160:320])
    second_ref[...] = jnp.where(even, total[:, 160:320], total[:, 0:160])


def small(kernel, operands, shapes, scalars=0, scratch=(), name=None):
    return pl.pallas_call(
        kernel,
        in_specs=[pl.BlockSpec(memory_space=pltpu.SMEM)] * scalars
        + whole(len(operands) - scalars),
        out_specs=whole(len(shapes)),
        out_shape=[jax.ShapeDtypeStruct(shape, F32) for shape in shapes],
        scratch_shapes=scratch,
        compiler_params=params(32),
        name=name,
    )(*operands)


def exchange_x(pieces):
    return [pieces[0]] + [
        lax.ppermute(pieces[m], "x", [(i, (i + m) % 4) for i in range(4)]) for m in (1, 2, 3)
    ]


def exchange_y(pieces):
    return [pieces[0]] + [
        lax.ppermute(pieces[m], ("yl", "yh"), [(i, i ^ m) for i in range(4)]) for m in (1, 2, 3)
    ]


def after(value, earlier):
    return lax.optimization_barrier((value, earlier))[0]


def spectrum_kernel(
    block_ref, top_ref, low_ref, out_ref, first_ref, final_ref, mixing_ref, flat_ref
):
    for p in range(COLS // 2):
        pair = jnp.concatenate([block_ref[:, 2 * p, :], block_ref[:, 2 * p + 1, :]], axis=0)
        flat_ref[0:128, 128 * p : 128 * (p + 1)] = pair.T
    rest = [block_ref[:, 12 + q, :].T for q in range(3)]
    pieces = [rest[q][32 * g : 32 * (g + 1), :] for g in range(4) for q in range(3)]
    flat_ref[128:160, :] = jnp.concatenate(pieces, axis=1)
    result = dot3(split(flat_ref[...]), (top_ref[...], low_ref[...]), ((1,), (0,)))
    out_ref[...] = result
    mixing_ref[...] = jnp.sum(block_ref[:, 15, :], axis=0, keepdims=True)
    for r in range(OWN):
        first_ref[3 * r : 3 * r + 3, :] = result[ROWS * r : ROWS * r + 3, :]
        final_ref[3 * r : 3 * r + 3, :] = result[ROWS * r + 13 : ROWS * r + 16, :]


def spectrum(block):
    top, low = forward_table(shard_order())
    rows = OWN * ROWS
    return pl.pallas_call(
        spectrum_kernel,
        in_specs=whole(3),
        out_specs=whole(4),
        out_shape=[
            jax.ShapeDtypeStruct((rows, CIRCLE), F32),
            jax.ShapeDtypeStruct((3 * OWN, CIRCLE), F32),
            jax.ShapeDtypeStruct((3 * OWN, CIRCLE), F32),
            jax.ShapeDtypeStruct((1, 128), F32),
        ],
        scratch_shapes=[pltpu.VMEM((rows, CIRCLE), F32)],
        compiler_params=params(24),
        cost_estimate=cost(6 * rows * CIRCLE * CIRCLE, 4_000_000),
        name="spectrum",
    )(block, jnp.asarray(top), jnp.asarray(low))


def kernel_spectrum_kernel(kernel_ref, top_ref, low_ref, out_ref):
    out_ref[...] = dot3(split(kernel_ref[...]), (top_ref[...], low_ref[...]), ((1,), (0,)))


def kernel_spectrum(kernels):
    top, low = forward_table(np.arange(CIRCLE))
    rows = BASIS * TAPS * ROWS
    flat = kernels.transpose(0, 2, 1, 3).reshape(rows, CIRCLE)
    return pl.pallas_call(
        kernel_spectrum_kernel,
        in_specs=whole(3),
        out_specs=whole(1)[0],
        out_shape=jax.ShapeDtypeStruct((rows, CIRCLE), F32),
        compiler_params=params(24),
        cost_estimate=cost(6 * rows * CIRCLE * CIRCLE, 5_000_000),
        name="kernel_spectrum",
    )(flat, jnp.asarray(top), jnp.asarray(low))


def filter_kernel(
    mixing_ref, data_ref, before_ref, after_ref, kernel_ref, top_ref, low_ref, out_ref, rows_ref, sum_ref
):
    for r in range(OWN):
        rows_ref[r, 0:3, :] = before_ref[3 * r : 3 * r + 3, :]
        rows_ref[r, 3 : 3 + ROWS, :] = data_ref[ROWS * r : ROWS * (r + 1), :]
        rows_ref[r, 3 + ROWS : 6 + ROWS, :] = after_ref[3 * r : 3 * r + 3, :]
    lane = lax.broadcasted_iota(jnp.int32, (ROWS, HALF), 1)
    ends = lane == 0

    def channel(r, carry):
        real = jnp.zeros((ROWS, HALF), F32)
        imag = jnp.zeros((ROWS, HALF), F32)
        for k in range(TAPS):
            mixed_real = jnp.zeros((ROWS, HALF), F32)
            mixed_imag = jnp.zeros((ROWS, HALF), F32)
            for b in range(BASIS):
                weight = mixing_ref[0, BASIS * r + b]
                at = ROWS * (TAPS * b + k)
                mixed_real += weight * kernel_ref[at : at + ROWS, 0:HALF]
                mixed_imag += weight * kernel_ref[at : at + ROWS, HALF:CIRCLE]
            own = jnp.where(ends, mixed_imag, mixed_real)
            cross = jnp.where(ends, 0.0, mixed_imag)
            data_real = rows_ref[r, 6 - k : 6 - k + ROWS, 0:HALF]
            data_imag = rows_ref[r, 6 - k : 6 - k + ROWS, HALF:CIRCLE]
            real += mixed_real * data_real + cross * data_imag
            imag += own * data_imag - cross * data_real
        sum_ref[r, :, 0:HALF] = real
        sum_ref[r, :, HALF:CIRCLE] = imag
        return carry

    lax.fori_loop(0, OWN, channel, 0)
    total = split(sum_ref[...].reshape(OWN * ROWS, CIRCLE))
    field = dot3((top_ref[...], low_ref[...]), total, ((1,), (1,)))
    for l in range(COLS):
        out_ref[:, l, :] = field[SHARDS * l : SHARDS * (l + 1), 0:128]
    for q in range(3):
        pieces = [
            field[SHARDS * (3 * g + q) : SHARDS * (3 * g + q + 1), 128:160] for g in range(4)
        ]
        out_ref[:, 12 + q, :] = jnp.concatenate(pieces, axis=1)
    out_ref[:, 15, :] = jnp.zeros((SHARDS, 128), F32)


def filtered(mixing, data, before, after, kernel):
    top, low = backward_table(shard_order())
    return pl.pallas_call(
        filter_kernel,
        in_specs=[pl.BlockSpec(memory_space=pltpu.SMEM)] + whole(6),
        out_specs=whole(1)[0],
        out_shape=jax.ShapeDtypeStruct((SHARDS, 16, 128), F32),
        scratch_shapes=[
            pltpu.VMEM((OWN, 24, CIRCLE), F32),
            pltpu.VMEM((OWN, ROWS, CIRCLE), F32),
        ],
        compiler_params=params(32),
        cost_estimate=cost(6 * OWN * ROWS * CIRCLE * CIRCLE, 5_000_000),
        name="filter",
    )(mixing, data, before, after, kernel, jnp.asarray(top), jnp.asarray(low))


def unpack_kernel(block_ref, out_ref):
    def put(l, r, pair):
        out_ref[ROWS * l : ROWS * (l + 1), SHARDS * r : SHARDS * (r + 2)] = jnp.concatenate(
            pair, axis=1
        )

    for l in range(COLS):
        turned = block_ref[:, l, :].T
        for r in range(0, 8, 2):
            put(l, r, [turned[ROWS * r : ROWS * (r + 1)], turned[ROWS * (r + 1) : ROWS * (r + 2)]])
    for q in range(3):
        turned = block_ref[:, 12 + q, :].T
        for g in range(4):
            at = 32 * g
            put(3 * g + q, 8, [turned[at : at + ROWS], turned[at + ROWS : at + 2 * ROWS]])


def unpack(block):
    return pl.pallas_call(
        unpack_kernel,
        in_specs=whole(1),
        out_specs=whole(1)[0],
        out_shape=jax.ShapeDtypeStruct((ROWS * COLS, SHARDS * OWN), F32),
        name="unpack",
    )(block)


def across(block):
    return lax.all_to_all(block, LON, split_axis=0, concat_axis=0, tiled=True)


def per_device(activation, cotangent, weight_in, weight_out, kernels, mixing):
    points = ROWS * COLS
    width = activation.shape[2]
    act = activation.transpose(1, 0, 2).reshape(points, width)
    cot = cotangent.transpose(1, 0, 2).reshape(points, width)
    place = jnp.stack([lax.axis_index(axis) for axis in (LON, "co", "yl", "yh", "x")])
    block, own, other = mlp(place, mixing, act, cot, weight_in, weight_out)
    arrived = lax.ppermute(other, "co", [(0, 1), (1, 0)])
    cut = small(cut_kernel, (place, own, arrived), [(160, 640)] * 8, 1, name="cut")
    spread = across(after(block, cut[0]))
    moved = exchange_x(cut[:4]) + exchange_y(cut[4:])
    swapped = small(
        swap_kernel, (place, *moved), [(40, 640)] * 8, 1, (pltpu.VMEM((4, 40, 640), F32),), "swap"
    )
    moved = exchange_y(swapped[:4]) + exchange_x(swapped[4:])
    kernel = kernel_spectrum(kernels)
    data, first, final, own_mixing = spectrum(after(spread, swapped[0]))
    forward = [(i, i + 1) for i in range(3)]
    backward = [(target, source) for source, target in forward]
    before = lax.ppermute(final, LAT, forward)
    after_rows = lax.ppermute(first, LAT, backward)
    sent = filtered(own_mixing, data, before, after_rows, kernel)
    (blocks,) = small(stack_kernel, moved, [(192, 384)], name="stack")
    result = across(after(sent, blocks))
    total = lax.psum_scatter(blocks, "z", scatter_dimension=0, tiled=True)
    grad_in, grad_out = small(last_kernel, (place, total), [(20, 160)] * 2, 1, name="last")
    field = unpack(result).reshape(COLS, ROWS, width).transpose(1, 0, 2)
    return (field, grad_in, grad_out)


def solution(mesh):
    fine = Mesh(mesh.devices.reshape(2, 2, 4, 8, 2), AXES)
    placed = (
        P(LAT, LON, None),
        P(LAT, LON, None),
        P(),
        P(),
        P(None, LAT, None, None),
        P(LON, None),
    )
    return jax.shard_map(
        per_device,
        mesh=fine,
        in_specs=placed,
        out_specs=(P(LAT, LON, None), P(LON, LAT), P(LON, LAT)),
        check_vma=False,
    )
```

```python
import functools
import math

import jax
import jax.numpy as jnp
import ml_dtypes
import numpy as np
from jax import lax
from jax.experimental import pallas as pl
from jax.experimental.pallas import tpu as pltpu
from jax.sharding import Mesh
from jax.sharding import PartitionSpec as P

AXES = ("yl", "co", "x", "z", "yh")
LAT = ("yl", "co")
LON = ("x", "z", "yh")
F32 = jnp.float32
BF16 = jnp.bfloat16
SHARDS = 64
COLS = 12
ROWS = 16
OWN = 10
CIRCLE = 768
HALF = 384
TAPS = 7
BASIS = 3
MIB = 1 << 20


def split(value):
    top = value.astype(BF16)
    return top, (value - top.astype(F32)).astype(BF16)


def dot3(left, right, dims):
    (a, b), (c, d) = left, right
    numbers = (dims, ((), ()))
    one = functools.partial(lax.dot_general, dimension_numbers=numbers, preferred_element_type=F32)
    return one(a, c) + (one(a, d) + one(b, c))


def whole(n):
    return [pl.BlockSpec(memory_space=pltpu.VMEM)] * n


def params(mib):
    return pltpu.CompilerParams(vmem_limit_bytes=mib * MIB)


def cost(flops, moved):
    return pl.CostEstimate(flops=flops, bytes_accessed=moved, transcendentals=0)


def table(order):
    angle = 2.0 * np.pi / CIRCLE * (order[:, None] * np.arange(HALF)[None, :] % CIRCLE)
    nyquist = np.where(order % 2 == 0, 1.0, -1.0)
    real, imag = np.cos(angle), -np.sin(angle)
    imag[:, 0] = nyquist
    return np.concatenate([real, imag], axis=1)


def parts(matrix):
    exact = matrix.astype(np.float32)
    top = exact.astype(ml_dtypes.bfloat16)
    return top, (exact - top.astype(np.float32)).astype(ml_dtypes.bfloat16)


def forward_table(order):
    return parts(table(order))


def backward_table(order):
    weight = np.full((2, HALF), 2.0 / CIRCLE)
    weight[:, 0] = 1.0 / CIRCLE
    return parts(table(order) * weight.reshape(1, -1))


def shard_order():
    return (np.arange(COLS)[:, None] + COLS * np.arange(SHARDS)[None, :]).reshape(-1)


def pack(unit, mixing_ref, shard, out_ref):
    def piece(l, r):
        return unit[ROWS * l : ROWS * (l + 1), SHARDS * r : SHARDS * (r + 1)]

    for l in range(COLS):
        out_ref[:, l, :] = jnp.concatenate([piece(l, r) for r in range(8)], axis=0).T
    for q in range(3):
        chunk = [piece(3 * g + q, r) for g in range(4) for r in (8, 9)]
        out_ref[:, 12 + q, :] = jnp.concatenate(chunk, axis=0).T
    target = lax.broadcasted_iota(jnp.int32, (SHARDS, 128), 0)
    lane = lax.broadcasted_iota(jnp.int32, (SHARDS, 128), 1)
    weights = jnp.zeros((SHARDS, 128), F32)
    for i in range(OWN):
        channel = OWN * shard + i
        here = target == lax.rem(channel, SHARDS)
        first = BASIS * lax.div(channel, SHARDS)
        for b in range(BASIS):
            weights = jnp.where(here & (lane == first + b), mixing_ref[b, i], weights)
    out_ref[:, 15, :] = weights


def mlp_kernel(
    place_ref,
    mixing_ref,
    act_ref,
    cot_ref,
    in_ref,
    out_ref,
    block_ref,
    own_ref,
    other_ref,
    unit_ref,
    act_top,
    act_low,
    cot_top,
    cot_low,
    cot_cols_top,
    cot_cols_low,
):
    step = pl.program_id(0)

    @pl.when(step == 0)
    def _():
        act, cot = act_ref[...], cot_ref[...]
        act_top[...], act_low[...] = split(act)
        cot_top[...], cot_low[...] = split(cot)
        pairs = [cot[:, 160:320], cot[:, 0:160], cot[:, 480:640], cot[:, 320:480]]
        cot_cols_top[...], cot_cols_low[...] = split(jnp.concatenate(pairs, axis=1))

    w_in, w_out = split(in_ref[...]), split(out_ref[...])
    preact = dot3((act_top[...], act_low[...]), w_in, ((1,), (1,)))
    cdf = 0.5 * (1.0 + lax.erf(preact * (1.0 / math.sqrt(2.0))))
    density = jnp.exp(-0.5 * preact * preact) * (1.0 / math.sqrt(2.0 * math.pi))
    hidden = split(preact * cdf)
    slope = cdf + preact * density
    grad = split(dot3((cot_top[...], cot_low[...]), w_out, ((1,), (1,))) * slope)
    term = dot3(grad, w_in, ((1,), (0,)))

    @pl.when(step == 0)
    def _():
        unit_ref[...] = cot_ref[...] + term

    @pl.when(step > 0)
    def _():
        unit_ref[...] += term

    contract = ((0,), (0,))
    first = dot3(grad, (act_top[...], act_low[...]), contract)
    second = dot3(hidden, (cot_cols_top[...], cot_cols_low[...]), contract)
    lane = lax.broadcasted_iota(jnp.int32, first.shape, 1)
    even = (lane < 160) | ((lane >= 320) & (lane < 480))
    mine = even == (place_ref[1] == 0)
    own_ref[...] = jnp.where(mine, first, second)
    other_ref[...] = jnp.where(mine, second, first)

    @pl.when(step == pl.num_programs(0) - 1)
    def _():
        pack(unit_ref[...], mixing_ref, place_ref[0], block_ref)


def mlp(place, mixing, act, cot, weight_in, weight_out):
    points, width = act.shape
    units = weight_in.shape[0]
    tile = 256
    full = lambda shape: pl.BlockSpec(shape, lambda i: (0,) * len(shape))
    rows = pl.BlockSpec((tile, width), lambda i: (i, 0))
    scalars = pl.BlockSpec(memory_space=pltpu.SMEM)
    return pl.pallas_call(
        mlp_kernel,
        grid=(units // tile,),
        in_specs=[scalars, scalars, full((points, width)), full((points, width)), rows, rows],
        out_specs=[full((SHARDS, 16, 128)), rows, rows],
        out_shape=[
            jax.ShapeDtypeStruct((SHARDS, 16, 128), F32),
            jax.ShapeDtypeStruct((units, width), F32),
            jax.ShapeDtypeStruct((units, width), F32),
        ],
        scratch_shapes=[pltpu.VMEM((points, width), F32)]
        + [pltpu.VMEM((points, width), BF16)] * 6,
        compiler_params=params(60),
        cost_estimate=cost(30 * points * width * units, 15_000_000),
        name="mlp",
    )(place, mixing, act, cot, weight_in, weight_out)


def partner(place_ref, m):
    upper, right = place_ref[2], place_ref[3]
    return 2 * (1 - upper if m & 2 else upper) + (1 - right if m & 1 else right)


def by_chip(rows):
    low = jnp.concatenate([rows[40 * z : 40 * z + 20] for z in range(4)], axis=0)
    high = jnp.concatenate([rows[40 * z + 20 : 40 * z + 40] for z in range(4)], axis=0)
    return [low[:, 0:320], high[:, 0:320], low[:, 320:640], high[:, 320:640]]


def cut_kernel(place_ref, own_ref, arrived_ref, half_ref, *refs):
    outs, kept_ref = refs[:4], refs[4]
    x = pl.program_id(0)
    half_ref[...] = own_ref[0:160, :] + arrived_ref[0:160, :]
    pieces = by_chip(own_ref[160:320, :] + arrived_ref[160:320, :])
    for at in range(4):

        @pl.when(x == at)
        def _():
            row, col = 80 * (at % 2), 320 * (at // 2)
            for chip in range(4):
                kept_ref[chip, row : row + 80, col : col + 320] = pieces[chip]

    @pl.when(x == 3)
    def _():
        for m in range(4):
            outs[m][...] = kept_ref[partner(place_ref, m)]


def cut(place, own, arrived):
    rows = pl.BlockSpec((320, 640), lambda i: (i, 0))
    return pl.pallas_call(
        cut_kernel,
        grid=(4,),
        in_specs=[pl.BlockSpec(memory_space=pltpu.SMEM), rows, rows],
        out_specs=[pl.BlockSpec((160, 640), lambda i: (i, 0))]
        + [pl.BlockSpec((160, 640), lambda i: (0, 0))] * 4,
        out_shape=[jax.ShapeDtypeStruct((640, 640), F32)]
        + [jax.ShapeDtypeStruct((160, 640), F32)] * 4,
        scratch_shapes=[pltpu.VMEM((4, 160, 640), F32)],
        compiler_params=params(60),
        cost_estimate=cost(2_000_000, 10_000_000),
        name="cut",
    )(place, own, arrived)


def swap_kernel(place_ref, half_ref, *refs):
    ins, outs, kept_ref = refs[:4], refs[4:12], refs[12]
    along_y = (ins[0][...] + ins[1][...]) + (ins[2][...] + ins[3][...])
    for chip, piece in enumerate(by_chip(half_ref[...])):
        kept_ref[chip] = jnp.concatenate([piece[0:40], piece[40:80]], axis=1)
    for x in range(4):
        row, col = 80 * (x % 2), 320 * (x // 2)
        part = along_y[row : row + 80, col : col + 320]
        kept_ref[4 + x] = jnp.concatenate([part[0:40], part[40:80]], axis=1)
    for m in range(4):
        outs[m][...] = kept_ref[partner(place_ref, m)]
        outs[4 + m][...] = kept_ref[4 + lax.rem(place_ref[4] + m, 4)]


def stack_kernel(*refs):
    out_ref = refs[8]
    out_ref[...] = jnp.zeros(out_ref.shape, F32)
    for half in range(2):
        ins = refs[4 * half : 4 * half + 4]
        total = (ins[0][...] + ins[1][...]) + (ins[2][...] + ins[3][...])
        for z in range(4):
            row, col = 20 * (z % 2), 320 * (z // 2)
            out_ref[4 * half + z, 0:20, 0:320] = total[row : row + 20, col : col + 320]


def last_kernel(place_ref, blocks_ref, first_ref, second_ref):
    total = blocks_ref[0, 0:20, 0:320]
    for z in range(1, 8):
        total += blocks_ref[z, 0:20, 0:320]
    even = place_ref[1] == 0
    first_ref[...] = jnp.where(even, total[:, 0:160], total[:, 160:320])
    second_ref[...] = jnp.where(even, total[:, 160:320], total[:, 0:160])


def small(kernel, operands, shapes, scalars=0, scratch=(), name=None):
    return pl.pallas_call(
        kernel,
        in_specs=[pl.BlockSpec(memory_space=pltpu.SMEM)] * scalars
        + whole(len(operands) - scalars),
        out_specs=whole(len(shapes)),
        out_shape=[jax.ShapeDtypeStruct(shape, F32) for shape in shapes],
        scratch_shapes=scratch,
        compiler_params=params(32),
        name=name,
    )(*operands)


def exchange_x(pieces):
    return [pieces[0]] + [
        lax.ppermute(pieces[m], "x", [(i, (i + m) % 4) for i in range(4)]) for m in (1, 2, 3)
    ]


def exchange_y(pieces):
    return [pieces[0]] + [
        lax.ppermute(pieces[m], ("yl", "yh"), [(i, i ^ m) for i in range(4)]) for m in (1, 2, 3)
    ]


def after(value, earlier):
    return lax.optimization_barrier((value, earlier))[0]


def spectrum_kernel(
    block_ref, top_ref, low_ref, out_ref, first_ref, final_ref, mixing_ref, flat_ref
):
    for p in range(COLS // 2):
        pair = jnp.concatenate([block_ref[:, 2 * p, :], block_ref[:, 2 * p + 1, :]], axis=0)
        flat_ref[0:128, 128 * p : 128 * (p + 1)] = pair.T
    rest = [block_ref[:, 12 + q, :].T for q in range(3)]
    pieces = [rest[q][32 * g : 32 * (g + 1), :] for g in range(4) for q in range(3)]
    flat_ref[128:160, :] = jnp.concatenate(pieces, axis=1)
    result = dot3(split(flat_ref[...]), (top_ref[...], low_ref[...]), ((1,), (0,)))
    out_ref[...] = result
    mixing_ref[...] = jnp.sum(block_ref[:, 15, :], axis=0, keepdims=True)
    for r in range(OWN):
        first_ref[3 * r : 3 * r + 3, :] = result[ROWS * r : ROWS * r + 3, :]
        final_ref[3 * r : 3 * r + 3, :] = result[ROWS * r + 13 : ROWS * r + 16, :]


def spectrum(block):
    top, low = forward_table(shard_order())
    rows = OWN * ROWS
    return pl.pallas_call(
        spectrum_kernel,
        in_specs=whole(3),
        out_specs=whole(4),
        out_shape=[
            jax.ShapeDtypeStruct((rows, CIRCLE), F32),
            jax.ShapeDtypeStruct((3 * OWN, CIRCLE), F32),
            jax.ShapeDtypeStruct((3 * OWN, CIRCLE), F32),
            jax.ShapeDtypeStruct((1, 128), F32),
        ],
        scratch_shapes=[pltpu.VMEM((rows, CIRCLE), F32)],
        compiler_params=params(24),
        cost_estimate=cost(6 * rows * CIRCLE * CIRCLE, 4_000_000),
        name="spectrum",
    )(block, jnp.asarray(top), jnp.asarray(low))


def kernel_spectrum_kernel(kernel_ref, top_ref, low_ref, out_ref):
    out_ref[...] = dot3(split(kernel_ref[...]), (top_ref[...], low_ref[...]), ((1,), (0,)))


def kernel_spectrum(kernels):
    top, low = forward_table(np.arange(CIRCLE))
    rows = BASIS * TAPS * ROWS
    flat = kernels.transpose(0, 2, 1, 3).reshape(rows, CIRCLE)
    return pl.pallas_call(
        kernel_spectrum_kernel,
        in_specs=whole(3),
        out_specs=whole(1)[0],
        out_shape=jax.ShapeDtypeStruct((rows, CIRCLE), F32),
        compiler_params=params(24),
        cost_estimate=cost(6 * rows * CIRCLE * CIRCLE, 5_000_000),
        name="kernel_spectrum",
    )(flat, jnp.asarray(top), jnp.asarray(low))


def filter_kernel(
    mixing_ref, data_ref, before_ref, after_ref, kernel_ref, top_ref, low_ref, out_ref, rows_ref, sum_ref
):
    for r in range(OWN):
        rows_ref[r, 0:3, :] = before_ref[3 * r : 3 * r + 3, :]
        rows_ref[r, 3 : 3 + ROWS, :] = data_ref[ROWS * r : ROWS * (r + 1), :]
        rows_ref[r, 3 + ROWS : 6 + ROWS, :] = after_ref[3 * r : 3 * r + 3, :]
    lane = lax.broadcasted_iota(jnp.int32, (ROWS, HALF), 1)
    ends = lane == 0

    def channel(r, carry):
        real = jnp.zeros((ROWS, HALF), F32)
        imag = jnp.zeros((ROWS, HALF), F32)
        for k in range(TAPS):
            mixed_real = jnp.zeros((ROWS, HALF), F32)
            mixed_imag = jnp.zeros((ROWS, HALF), F32)
            for b in range(BASIS):
                weight = mixing_ref[0, BASIS * r + b]
                at = ROWS * (TAPS * b + k)
                mixed_real += weight * kernel_ref[at : at + ROWS, 0:HALF]
                mixed_imag += weight * kernel_ref[at : at + ROWS, HALF:CIRCLE]
            own = jnp.where(ends, mixed_imag, mixed_real)
            cross = jnp.where(ends, 0.0, mixed_imag)
            data_real = rows_ref[r, 6 - k : 6 - k + ROWS, 0:HALF]
            data_imag = rows_ref[r, 6 - k : 6 - k + ROWS, HALF:CIRCLE]
            real += mixed_real * data_real + cross * data_imag
            imag += own * data_imag - cross * data_real
        sum_ref[r, :, 0:HALF] = real
        sum_ref[r, :, HALF:CIRCLE] = imag
        return carry

    lax.fori_loop(0, OWN, channel, 0)
    total = split(sum_ref[...].reshape(OWN * ROWS, CIRCLE))
    field = dot3((top_ref[...], low_ref[...]), total, ((1,), (1,)))
    for l in range(COLS):
        out_ref[:, l, :] = field[SHARDS * l : SHARDS * (l + 1), 0:128]
    for q in range(3):
        pieces = [
            field[SHARDS * (3 * g + q) : SHARDS * (3 * g + q + 1), 128:160] for g in range(4)
        ]
        out_ref[:, 12 + q, :] = jnp.concatenate(pieces, axis=1)
    out_ref[:, 15, :] = jnp.zeros((SHARDS, 128), F32)


def filtered(mixing, data, before, after, kernel):
    top, low = backward_table(shard_order())
    return pl.pallas_call(
        filter_kernel,
        in_specs=[pl.BlockSpec(memory_space=pltpu.SMEM)] + whole(6),
        out_specs=whole(1)[0],
        out_shape=jax.ShapeDtypeStruct((SHARDS, 16, 128), F32),
        scratch_shapes=[
            pltpu.VMEM((OWN, 24, CIRCLE), F32),
            pltpu.VMEM((OWN, ROWS, CIRCLE), F32),
        ],
        compiler_params=params(32),
        cost_estimate=cost(6 * OWN * ROWS * CIRCLE * CIRCLE, 5_000_000),
        name="filter",
    )(mixing, data, before, after, kernel, jnp.asarray(top), jnp.asarray(low))


def unpack_kernel(block_ref, out_ref):
    def put(l, r, pair):
        out_ref[ROWS * l : ROWS * (l + 1), SHARDS * r : SHARDS * (r + 2)] = jnp.concatenate(
            pair, axis=1
        )

    for l in range(COLS):
        turned = block_ref[:, l, :].T
        for r in range(0, 8, 2):
            put(l, r, [turned[ROWS * r : ROWS * (r + 1)], turned[ROWS * (r + 1) : ROWS * (r + 2)]])
    for q in range(3):
        turned = block_ref[:, 12 + q, :].T
        for g in range(4):
            at = 32 * g
            put(3 * g + q, 8, [turned[at : at + ROWS], turned[at + ROWS : at + 2 * ROWS]])


def unpack(block):
    return pl.pallas_call(
        unpack_kernel,
        in_specs=whole(1),
        out_specs=whole(1)[0],
        out_shape=jax.ShapeDtypeStruct((ROWS * COLS, SHARDS * OWN), F32),
        name="unpack",
    )(block)


def across(block):
    return lax.all_to_all(block, LON, split_axis=0, concat_axis=0, tiled=True)


def per_device(activation, cotangent, weight_in, weight_out, kernels, mixing):
    points = ROWS * COLS
    width = activation.shape[2]
    act = activation.transpose(1, 0, 2).reshape(points, width)
    cot = cotangent.transpose(1, 0, 2).reshape(points, width)
    place = jnp.stack([lax.axis_index(axis) for axis in (LON, "co", "yl", "yh", "x")])
    block, own, other = mlp(place, mixing.T, act, cot, weight_in, weight_out)
    arrived = lax.ppermute(other, "co", [(0, 1), (1, 0)])
    half, *pieces = cut(place, own, arrived)
    half = lax.psum_scatter(half, "x", scatter_dimension=0, tiled=True)
    moved = exchange_y(pieces)
    spread = across(block)
    kernel = kernel_spectrum(kernels)
    data, first, final, own_mixing = spectrum(after(spread, moved))
    forward = [(i, i + 1) for i in range(3)]
    backward = [(target, source) for source, target in forward]
    before = lax.ppermute(final, LAT, forward)
    beyond = lax.ppermute(first, LAT, backward)
    result = across(filtered(own_mixing, data, before, beyond, kernel))
    swapped = small(
        swap_kernel, (place, half, *moved), [(40, 640)] * 8, 1, (pltpu.VMEM((8, 40, 640), F32),), "swap"
    )
    moved = exchange_y(swapped[:4]) + exchange_x(swapped[4:])
    (blocks,) = small(stack_kernel, moved, [(8, 24, 384)], name="stack")
    blocks = lax.all_to_all(blocks, "z", split_axis=0, concat_axis=0, tiled=True)
    grad_in, grad_out = small(last_kernel, (place, blocks), [(20, 160)] * 2, 1, name="last")
    field = unpack(result).reshape(COLS, ROWS, width).transpose(1, 0, 2)
    return (field, grad_in, grad_out)


def solution(mesh):
    fine = Mesh(mesh.devices.reshape(2, 2, 4, 8, 2), AXES)
    placed = (
        P(LAT, LON, None),
        P(LAT, LON, None),
        P(),
        P(),
        P(None, LAT, None, None),
        P(LON, None),
    )
    return jax.shard_map(
        per_device,
        mesh=fine,
        in_specs=placed,
        out_specs=(P(LAT, LON, None), P(LON, LAT), P(LON, LAT)),
        check_vma=False,
    )
```

```python
import functools
import math

import jax
import jax.numpy as jnp
import ml_dtypes
import numpy as np
from jax import lax
from jax.experimental import pallas as pl
from jax.experimental.pallas import tpu as pltpu
from jax.sharding import Mesh
from jax.sharding import PartitionSpec as P

AXES = ("yl", "co", "x", "z", "yh")
LAT = ("yl", "co")
LON = ("x", "z", "yh")
F32 = jnp.float32
BF16 = jnp.bfloat16
SHARDS = 64
COLS = 12
ROWS = 16
OWN = 10
CIRCLE = 768
HALF = 384
TAPS = 7
BASIS = 3
MIB = 1 << 20


def split(value):
    top = value.astype(BF16)
    return top, (value - top.astype(F32)).astype(BF16)


def dot3(left, right, dims):
    (a, b), (c, d) = left, right
    numbers = (dims, ((), ()))
    one = functools.partial(lax.dot_general, dimension_numbers=numbers, preferred_element_type=F32)
    return one(a, c) + (one(a, d) + one(b, c))


def whole(n):
    return [pl.BlockSpec(memory_space=pltpu.VMEM)] * n


def params(mib):
    return pltpu.CompilerParams(vmem_limit_bytes=mib * MIB)


def cost(flops, moved):
    return pl.CostEstimate(flops=flops, bytes_accessed=moved, transcendentals=0)


def table(order):
    angle = 2.0 * np.pi / CIRCLE * (order[:, None] * np.arange(HALF)[None, :] % CIRCLE)
    nyquist = np.where(order % 2 == 0, 1.0, -1.0)
    real, imag = np.cos(angle), -np.sin(angle)
    imag[:, 0] = nyquist
    return np.concatenate([real, imag], axis=1)


def parts(matrix):
    exact = matrix.astype(np.float32)
    top = exact.astype(ml_dtypes.bfloat16)
    return top, (exact - top.astype(np.float32)).astype(ml_dtypes.bfloat16)


def forward_table(order):
    return parts(table(order))


def backward_table(order):
    weight = np.full((2, HALF), 2.0 / CIRCLE)
    weight[:, 0] = 1.0 / CIRCLE
    return parts(table(order) * weight.reshape(1, -1))


def shard_order():
    return (np.arange(COLS)[:, None] + COLS * np.arange(SHARDS)[None, :]).reshape(-1)


def pack(unit, mixing_ref, shard, out_ref):
    def piece(l, r):
        return unit[ROWS * l : ROWS * (l + 1), SHARDS * r : SHARDS * (r + 1)]

    for l in range(COLS):
        out_ref[:, l, :] = jnp.concatenate([piece(l, r) for r in range(8)], axis=0).T
    for q in range(3):
        chunk = [piece(3 * g + q, r) for g in range(4) for r in (8, 9)]
        out_ref[:, 12 + q, :] = jnp.concatenate(chunk, axis=0).T
    target = lax.broadcasted_iota(jnp.int32, (SHARDS, 128), 0)
    lane = lax.broadcasted_iota(jnp.int32, (SHARDS, 128), 1)
    weights = jnp.zeros((SHARDS, 128), F32)
    for i in range(OWN):
        channel = OWN * shard + i
        here = target == lax.rem(channel, SHARDS)
        first = BASIS * lax.div(channel, SHARDS)
        for b in range(BASIS):
            weights = jnp.where(here & (lane == first + b), mixing_ref[b, i], weights)
    out_ref[:, 15, :] = weights


def pack_kernel(place_ref, mixing_ref, unit_ref, arrived_ref, block_ref):
    pack(unit_ref[...] + arrived_ref[...], mixing_ref, place_ref[0], block_ref)


def along_x(place_ref, m):
    return lax.rem(place_ref[4] + m, 4)


def along_y(place_ref, m):
    upper, right = place_ref[2], place_ref[3]
    return 2 * (1 - upper if m & 2 else upper) + (1 - right if m & 1 else right)


def low_high(rows):
    low = jnp.concatenate([rows[40 * z : 40 * z + 20] for z in range(4)], axis=0)
    high = jnp.concatenate([rows[40 * z + 20 : 40 * z + 40] for z in range(4)], axis=0)
    return low, high


def mlp_kernel(
    place_ref,
    act_ref,
    act_other_ref,
    cot_ref,
    cot_other_ref,
    in_ref,
    out_ref,
    own_ref,
    other_ref,
    *refs,
):
    outs, (unit_ref, act_top, act_low, cot_top, cot_low, kept_ref) = refs[:4], refs[4:]
    step = pl.program_id(0)
    core = place_ref[1]
    points = act_ref.shape[0]

    @pl.when(step == 0)
    def _():
        act_top[0:points, :], act_low[0:points, :] = split(act_ref[...])
        act_top[points:, :], act_low[points:, :] = split(act_other_ref[...])
        cot_top[0:points, :], cot_low[0:points, :] = split(cot_ref[...])
        cot_top[points:, :], cot_low[points:, :] = split(cot_other_ref[...])

    act, cot = (act_top[...], act_low[...]), (cot_top[...], cot_low[...])
    w_in = split(in_ref[...].reshape(320, 640))
    w_out = split(out_ref[...].reshape(320, 640))
    preact = dot3(act, w_in, ((1,), (1,)))
    cdf = 0.5 * (1.0 + lax.erf(preact * (1.0 / math.sqrt(2.0))))
    density = jnp.exp(-0.5 * preact * preact) * (1.0 / math.sqrt(2.0 * math.pi))
    hidden = split(preact * cdf)
    slope = cdf + preact * density
    grad = split(dot3(cot, w_out, ((1,), (1,))) * slope)
    term = dot3(grad, w_in, ((1,), (0,)))
    contract = ((0,), (0,))
    first = dot3(grad, act, contract)
    second = dot3(hidden, cot, contract)

    @pl.when(step == 0)
    def _():
        unit_ref[...] = term

    @pl.when(core == 0)
    def _():
        for x in range(2):
            rows = slice(160 * x, 160 * x + 160)
            kept_ref[2 * step + x, :, 0:640] = first[rows]
            kept_ref[2 * step + x, :, 640:1280] = second[rows]

    @pl.when(core == 1)
    def _():
        lanes = pl.ds(pl.multiple_of(640 * step, 128), 640)
        for x in range(2):
            rows = slice(160 * x, 160 * x + 160)
            parts = zip(low_high(first[rows]), low_high(second[rows]))
            for right, (a, b) in enumerate(parts):
                for upper in range(2):
                    cols = slice(320 * upper, 320 * upper + 320)
                    piece = jnp.concatenate([a[:, cols], b[:, cols]], axis=1)
                    kept_ref[2 * upper + right, 80 * x : 80 * x + 80, lanes] = piece

    @pl.when(step == 1)
    def _():
        total = unit_ref[...] + term
        own_ref[...] = cot_ref[...] + total[0:points]
        other_ref[...] = total[points:]
        for m in range(4):
            index = jnp.where(core == 0, along_x(place_ref, m), along_y(place_ref, m))
            outs[m][...] = kept_ref[index]


def mlp(place, act, act_other, cot, cot_other, weight_in, weight_out):
    points, width = act.shape
    units = weight_in.shape[0]
    full = lambda shape: pl.BlockSpec(shape, lambda i, place: (0,) * len(shape))
    rows = pl.BlockSpec((2, None, 160, width), lambda i, place: (i, place[1], 0, 0))
    return pl.pallas_call(
        mlp_kernel,
        grid_spec=pltpu.PrefetchScalarGridSpec(
            num_scalar_prefetch=1,
            grid=(2,),
            in_specs=[full((points, width))] * 4 + [rows, rows],
            out_specs=[full((points, width))] * 2 + [full((160, 1280))] * 4,
            scratch_shapes=[pltpu.VMEM((2 * points, width), F32)]
            + [pltpu.VMEM((2 * points, width), BF16)] * 4
            + [pltpu.VMEM((4, 160, 1280), F32)],
        ),
        out_shape=[jax.ShapeDtypeStruct((points, width), F32)] * 2
        + [jax.ShapeDtypeStruct((160, 1280), F32)] * 4,
        compiler_params=params(60),
        cost_estimate=cost(30 * points * width * units, 12_000_000),
        name="mlp",
    )(
        place,
        act,
        act_other,
        cot,
        cot_other,
        weight_in.reshape(4, 2, 160, width),
        weight_out.reshape(4, 2, 160, width),
    )


def swap_kernel(place_ref, *refs):
    ins, outs, kept_ref = refs[:4], refs[4:8], refs[8]
    core = place_ref[1]
    total = (ins[0][...] + ins[1][...]) + (ins[2][...] + ins[3][...])

    @pl.when(core == 0)
    def _():
        for right, part in enumerate(low_high(total)):
            for upper in range(2):
                at = 320 * upper
                pair = [part[:, at : at + 320], part[:, 640 + at : 960 + at]]
                kept_ref[2 * upper + right] = jnp.concatenate(pair, axis=1)

    @pl.when(core == 1)
    def _():
        for x in range(4):
            row, col = 80 * (x % 2), 640 * (x // 2)
            kept_ref[x] = total[row : row + 80, col : col + 640]

    for m in range(4):
        index = jnp.where(core == 0, along_y(place_ref, m), along_x(place_ref, m))
        outs[m][...] = kept_ref[index]


def pair_kernel(place_ref, *refs):
    ins, (mine_ref, send_ref) = refs[:4], refs[4:]
    total = (ins[0][...] + ins[1][...]) + (ins[2][...] + ins[3][...])
    even = jnp.concatenate([total[:, 0:160], total[:, 320:480]], axis=1)
    odd = jnp.concatenate([total[:, 160:320], total[:, 480:640]], axis=1)
    first = place_ref[1] == 0
    mine_ref[...] = jnp.where(first, even, odd)
    send_ref[...] = jnp.where(first, odd, even)


def stack_kernel(place_ref, mine_ref, arrived_ref, out_ref):
    out_ref[...] = jnp.zeros(out_ref.shape, F32)
    first = place_ref[1] == 0
    mine, arrived = mine_ref[...], arrived_ref[...]
    below, above = jnp.where(first, mine, arrived), jnp.where(first, arrived, mine)
    for z in range(4):
        out_ref[z, 0:20, 0:320] = below[20 * z : 20 * z + 20]
        out_ref[4 + z, 0:20, 0:320] = above[20 * z : 20 * z + 20]


def last_kernel(blocks_ref, first_ref, second_ref):
    total = blocks_ref[0, 0:20, 0:320]
    for z in range(1, 8):
        total += blocks_ref[z, 0:20, 0:320]
    first_ref[...] = total[:, 0:160]
    second_ref[...] = total[:, 160:320]


def small(kernel, operands, shapes, scalars=0, scratch=(), name=None):
    return pl.pallas_call(
        kernel,
        in_specs=[pl.BlockSpec(memory_space=pltpu.SMEM)] * scalars
        + whole(len(operands) - scalars),
        out_specs=whole(len(shapes)),
        out_shape=[jax.ShapeDtypeStruct(shape, F32) for shape in shapes],
        scratch_shapes=scratch,
        compiler_params=params(32),
        name=name,
    )(*operands)


def exchange(pieces, cores):
    def target(m, yl, co, x, z, yh):
        if cores[co] == "x":
            x = (x + m) % 4
        else:
            yl, yh = yl ^ (m >> 1), yh ^ (m & 1)
        return yl, co, x, z, yh

    sizes = (2, 2, 4, 8, 2)
    order = lambda at: int(np.ravel_multi_index(at, sizes))
    moved = [pieces[0]]
    for m in (1, 2, 3):
        pairs = [(order(at), order(target(m, *at))) for at in np.ndindex(*sizes)]
        moved.append(lax.ppermute(pieces[m], AXES, pairs))
    return moved


def to_core(value):
    return lax.ppermute(value, "co", [(0, 1), (1, 0)])


def after(value, earlier):
    return lax.optimization_barrier((value, earlier))[0]


def spectrum_kernel(
    block_ref, top_ref, low_ref, out_ref, first_ref, final_ref, mixing_ref, flat_ref
):
    for p in range(COLS // 2):
        pair = jnp.concatenate([block_ref[:, 2 * p, :], block_ref[:, 2 * p + 1, :]], axis=0)
        flat_ref[0:128, 128 * p : 128 * (p + 1)] = pair.T
    rest = [block_ref[:, 12 + q, :].T for q in range(3)]
    pieces = [rest[q][32 * g : 32 * (g + 1), :] for g in range(4) for q in range(3)]
    flat_ref[128:160, :] = jnp.concatenate(pieces, axis=1)
    result = dot3(split(flat_ref[...]), (top_ref[...], low_ref[...]), ((1,), (0,)))
    out_ref[...] = result
    mixing_ref[...] = jnp.sum(block_ref[:, 15, :], axis=0, keepdims=True)
    for r in range(OWN):
        first_ref[3 * r : 3 * r + 3, :] = result[ROWS * r : ROWS * r + 3, :]
        final_ref[3 * r : 3 * r + 3, :] = result[ROWS * r + 13 : ROWS * r + 16, :]


def spectrum(block):
    top, low = forward_table(shard_order())
    rows = OWN * ROWS
    return pl.pallas_call(
        spectrum_kernel,
        in_specs=whole(3),
        out_specs=whole(4),
        out_shape=[
            jax.ShapeDtypeStruct((rows, CIRCLE), F32),
            jax.ShapeDtypeStruct((3 * OWN, CIRCLE), F32),
            jax.ShapeDtypeStruct((3 * OWN, CIRCLE), F32),
            jax.ShapeDtypeStruct((1, 128), F32),
        ],
        scratch_shapes=[pltpu.VMEM((rows, CIRCLE), F32)],
        compiler_params=params(24),
        cost_estimate=cost(6 * rows * CIRCLE * CIRCLE, 4_000_000),
        name="spectrum",
    )(block, jnp.asarray(top), jnp.asarray(low))


def kernel_spectrum_kernel(kernel_ref, top_ref, low_ref, out_ref):
    out_ref[...] = dot3(split(kernel_ref[...]), (top_ref[...], low_ref[...]), ((1,), (0,)))


def kernel_spectrum(kernels):
    top, low = forward_table(np.arange(CIRCLE))
    rows = BASIS * TAPS * ROWS
    flat = kernels.transpose(0, 2, 1, 3).reshape(rows, CIRCLE)
    return pl.pallas_call(
        kernel_spectrum_kernel,
        in_specs=whole(3),
        out_specs=whole(1)[0],
        out_shape=jax.ShapeDtypeStruct((rows, CIRCLE), F32),
        compiler_params=params(24),
        cost_estimate=cost(6 * rows * CIRCLE * CIRCLE, 5_000_000),
        name="kernel_spectrum",
    )(flat, jnp.asarray(top), jnp.asarray(low))


def filter_kernel(
    mixing_ref, data_ref, before_ref, after_ref, kernel_ref, top_ref, low_ref, out_ref, rows_ref, sum_ref
):
    for r in range(OWN):
        rows_ref[r, 0:3, :] = before_ref[3 * r : 3 * r + 3, :]
        rows_ref[r, 3 : 3 + ROWS, :] = data_ref[ROWS * r : ROWS * (r + 1), :]
        rows_ref[r, 3 + ROWS : 6 + ROWS, :] = after_ref[3 * r : 3 * r + 3, :]
    lane = lax.broadcasted_iota(jnp.int32, (ROWS, HALF), 1)
    ends = lane == 0

    def channel(r, carry):
        real = jnp.zeros((ROWS, HALF), F32)
        imag = jnp.zeros((ROWS, HALF), F32)
        for k in range(TAPS):
            mixed_real = jnp.zeros((ROWS, HALF), F32)
            mixed_imag = jnp.zeros((ROWS, HALF), F32)
            for b in range(BASIS):
                weight = mixing_ref[0, BASIS * r + b]
                at = ROWS * (TAPS * b + k)
                mixed_real += weight * kernel_ref[at : at + ROWS, 0:HALF]
                mixed_imag += weight * kernel_ref[at : at + ROWS, HALF:CIRCLE]
            own = jnp.where(ends, mixed_imag, mixed_real)
            cross = jnp.where(ends, 0.0, mixed_imag)
            data_real = rows_ref[r, 6 - k : 6 - k + ROWS, 0:HALF]
            data_imag = rows_ref[r, 6 - k : 6 - k + ROWS, HALF:CIRCLE]
            real += mixed_real * data_real + cross * data_imag
            imag += own * data_imag - cross * data_real
        sum_ref[r, :, 0:HALF] = real
        sum_ref[r, :, HALF:CIRCLE] = imag
        return carry

    lax.fori_loop(0, OWN, channel, 0)
    total = split(sum_ref[...].reshape(OWN * ROWS, CIRCLE))
    field = dot3((top_ref[...], low_ref[...]), total, ((1,), (1,)))
    for l in range(COLS):
        out_ref[:, l, :] = field[SHARDS * l : SHARDS * (l + 1), 0:128]
    for q in range(3):
        pieces = [
            field[SHARDS * (3 * g + q) : SHARDS * (3 * g + q + 1), 128:160] for g in range(4)
        ]
        out_ref[:, 12 + q, :] = jnp.concatenate(pieces, axis=1)
    out_ref[:, 15, :] = jnp.zeros((SHARDS, 128), F32)


def filtered(mixing, data, before, after, kernel):
    top, low = backward_table(shard_order())
    return pl.pallas_call(
        filter_kernel,
        in_specs=[pl.BlockSpec(memory_space=pltpu.SMEM)] + whole(6),
        out_specs=whole(1)[0],
        out_shape=jax.ShapeDtypeStruct((SHARDS, 16, 128), F32),
        scratch_shapes=[
            pltpu.VMEM((OWN, 24, CIRCLE), F32),
            pltpu.VMEM((OWN, ROWS, CIRCLE), F32),
        ],
        compiler_params=params(32),
        cost_estimate=cost(6 * OWN * ROWS * CIRCLE * CIRCLE, 5_000_000),
        name="filter",
    )(mixing, data, before, after, kernel, jnp.asarray(top), jnp.asarray(low))


def unpack_kernel(block_ref, out_ref):
    def put(l, r, pair):
        out_ref[ROWS * l : ROWS * (l + 1), SHARDS * r : SHARDS * (r + 2)] = jnp.concatenate(
            pair, axis=1
        )

    for l in range(COLS):
        turned = block_ref[:, l, :].T
        for r in range(0, 8, 2):
            put(l, r, [turned[ROWS * r : ROWS * (r + 1)], turned[ROWS * (r + 1) : ROWS * (r + 2)]])
    for q in range(3):
        turned = block_ref[:, 12 + q, :].T
        for g in range(4):
            at = 32 * g
            put(3 * g + q, 8, [turned[at : at + ROWS], turned[at + ROWS : at + 2 * ROWS]])


def unpack(block):
    return pl.pallas_call(
        unpack_kernel,
        in_specs=whole(1),
        out_specs=whole(1)[0],
        out_shape=jax.ShapeDtypeStruct((ROWS * COLS, SHARDS * OWN), F32),
        name="unpack",
    )(block)


def across(block):
    return lax.all_to_all(block, LON, split_axis=0, concat_axis=0, tiled=True)


def per_device(activation, cotangent, weight_in, weight_out, kernels, mixing):
    points = ROWS * COLS
    width = activation.shape[2]
    act = activation.transpose(1, 0, 2).reshape(points, width)
    cot = cotangent.transpose(1, 0, 2).reshape(points, width)
    place = jnp.stack([lax.axis_index(axis) for axis in (LON, "co", "yl", "yh", "x")])
    unit, other, *pieces = mlp(place, act, to_core(act), cot, to_core(cot), weight_in, weight_out)
    (block,) = small(
        pack_kernel, (place, mixing.T, unit, to_core(other)), [(SHARDS, 16, 128)], 2, name="pack"
    )
    moved = exchange(pieces, "xy")
    spread = across(block)
    kernel = after(kernel_spectrum(kernels), moved)
    data, first, final, own_mixing = spectrum(spread)
    forward = [(i, i + 1) for i in range(3)]
    backward = [(target, source) for source, target in forward]
    before = lax.ppermute(final, LAT, forward)
    beyond = lax.ppermute(first, LAT, backward)
    result = across(filtered(own_mixing, data, before, beyond, kernel))
    kept = (pltpu.VMEM((4, 80, 640), F32),)
    swapped = small(swap_kernel, (place, *moved), [(80, 640)] * 4, 1, kept, "swap")
    moved = exchange(swapped, "yx")
    mine, send = small(pair_kernel, (place, *moved), [(80, 320)] * 2, 1, name="pair")
    (blocks,) = small(stack_kernel, (place, mine, to_core(send)), [(8, 24, 384)], 1, name="stack")
    blocks = lax.all_to_all(blocks, "z", split_axis=0, concat_axis=0, tiled=True)
    grad_in, grad_out = small(last_kernel, (blocks,), [(20, 160)] * 2, name="last")
    field = unpack(result).reshape(COLS, ROWS, width).transpose(1, 0, 2)
    return (field, grad_in, grad_out)


def solution(mesh):
    fine = Mesh(mesh.devices.reshape(2, 2, 4, 8, 2), AXES)
    placed = (
        P(LAT, LON, None),
        P(LAT, LON, None),
        P(),
        P(),
        P(None, LAT, None, None),
        P(LON, None),
    )
    return jax.shard_map(
        per_device,
        mesh=fine,
        in_specs=placed,
        out_specs=(P(LAT, LON, None), P(LON, LAT), P(LON, LAT)),
        check_vma=False,
    )
```

```python
import functools
import math

import jax
import jax.numpy as jnp
import ml_dtypes
import numpy as np
from jax import lax
from jax.experimental import pallas as pl
from jax.experimental.pallas import tpu as pltpu
from jax.sharding import Mesh
from jax.sharding import PartitionSpec as P

AXES = ("yl", "co", "x", "z", "yh")
LAT = ("yl", "co")
LON = ("x", "z", "yh")
F32 = jnp.float32
BF16 = jnp.bfloat16
SHARDS = 64
COLS = 12
ROWS = 16
OWN = 10
CIRCLE = 768
HALF = 384
TAPS = 7
BASIS = 3
MIB = 1 << 20


def split(value):
    top = value.astype(BF16)
    return top, (value - top.astype(F32)).astype(BF16)


def dot3(left, right, dims):
    (a, b), (c, d) = left, right
    numbers = (dims, ((), ()))
    one = functools.partial(lax.dot_general, dimension_numbers=numbers, preferred_element_type=F32)
    return one(a, c) + (one(a, d) + one(b, c))


def whole(n):
    return [pl.BlockSpec(memory_space=pltpu.VMEM)] * n


EARLIER = [pl.BlockSpec(memory_space=pl.ANY)]


def params(mib):
    return pltpu.CompilerParams(vmem_limit_bytes=mib * MIB)


def cost(flops, moved):
    return pl.CostEstimate(flops=flops, bytes_accessed=moved, transcendentals=0)


def table(order):
    angle = 2.0 * np.pi / CIRCLE * (order[:, None] * np.arange(HALF)[None, :] % CIRCLE)
    nyquist = np.where(order % 2 == 0, 1.0, -1.0)
    real, imag = np.cos(angle), -np.sin(angle)
    imag[:, 0] = nyquist
    return np.concatenate([real, imag], axis=1)


def parts(matrix):
    exact = matrix.astype(np.float32)
    top = exact.astype(ml_dtypes.bfloat16)
    return top, (exact - top.astype(np.float32)).astype(ml_dtypes.bfloat16)


def forward_table(order):
    return parts(table(order))


def backward_table(order):
    weight = np.full((2, HALF), 2.0 / CIRCLE)
    weight[:, 0] = 1.0 / CIRCLE
    return parts(table(order) * weight.reshape(1, -1))


def shard_order():
    return (np.arange(COLS)[:, None] + COLS * np.arange(SHARDS)[None, :]).reshape(-1)


def pack(unit, mixing_ref, shard, out_ref):
    def piece(l, r):
        return unit[ROWS * l : ROWS * (l + 1), SHARDS * r : SHARDS * (r + 1)]

    for l in range(COLS):
        out_ref[:, l, :] = jnp.concatenate([piece(l, r) for r in range(8)], axis=0).T
    for q in range(3):
        chunk = [piece(3 * g + q, r) for g in range(4) for r in (8, 9)]
        out_ref[:, 12 + q, :] = jnp.concatenate(chunk, axis=0).T
    target = lax.broadcasted_iota(jnp.int32, (SHARDS, 128), 0)
    lane = lax.broadcasted_iota(jnp.int32, (SHARDS, 128), 1)
    weights = jnp.zeros((SHARDS, 128), F32)
    for i in range(OWN):
        channel = OWN * shard + i
        here = target == lax.rem(channel, SHARDS)
        first = BASIS * lax.div(channel, SHARDS)
        for b in range(BASIS):
            weights = jnp.where(here & (lane == first + b), mixing_ref[b, i], weights)
    out_ref[:, 15, :] = weights


def pack_kernel(place_ref, mixing_ref, _, unit_ref, arrived_ref, block_ref):
    pack(unit_ref[...] + arrived_ref[...], mixing_ref, place_ref[0], block_ref)


def along_x(place_ref, m):
    return lax.rem(place_ref[4] + m, 4)


def along_y(place_ref, m):
    upper, right = place_ref[2], place_ref[3]
    return 2 * (1 - upper if m & 2 else upper) + (1 - right if m & 1 else right)


def low_high(rows):
    low = jnp.concatenate([rows[40 * z : 40 * z + 20] for z in range(4)], axis=0)
    high = jnp.concatenate([rows[40 * z + 20 : 40 * z + 40] for z in range(4)], axis=0)
    return low, high


def mlp_kernel(
    place_ref,
    act_ref,
    act_other_ref,
    cot_ref,
    cot_other_ref,
    in_ref,
    out_ref,
    own_ref,
    other_ref,
    *refs,
):
    outs, (unit_ref, act_top, act_low, cot_top, cot_low, kept_ref) = refs[:4], refs[4:]
    step = pl.program_id(0)
    core = place_ref[1]
    points = act_ref.shape[0]

    @pl.when(step == 0)
    def _():
        act_top[0:points, :], act_low[0:points, :] = split(act_ref[...])
        act_top[points:, :], act_low[points:, :] = split(act_other_ref[...])
        cot_top[0:points, :], cot_low[0:points, :] = split(cot_ref[...])
        cot_top[points:, :], cot_low[points:, :] = split(cot_other_ref[...])

    act, cot = (act_top[...], act_low[...]), (cot_top[...], cot_low[...])
    w_in = split(in_ref[...].reshape(320, 640))
    w_out = split(out_ref[...].reshape(320, 640))
    preact = dot3(act, w_in, ((1,), (1,)))
    cdf = 0.5 * (1.0 + lax.erf(preact * (1.0 / math.sqrt(2.0))))
    density = jnp.exp(-0.5 * preact * preact) * (1.0 / math.sqrt(2.0 * math.pi))
    hidden = split(preact * cdf)
    slope = cdf + preact * density
    grad = split(dot3(cot, w_out, ((1,), (1,))) * slope)
    term = dot3(grad, w_in, ((1,), (0,)))
    contract = ((0,), (0,))
    first = dot3(grad, act, contract)
    second = dot3(hidden, cot, contract)

    @pl.when(step == 0)
    def _():
        unit_ref[...] = term

    @pl.when(core == 0)
    def _():
        for x in range(2):
            rows = slice(160 * x, 160 * x + 160)
            kept_ref[2 * step + x, :, 0:640] = first[rows]
            kept_ref[2 * step + x, :, 640:1280] = second[rows]

    @pl.when(core == 1)
    def _():
        lanes = pl.ds(pl.multiple_of(640 * step, 128), 640)
        for x in range(2):
            rows = slice(160 * x, 160 * x + 160)
            parts = zip(low_high(first[rows]), low_high(second[rows]))
            for right, (a, b) in enumerate(parts):
                for upper in range(2):
                    cols = slice(320 * upper, 320 * upper + 320)
                    piece = jnp.concatenate([a[:, cols], b[:, cols]], axis=1)
                    kept_ref[2 * upper + right, 80 * x : 80 * x + 80, lanes] = piece

    @pl.when(step == 1)
    def _():
        total = unit_ref[...] + term
        own_ref[...] = cot_ref[...] + total[0:points]
        other_ref[...] = total[points:]
        for m in range(4):
            index = jnp.where(core == 0, along_x(place_ref, m), along_y(place_ref, m))
            outs[m][...] = kept_ref[index]


def mlp(place, act, act_other, cot, cot_other, weight_in, weight_out):
    points, width = act.shape
    units = weight_in.shape[0]
    full = lambda shape: pl.BlockSpec(shape, lambda i, place: (0,) * len(shape))
    rows = pl.BlockSpec((2, None, 160, width), lambda i, place: (i, place[1], 0, 0))
    return pl.pallas_call(
        mlp_kernel,
        grid_spec=pltpu.PrefetchScalarGridSpec(
            num_scalar_prefetch=1,
            grid=(2,),
            in_specs=[full((points, width))] * 4 + [rows, rows],
            out_specs=[full((points, width))] * 2 + [full((160, 1280))] * 4,
            scratch_shapes=[pltpu.VMEM((2 * points, width), F32)]
            + [pltpu.VMEM((2 * points, width), BF16)] * 4
            + [pltpu.VMEM((4, 160, 1280), F32)],
        ),
        out_shape=[jax.ShapeDtypeStruct((points, width), F32)] * 2
        + [jax.ShapeDtypeStruct((160, 1280), F32)] * 4,
        compiler_params=params(60),
        cost_estimate=cost(30 * points * width * units, 12_000_000),
        name="mlp",
    )(
        place,
        act,
        act_other,
        cot,
        cot_other,
        weight_in.reshape(4, 2, 160, width),
        weight_out.reshape(4, 2, 160, width),
    )


def swap_kernel(place_ref, *refs):
    ins, outs, kept_ref = refs[:4], refs[4:8], refs[8]
    core = place_ref[1]
    total = (ins[0][...] + ins[1][...]) + (ins[2][...] + ins[3][...])

    @pl.when(core == 0)
    def _():
        for right, part in enumerate(low_high(total)):
            for upper in range(2):
                at = 320 * upper
                pair = [part[:, at : at + 320], part[:, 640 + at : 960 + at]]
                kept_ref[2 * upper + right] = jnp.concatenate(pair, axis=1)

    @pl.when(core == 1)
    def _():
        for x in range(4):
            row, col = 80 * (x % 2), 640 * (x // 2)
            kept_ref[x] = total[row : row + 80, col : col + 640]

    for m in range(4):
        index = jnp.where(core == 0, along_y(place_ref, m), along_x(place_ref, m))
        outs[m][...] = kept_ref[index]


def pair_kernel(place_ref, _, *refs):
    ins, (mine_ref, send_ref) = refs[:4], refs[4:]
    total = (ins[0][...] + ins[1][...]) + (ins[2][...] + ins[3][...])
    even = jnp.concatenate([total[:, 0:160], total[:, 320:480]], axis=1)
    odd = jnp.concatenate([total[:, 160:320], total[:, 480:640]], axis=1)
    first = place_ref[1] == 0
    mine_ref[...] = jnp.where(first, even, odd)
    send_ref[...] = jnp.where(first, odd, even)


def stack_kernel(place_ref, mine_ref, arrived_ref, *refs):
    outs, kept_ref = refs[:8], refs[8]
    first = place_ref[1] == 0
    mine, arrived = mine_ref[...], arrived_ref[...]
    below, above = jnp.where(first, mine, arrived), jnp.where(first, arrived, mine)
    for z in range(4):
        kept_ref[z, 0:20, :] = below[20 * z : 20 * z + 20]
        kept_ref[4 + z, 0:20, :] = above[20 * z : 20 * z + 20]
    for m in range(8):
        outs[m][...] = kept_ref[lax.rem(place_ref[5] + m, 8), 0:20, :]


def last_kernel(*refs):
    first_ref, second_ref = refs[8:]
    a, b, c, d = (refs[m][...] + refs[m + 4][...] for m in range(4))
    total = (a + b) + (c + d)
    first_ref[...] = total[:, 0:160]
    second_ref[...] = total[:, 160:320]


def small(kernel, operands, shapes, scalars=0, scratch=(), earlier=(), name=None, flops=0):
    return pl.pallas_call(
        kernel,
        in_specs=[pl.BlockSpec(memory_space=pltpu.SMEM)] * scalars
        + EARLIER * len(earlier)
        + whole(len(operands) - scalars),
        out_specs=whole(len(shapes)),
        out_shape=[jax.ShapeDtypeStruct(shape, F32) for shape in shapes],
        scratch_shapes=scratch,
        compiler_params=params(32),
        cost_estimate=cost(flops, 4_000_000) if flops else None,
        name=name,
    )(*operands[:scalars], *earlier, *operands[scalars:])


def exchange(pieces, cores):
    def target(m, yl, co, x, z, yh):
        if cores[co] == "x":
            x = (x + m) % 4
        else:
            yl, yh = yl ^ (m >> 1), yh ^ (m & 1)
        return yl, co, x, z, yh

    sizes = (2, 2, 4, 8, 2)
    order = lambda at: int(np.ravel_multi_index(at, sizes))
    moved = [pieces[0]]
    for m in (1, 2, 3):
        pairs = [(order(at), order(target(m, *at))) for at in np.ndindex(*sizes)]
        moved.append(lax.ppermute(pieces[m], AXES, pairs))
    return moved


def to_core(value):
    return lax.ppermute(value, "co", [(0, 1), (1, 0)])


def spectrum_kernel(
    block_ref, top_ref, low_ref, _, out_ref, first_ref, final_ref, mixing_ref, flat_ref
):
    for p in range(COLS // 2):
        pair = jnp.concatenate([block_ref[:, 2 * p, :], block_ref[:, 2 * p + 1, :]], axis=0)
        flat_ref[0:128, 128 * p : 128 * (p + 1)] = pair.T
    rest = [block_ref[:, 12 + q, :].T for q in range(3)]
    pieces = [rest[q][32 * g : 32 * (g + 1), :] for g in range(4) for q in range(3)]
    flat_ref[128:160, :] = jnp.concatenate(pieces, axis=1)
    result = dot3(split(flat_ref[...]), (top_ref[...], low_ref[...]), ((1,), (0,)))
    out_ref[...] = result
    mixing_ref[...] = jnp.sum(block_ref[:, 15, :], axis=0, keepdims=True)
    for r in range(OWN):
        first_ref[3 * r : 3 * r + 3, :] = result[ROWS * r : ROWS * r + 3, :]
        final_ref[3 * r : 3 * r + 3, :] = result[ROWS * r + 13 : ROWS * r + 16, :]


def spectrum(block, earlier):
    top, low = forward_table(shard_order())
    rows = OWN * ROWS
    return pl.pallas_call(
        spectrum_kernel,
        in_specs=whole(3) + EARLIER,
        out_specs=whole(4),
        out_shape=[
            jax.ShapeDtypeStruct((rows, CIRCLE), F32),
            jax.ShapeDtypeStruct((3 * OWN, CIRCLE), F32),
            jax.ShapeDtypeStruct((3 * OWN, CIRCLE), F32),
            jax.ShapeDtypeStruct((1, 128), F32),
        ],
        scratch_shapes=[pltpu.VMEM((rows, CIRCLE), F32)],
        compiler_params=params(24),
        cost_estimate=cost(6 * rows * CIRCLE * CIRCLE, 4_000_000),
        name="spectrum",
    )(block, jnp.asarray(top), jnp.asarray(low), earlier)


def kernel_spectrum_kernel(kernel_ref, top_ref, low_ref, out_ref):
    out_ref[...] = dot3(split(kernel_ref[...]), (top_ref[...], low_ref[...]), ((1,), (0,)))


def kernel_spectrum(kernels):
    top, low = forward_table(np.arange(CIRCLE))
    rows = BASIS * TAPS * ROWS
    flat = kernels.transpose(0, 2, 1, 3).reshape(rows, CIRCLE)
    return pl.pallas_call(
        kernel_spectrum_kernel,
        in_specs=whole(3),
        out_specs=whole(1)[0],
        out_shape=jax.ShapeDtypeStruct((rows, CIRCLE), F32),
        compiler_params=params(24),
        cost_estimate=cost(6 * rows * CIRCLE * CIRCLE, 5_000_000),
        name="kernel_spectrum",
    )(flat, jnp.asarray(top), jnp.asarray(low))


def filter_kernel(
    mixing_ref, data_ref, before_ref, after_ref, kernel_ref, top_ref, low_ref, *refs
):
    out_ref, rows_ref, sum_ref = refs[-3:]
    for r in range(OWN):
        rows_ref[r, 0:3, :] = before_ref[3 * r : 3 * r + 3, :]
        rows_ref[r, 3 : 3 + ROWS, :] = data_ref[ROWS * r : ROWS * (r + 1), :]
        rows_ref[r, 3 + ROWS : 6 + ROWS, :] = after_ref[3 * r : 3 * r + 3, :]
    lane = lax.broadcasted_iota(jnp.int32, (ROWS, HALF), 1)
    ends = lane == 0

    def channel(r, carry):
        real = jnp.zeros((ROWS, HALF), F32)
        imag = jnp.zeros((ROWS, HALF), F32)
        for k in range(TAPS):
            mixed_real = jnp.zeros((ROWS, HALF), F32)
            mixed_imag = jnp.zeros((ROWS, HALF), F32)
            for b in range(BASIS):
                weight = mixing_ref[0, BASIS * r + b]
                at = ROWS * (TAPS * b + k)
                mixed_real += weight * kernel_ref[at : at + ROWS, 0:HALF]
                mixed_imag += weight * kernel_ref[at : at + ROWS, HALF:CIRCLE]
            own = jnp.where(ends, mixed_imag, mixed_real)
            cross = jnp.where(ends, 0.0, mixed_imag)
            data_real = rows_ref[r, 6 - k : 6 - k + ROWS, 0:HALF]
            data_imag = rows_ref[r, 6 - k : 6 - k + ROWS, HALF:CIRCLE]
            real += mixed_real * data_real + cross * data_imag
            imag += own * data_imag - cross * data_real
        sum_ref[r, :, 0:HALF] = real
        sum_ref[r, :, HALF:CIRCLE] = imag
        return carry

    lax.fori_loop(0, OWN, channel, 0)
    total = split(sum_ref[...].reshape(OWN * ROWS, CIRCLE))
    field = dot3((top_ref[...], low_ref[...]), total, ((1,), (1,)))
    for l in range(COLS):
        out_ref[:, l, :] = field[SHARDS * l : SHARDS * (l + 1), 0:128]
    for q in range(3):
        pieces = [
            field[SHARDS * (3 * g + q) : SHARDS * (3 * g + q + 1), 128:160] for g in range(4)
        ]
        out_ref[:, 12 + q, :] = jnp.concatenate(pieces, axis=1)
    out_ref[:, 15, :] = jnp.zeros((SHARDS, 128), F32)


def filtered(mixing, data, before, beyond, kernel, earlier):
    top, low = backward_table(shard_order())
    return pl.pallas_call(
        filter_kernel,
        in_specs=[pl.BlockSpec(memory_space=pltpu.SMEM)] + whole(6) + EARLIER * len(earlier),
        out_specs=whole(1)[0],
        out_shape=jax.ShapeDtypeStruct((SHARDS, 16, 128), F32),
        scratch_shapes=[
            pltpu.VMEM((OWN, 24, CIRCLE), F32),
            pltpu.VMEM((OWN, ROWS, CIRCLE), F32),
        ],
        compiler_params=params(32),
        cost_estimate=cost(6 * OWN * ROWS * CIRCLE * CIRCLE, 5_000_000),
        name="filter",
    )(mixing, data, before, beyond, kernel, jnp.asarray(top), jnp.asarray(low), *earlier)


def unpack_kernel(block_ref, out_ref):
    def put(l, r, pair):
        out_ref[ROWS * l : ROWS * (l + 1), SHARDS * r : SHARDS * (r + 2)] = jnp.concatenate(
            pair, axis=1
        )

    for l in range(COLS):
        turned = block_ref[:, l, :].T
        for r in range(0, 8, 2):
            put(l, r, [turned[ROWS * r : ROWS * (r + 1)], turned[ROWS * (r + 1) : ROWS * (r + 2)]])
    for q in range(3):
        turned = block_ref[:, 12 + q, :].T
        for g in range(4):
            at = 32 * g
            put(3 * g + q, 8, [turned[at : at + ROWS], turned[at + ROWS : at + 2 * ROWS]])


def unpack(block):
    return pl.pallas_call(
        unpack_kernel,
        in_specs=whole(1),
        out_specs=whole(1)[0],
        out_shape=jax.ShapeDtypeStruct((ROWS * COLS, SHARDS * OWN), F32),
        name="unpack",
    )(block)


def across(block):
    return lax.all_to_all(block, LON, split_axis=0, concat_axis=0, tiled=True)


def per_device(activation, cotangent, weight_in, weight_out, kernels, mixing):
    points = ROWS * COLS
    width = activation.shape[2]
    act = activation.transpose(1, 0, 2).reshape(points, width)
    cot = cotangent.transpose(1, 0, 2).reshape(points, width)
    place = jnp.stack([lax.axis_index(axis) for axis in (LON, "co", "yl", "yh", "x", "z")])
    unit, other, *pieces = mlp(place, act, to_core(act), cot, to_core(cot), weight_in, weight_out)
    kernel = kernel_spectrum(kernels)
    operands = (place, mixing.T, unit, to_core(other))
    (block,) = small(pack_kernel, operands, [(SHARDS, 16, 128)], 2, (), (kernel,), "pack")
    moved = exchange(pieces, "xy")
    spread = across(block)
    kept = (pltpu.VMEM((4, 80, 640), F32),)
    swapped = small(swap_kernel, (place, *moved), [(80, 640)] * 4, 1, kept, (), "swap", 10**10)
    data, first, final, own_mixing = spectrum(spread, swapped[0])
    forward = [(i, i + 1) for i in range(3)]
    backward = [(target, source) for source, target in forward]
    before = lax.ppermute(final, LAT, forward)
    beyond = lax.ppermute(first, LAT, backward)
    moved = exchange(swapped, "yx")
    sent = filtered(own_mixing, data, before, beyond, kernel, moved)
    result = across(sent)
    mine, send = small(pair_kernel, (place, *moved), [(80, 320)] * 2, 1, (), (sent,), "pair")
    kept = (pltpu.VMEM((8, 24, 320), F32),)
    stacked = small(
        stack_kernel, (place, mine, to_core(send)), [(20, 320)] * 8, 1, kept, name="stack"
    )
    moved = [stacked[0]] + [
        lax.ppermute(stacked[m], "z", [(i, (i + m) % 8) for i in range(8)]) for m in range(1, 8)
    ]
    grad_in, grad_out = small(last_kernel, moved, [(20, 160)] * 2, name="last")
    field = unpack(result).reshape(COLS, ROWS, width).transpose(1, 0, 2)
    return (field, grad_in, grad_out)


def solution(mesh):
    fine = Mesh(mesh.devices.reshape(2, 2, 4, 8, 2), AXES)
    placed = (
        P(LAT, LON, None),
        P(LAT, LON, None),
        P(),
        P(),
        P(None, LAT, None, None),
        P(LON, None),
    )
    return jax.shard_map(
        per_device,
        mesh=fine,
        in_specs=placed,
        out_specs=(P(LAT, LON, None), P(LON, LAT), P(LON, LAT)),
        check_vma=False,
    )
```

```python
import functools
import math

import jax
import jax.numpy as jnp
import ml_dtypes
import numpy as np
from jax import lax
from jax.experimental import pallas as pl
from jax.experimental.pallas import tpu as pltpu
from jax.sharding import Mesh
from jax.sharding import PartitionSpec as P

AXES = ("yl", "co", "x", "z", "yh")
LAT = ("yl", "co")
LON = ("x", "z", "yh")
F32 = jnp.float32
BF16 = jnp.bfloat16
SHARDS = 64
COLS = 12
ROWS = 16
OWN = 10
CIRCLE = 768
HALF = 384
TAPS = 7
BASIS = 3
MIB = 1 << 20


def split(value):
    top = value.astype(BF16)
    return top, (value - top.astype(F32)).astype(BF16)


def dot3(left, right, dims):
    (a, b), (c, d) = left, right
    (at,), (to,) = dims
    return lax.dot_general(
        jnp.concatenate([a, b, a], axis=at),
        jnp.concatenate([c, c, d], axis=to),
        dimension_numbers=(dims, ((), ())),
        preferred_element_type=F32,
    )


def whole(n):
    return [pl.BlockSpec(memory_space=pltpu.VMEM)] * n


EARLIER = [pl.BlockSpec(memory_space=pl.ANY)]


def params(mib):
    return pltpu.CompilerParams(vmem_limit_bytes=mib * MIB)


def cost(flops, moved):
    return pl.CostEstimate(flops=flops, bytes_accessed=moved, transcendentals=0)


def table(order):
    angle = 2.0 * np.pi / CIRCLE * (order[:, None] * np.arange(HALF)[None, :] % CIRCLE)
    nyquist = np.where(order % 2 == 0, 1.0, -1.0)
    real, imag = np.cos(angle), -np.sin(angle)
    imag[:, 0] = nyquist
    return np.concatenate([real, imag], axis=1)


def parts(matrix):
    exact = matrix.astype(np.float32)
    top = exact.astype(ml_dtypes.bfloat16)
    return top, (exact - top.astype(np.float32)).astype(ml_dtypes.bfloat16)


def forward_table(order):
    return parts(table(order))


def backward_table(order):
    weight = np.full((2, HALF), 2.0 / CIRCLE)
    weight[:, 0] = 1.0 / CIRCLE
    return parts(table(order) * weight.reshape(1, -1))


def shard_order():
    return (np.arange(COLS)[:, None] + COLS * np.arange(SHARDS)[None, :]).reshape(-1)


def pack(unit, mixing_ref, shard, out_ref):
    def piece(l, r):
        return unit[ROWS * l : ROWS * (l + 1), SHARDS * r : SHARDS * (r + 1)]

    for l in range(COLS):
        out_ref[:, l, :] = jnp.concatenate([piece(l, r) for r in range(8)], axis=0).T
    for q in range(3):
        chunk = [piece(3 * g + q, r) for g in range(4) for r in (8, 9)]
        out_ref[:, 12 + q, :] = jnp.concatenate(chunk, axis=0).T
    target = lax.broadcasted_iota(jnp.int32, (SHARDS, 128), 0)
    lane = lax.broadcasted_iota(jnp.int32, (SHARDS, 128), 1)
    weights = jnp.zeros((SHARDS, 128), F32)
    for i in range(OWN):
        channel = OWN * shard + i
        here = target == lax.rem(channel, SHARDS)
        first = BASIS * lax.div(channel, SHARDS)
        for b in range(BASIS):
            weights = jnp.where(here & (lane == first + b), mixing_ref[b, i], weights)
    out_ref[:, 15, :] = weights


def pack_kernel(place_ref, mixing_ref, unit_ref, arrived_ref, block_ref):
    pack(unit_ref[...] + arrived_ref[...], mixing_ref, place_ref[0], block_ref)


def along_x(place_ref, m):
    return lax.rem(place_ref[4] + m, 4)


def along_y(place_ref, m):
    upper, right = place_ref[2], place_ref[3]
    return 2 * (1 - upper if m & 2 else upper) + (1 - right if m & 1 else right)


def low_high(rows):
    low = jnp.concatenate([rows[40 * z : 40 * z + 20] for z in range(4)], axis=0)
    high = jnp.concatenate([rows[40 * z + 20 : 40 * z + 40] for z in range(4)], axis=0)
    return low, high


def mlp_kernel(
    place_ref,
    act_ref,
    act_other_ref,
    cot_ref,
    cot_other_ref,
    in_ref,
    out_ref,
    own_ref,
    other_ref,
    *refs,
):
    outs, kept_ref = refs[:4], refs[4]
    core = place_ref[1]
    points = act_ref.shape[0]
    act = split(jnp.concatenate([act_ref[...], act_other_ref[...]], axis=0))
    cot = split(jnp.concatenate([cot_ref[...], cot_other_ref[...]], axis=0))
    w_in = split(in_ref[...].reshape(640, 640))
    w_out = split(out_ref[...].reshape(640, 640))
    preact = dot3(act, w_in, ((1,), (1,)))
    cdf = 0.5 * (1.0 + lax.erf(preact * (1.0 / math.sqrt(2.0))))
    density = jnp.exp(-0.5 * preact * preact) * (1.0 / math.sqrt(2.0 * math.pi))
    hidden = split(preact * cdf)
    slope = cdf + preact * density
    grad = split(dot3(cot, w_out, ((1,), (1,))) * slope)
    term = dot3(grad, w_in, ((1,), (0,)))
    own_ref[...] = cot_ref[...] + term[0:points]
    other_ref[...] = term[points:]
    contract = ((0,), (0,))
    first = dot3(grad, act, contract)
    second = dot3(hidden, cot, contract)

    @pl.when(core == 0)
    def _():
        for x in range(4):
            rows = slice(160 * x, 160 * x + 160)
            kept_ref[x, :, 0:640] = first[rows]
            kept_ref[x, :, 640:1280] = second[rows]

    @pl.when(core == 1)
    def _():
        for x in range(4):
            rows = slice(160 * x, 160 * x + 160)
            row, lane = 80 * (x % 2), 640 * (x // 2)
            parts = zip(low_high(first[rows]), low_high(second[rows]))
            for right, (a, b) in enumerate(parts):
                for upper in range(2):
                    cols = slice(320 * upper, 320 * upper + 320)
                    piece = jnp.concatenate([a[:, cols], b[:, cols]], axis=1)
                    kept_ref[2 * upper + right, row : row + 80, lane : lane + 640] = piece

    for m in range(4):
        index = jnp.where(core == 0, along_x(place_ref, m), along_y(place_ref, m))
        outs[m][...] = kept_ref[index]


def mlp(place, act, act_other, cot, cot_other, weight_in, weight_out):
    points, width = act.shape
    units = weight_in.shape[0]
    full = lambda shape: pl.BlockSpec(shape, lambda i, place: (0,) * len(shape))
    rows = pl.BlockSpec((4, None, 160, width), lambda i, place: (0, place[1], 0, 0))
    return pl.pallas_call(
        mlp_kernel,
        grid_spec=pltpu.PrefetchScalarGridSpec(
            num_scalar_prefetch=1,
            grid=(1,),
            in_specs=[full((points, width))] * 4 + [rows, rows],
            out_specs=[full((points, width))] * 2 + [full((160, 1280))] * 4,
            scratch_shapes=[pltpu.VMEM((4, 160, 1280), F32)],
        ),
        out_shape=[jax.ShapeDtypeStruct((points, width), F32)] * 2
        + [jax.ShapeDtypeStruct((160, 1280), F32)] * 4,
        compiler_params=params(60),
        cost_estimate=cost(30 * points * width * units, 12_000_000),
        name="mlp",
    )(
        place,
        act,
        act_other,
        cot,
        cot_other,
        weight_in.reshape(4, 2, 160, width),
        weight_out.reshape(4, 2, 160, width),
    )


def swap_kernel(place_ref, *refs):
    ins, outs, kept_ref = refs[:4], refs[4:8], refs[8]
    core = place_ref[1]
    total = (ins[0][...] + ins[1][...]) + (ins[2][...] + ins[3][...])

    @pl.when(core == 0)
    def _():
        for right, part in enumerate(low_high(total)):
            for upper in range(2):
                at = 320 * upper
                pair = [part[:, at : at + 320], part[:, 640 + at : 960 + at]]
                kept_ref[2 * upper + right] = jnp.concatenate(pair, axis=1)

    @pl.when(core == 1)
    def _():
        for x in range(4):
            row, col = 80 * (x % 2), 640 * (x // 2)
            kept_ref[x] = total[row : row + 80, col : col + 640]

    for m in range(4):
        index = jnp.where(core == 0, along_y(place_ref, m), along_x(place_ref, m))
        outs[m][...] = kept_ref[index]


def stack_kernel(place_ref, _, *refs):
    ins, outs, kept_ref = refs[:4], refs[4:12], refs[12]
    total = (ins[0][...] + ins[1][...]) + (ins[2][...] + ins[3][...])
    for core in range(2):
        at = 160 * core
        part = jnp.concatenate([total[:, at : at + 160], total[:, 320 + at : 480 + at]], axis=1)
        for z in range(4):
            kept_ref[2 * z + core, 0:20, :] = part[20 * z : 20 * z + 20]
    high, low = lax.div(place_ref[5], 4), lax.rem(place_ref[5], 4)
    for a in range(4):
        for b in range(2):
            index = 2 * lax.rem(low + a, 4) + (1 - high if b else high)
            outs[2 * a + b][...] = kept_ref[index, 0:20, :]


def last_kernel(*refs):
    first_ref, second_ref = refs[8:]
    a, b, c, d = (refs[m][...] + refs[m + 4][...] for m in range(4))
    total = (a + b) + (c + d)
    first_ref[...] = total[:, 0:160]
    second_ref[...] = total[:, 160:320]


def small(kernel, operands, shapes, scalars=0, scratch=(), earlier=(), name=None, flops=0):
    return pl.pallas_call(
        kernel,
        in_specs=[pl.BlockSpec(memory_space=pltpu.SMEM)] * scalars
        + EARLIER * len(earlier)
        + whole(len(operands) - scalars),
        out_specs=whole(len(shapes)),
        out_shape=[jax.ShapeDtypeStruct(shape, F32) for shape in shapes],
        scratch_shapes=scratch,
        compiler_params=params(32),
        cost_estimate=cost(flops, 4_000_000) if flops else None,
        name=name,
    )(*operands[:scalars], *earlier, *operands[scalars:])


def permute(value, target):
    sizes = (2, 2, 4, 8, 2)
    order = lambda at: int(np.ravel_multi_index(at, sizes))
    pairs = [(order(at), order(target(*at))) for at in np.ndindex(*sizes)]
    return lax.ppermute(value, AXES, pairs)


def exchange(pieces, cores):
    def target(m, yl, co, x, z, yh):
        if cores[co] == "x":
            x = (x + m) % 4
        else:
            yl, yh = yl ^ (m >> 1), yh ^ (m & 1)
        return yl, co, x, z, yh

    return [pieces[0]] + [permute(pieces[m], functools.partial(target, m)) for m in (1, 2, 3)]


def exchange_z(pieces):
    def target(m, yl, co, x, z, yh):
        return yl, (z // 4) ^ (m & 1), x, 4 * co + (z + (m >> 1)) % 4, yh

    return [permute(pieces[m], functools.partial(target, m)) for m in range(8)]


def to_core(value):
    return lax.ppermute(value, "co", [(0, 1), (1, 0)])


def spectrum_kernel(
    block_ref, top_ref, low_ref, _, out_ref, first_ref, final_ref, mixing_ref, flat_ref
):
    for p in range(COLS // 2):
        pair = jnp.concatenate([block_ref[:, 2 * p, :], block_ref[:, 2 * p + 1, :]], axis=0)
        flat_ref[0:128, 128 * p : 128 * (p + 1)] = pair.T
    rest = [block_ref[:, 12 + q, :].T for q in range(3)]
    pieces = [rest[q][32 * g : 32 * (g + 1), :] for g in range(4) for q in range(3)]
    flat_ref[128:160, :] = jnp.concatenate(pieces, axis=1)
    result = dot3(split(flat_ref[...]), (top_ref[...], low_ref[...]), ((1,), (0,)))
    out_ref[...] = result
    mixing_ref[...] = jnp.sum(block_ref[:, 15, :], axis=0, keepdims=True)
    for r in range(OWN):
        first_ref[3 * r : 3 * r + 3, :] = result[ROWS * r : ROWS * r + 3, :]
        final_ref[3 * r : 3 * r + 3, :] = result[ROWS * r + 13 : ROWS * r + 16, :]


def spectrum(block, earlier):
    top, low = forward_table(shard_order())
    rows = OWN * ROWS
    return pl.pallas_call(
        spectrum_kernel,
        in_specs=whole(3) + EARLIER,
        out_specs=whole(4),
        out_shape=[
            jax.ShapeDtypeStruct((rows, CIRCLE), F32),
            jax.ShapeDtypeStruct((3 * OWN, CIRCLE), F32),
            jax.ShapeDtypeStruct((3 * OWN, CIRCLE), F32),
            jax.ShapeDtypeStruct((1, 128), F32),
        ],
        scratch_shapes=[pltpu.VMEM((rows, CIRCLE), F32)],
        compiler_params=params(24),
        cost_estimate=cost(6 * rows * CIRCLE * CIRCLE, 4_000_000),
        name="spectrum",
    )(block, jnp.asarray(top), jnp.asarray(low), earlier)


def kernel_spectrum_kernel(kernel_ref, top_ref, low_ref, _, out_ref):
    out_ref[...] = dot3(split(kernel_ref[...]), (top_ref[...], low_ref[...]), ((1,), (0,)))


def kernel_spectrum(kernels, earlier):
    top, low = forward_table(np.arange(CIRCLE))
    rows = BASIS * TAPS * ROWS
    flat = kernels.transpose(0, 2, 1, 3).reshape(rows, CIRCLE)
    return pl.pallas_call(
        kernel_spectrum_kernel,
        in_specs=whole(3) + EARLIER,
        out_specs=whole(1)[0],
        out_shape=jax.ShapeDtypeStruct((rows, CIRCLE), F32),
        compiler_params=params(24),
        cost_estimate=cost(6 * rows * CIRCLE * CIRCLE, 5_000_000),
        name="kernel_spectrum",
    )(flat, jnp.asarray(top), jnp.asarray(low), earlier)


def filter_kernel(
    mixing_ref, data_ref, before_ref, after_ref, kernel_ref, top_ref, low_ref, *refs
):
    out_ref, rows_ref, sum_ref = refs[-3:]
    for r in range(OWN):
        rows_ref[r, 0:3, :] = before_ref[3 * r : 3 * r + 3, :]
        rows_ref[r, 3 : 3 + ROWS, :] = data_ref[ROWS * r : ROWS * (r + 1), :]
        rows_ref[r, 3 + ROWS : 6 + ROWS, :] = after_ref[3 * r : 3 * r + 3, :]
    lane = lax.broadcasted_iota(jnp.int32, (ROWS, HALF), 1)
    ends = lane == 0

    def channel(r, carry):
        real = jnp.zeros((ROWS, HALF), F32)
        imag = jnp.zeros((ROWS, HALF), F32)
        for k in range(TAPS):
            mixed_real = jnp.zeros((ROWS, HALF), F32)
            mixed_imag = jnp.zeros((ROWS, HALF), F32)
            for b in range(BASIS):
                weight = mixing_ref[0, BASIS * r + b]
                at = ROWS * (TAPS * b + k)
                mixed_real += weight * kernel_ref[at : at + ROWS, 0:HALF]
                mixed_imag += weight * kernel_ref[at : at + ROWS, HALF:CIRCLE]
            own = jnp.where(ends, mixed_imag, mixed_real)
            cross = jnp.where(ends, 0.0, mixed_imag)
            data_real = rows_ref[r, 6 - k : 6 - k + ROWS, 0:HALF]
            data_imag = rows_ref[r, 6 - k : 6 - k + ROWS, HALF:CIRCLE]
            real += mixed_real * data_real + cross * data_imag
            imag += own * data_imag - cross * data_real
        sum_ref[r, :, 0:HALF] = real
        sum_ref[r, :, HALF:CIRCLE] = imag
        return carry

    lax.fori_loop(0, OWN, channel, 0)
    total = split(sum_ref[...].reshape(OWN * ROWS, CIRCLE))
    field = dot3((top_ref[...], low_ref[...]), total, ((1,), (1,)))
    for l in range(COLS):
        out_ref[:, l, :] = field[SHARDS * l : SHARDS * (l + 1), 0:128]
    for q in range(3):
        pieces = [
            field[SHARDS * (3 * g + q) : SHARDS * (3 * g + q + 1), 128:160] for g in range(4)
        ]
        out_ref[:, 12 + q, :] = jnp.concatenate(pieces, axis=1)
    out_ref[:, 15, :] = jnp.zeros((SHARDS, 128), F32)


def filtered(mixing, data, before, beyond, kernel, earlier):
    top, low = backward_table(shard_order())
    return pl.pallas_call(
        filter_kernel,
        in_specs=[pl.BlockSpec(memory_space=pltpu.SMEM)] + whole(6) + EARLIER * len(earlier),
        out_specs=whole(1)[0],
        out_shape=jax.ShapeDtypeStruct((SHARDS, 16, 128), F32),
        scratch_shapes=[
            pltpu.VMEM((OWN, 24, CIRCLE), F32),
            pltpu.VMEM((OWN, ROWS, CIRCLE), F32),
        ],
        compiler_params=params(32),
        cost_estimate=cost(6 * OWN * ROWS * CIRCLE * CIRCLE, 5_000_000),
        name="filter",
    )(mixing, data, before, beyond, kernel, jnp.asarray(top), jnp.asarray(low), *earlier)


def unpack_kernel(block_ref, out_ref):
    def put(l, r, pair):
        out_ref[ROWS * l : ROWS * (l + 1), SHARDS * r : SHARDS * (r + 2)] = jnp.concatenate(
            pair, axis=1
        )

    for l in range(COLS):
        turned = block_ref[:, l, :].T
        for r in range(0, 8, 2):
            put(l, r, [turned[ROWS * r : ROWS * (r + 1)], turned[ROWS * (r + 1) : ROWS * (r + 2)]])
    for q in range(3):
        turned = block_ref[:, 12 + q, :].T
        for g in range(4):
            at = 32 * g
            put(3 * g + q, 8, [turned[at : at + ROWS], turned[at + ROWS : at + 2 * ROWS]])


def unpack(block):
    return pl.pallas_call(
        unpack_kernel,
        in_specs=whole(1),
        out_specs=whole(1)[0],
        out_shape=jax.ShapeDtypeStruct((ROWS * COLS, SHARDS * OWN), F32),
        name="unpack",
    )(block)


def across(block):
    return lax.all_to_all(block, LON, split_axis=0, concat_axis=0, tiled=True)


def per_device(activation, cotangent, weight_in, weight_out, kernels, mixing):
    points = ROWS * COLS
    width = activation.shape[2]
    act = activation.transpose(1, 0, 2).reshape(points, width)
    cot = cotangent.transpose(1, 0, 2).reshape(points, width)
    place = jnp.stack([lax.axis_index(axis) for axis in (LON, "co", "yl", "yh", "x", "z")])
    unit, other, *pieces = mlp(place, act, to_core(act), cot, to_core(cot), weight_in, weight_out)
    operands = (place, mixing.T, unit, to_core(other))
    (block,) = small(pack_kernel, operands, [(SHARDS, 16, 128)], 2, name="pack")
    moved = exchange(pieces, "xy")
    spread = across(block)
    kept = (pltpu.VMEM((4, 80, 640), F32),)
    swapped = small(swap_kernel, (place, *moved), [(80, 640)] * 4, 1, kept, (), "swap", 10**10)
    kernel = kernel_spectrum(kernels, swapped[0])
    moved = exchange(swapped, "yx")
    kept = (pltpu.VMEM((8, 24, 320), F32),)
    stacked = small(stack_kernel, (place, *moved), [(20, 320)] * 8, 1, kept, (kernel,), "stack")
    data, first, final, own_mixing = spectrum(spread, stacked[0])
    forward = [(i, i + 1) for i in range(3)]
    backward = [(target, source) for source, target in forward]
    before = lax.ppermute(final, LAT, forward)
    beyond = lax.ppermute(first, LAT, backward)
    sent = filtered(own_mixing, data, before, beyond, kernel, ())
    result = across(sent)
    grad_in, grad_out = small(last_kernel, exchange_z(stacked), [(20, 160)] * 2, name="last")
    field = unpack(result).reshape(COLS, ROWS, width).transpose(1, 0, 2)
    return (field, grad_in, grad_out)


def solution(mesh):
    fine = Mesh(mesh.devices.reshape(2, 2, 4, 8, 2), AXES)
    placed = (
        P(LAT, LON, None),
        P(LAT, LON, None),
        P(),
        P(),
        P(None, LAT, None, None),
        P(LON, None),
    )
    return jax.shard_map(
        per_device,
        mesh=fine,
        in_specs=placed,
        out_specs=(P(LAT, LON, None), P(LON, LAT), P(LON, LAT)),
        check_vma=False,
    )
```

```python
import functools
import math

import jax
import jax.numpy as jnp
import ml_dtypes
import numpy as np
from jax import lax
from jax.experimental import pallas as pl
from jax.experimental.pallas import tpu as pltpu
from jax.sharding import Mesh
from jax.sharding import PartitionSpec as P

AXES = ("yl", "co", "x", "z", "yh")
LAT = ("yl", "co")
LON = ("x", "z", "yh")
F32 = jnp.float32
BF16 = jnp.bfloat16
SHARDS = 64
COLS = 12
ROWS = 16
OWN = 10
CIRCLE = 768
HALF = 384
TAPS = 7
BASIS = 3
MIB = 1 << 20


def split(value):
    top = value.astype(BF16)
    return top, (value - top.astype(F32)).astype(BF16)


def dot3(left, right, dims):
    (a, b), (c, d) = left, right
    (at,), (to,) = dims
    return lax.dot_general(
        jnp.concatenate([a, b, a], axis=at),
        jnp.concatenate([c, c, d], axis=to),
        dimension_numbers=(dims, ((), ())),
        preferred_element_type=F32,
    )


def whole(n):
    return [pl.BlockSpec(memory_space=pltpu.VMEM)] * n


EARLIER = [pl.BlockSpec(memory_space=pl.ANY)]


def params(mib):
    return pltpu.CompilerParams(vmem_limit_bytes=mib * MIB)


def cost(flops, moved):
    return pl.CostEstimate(flops=flops, bytes_accessed=moved, transcendentals=0)


def table(order):
    angle = 2.0 * np.pi / CIRCLE * (order[:, None] * np.arange(HALF)[None, :] % CIRCLE)
    nyquist = np.where(order % 2 == 0, 1.0, -1.0)
    real, imag = np.cos(angle), -np.sin(angle)
    imag[:, 0] = nyquist
    return np.concatenate([real, imag], axis=1)


def parts(matrix):
    exact = matrix.astype(np.float32)
    top = exact.astype(ml_dtypes.bfloat16)
    return top, (exact - top.astype(np.float32)).astype(ml_dtypes.bfloat16)


def forward_table(order):
    return parts(table(order))


def backward_table(order):
    weight = np.full((2, HALF), 2.0 / CIRCLE)
    weight[:, 0] = 1.0 / CIRCLE
    return parts(table(order) * weight.reshape(1, -1))


def shard_order():
    return (np.arange(COLS)[:, None] + COLS * np.arange(SHARDS)[None, :]).reshape(-1)


def pack(unit, mixing_ref, shard, out_ref):
    def piece(l, r):
        return unit[ROWS * l : ROWS * (l + 1), SHARDS * r : SHARDS * (r + 1)]

    for l in range(COLS):
        out_ref[:, l, :] = jnp.concatenate([piece(l, r) for r in range(8)], axis=0).T
    for q in range(3):
        chunk = [piece(3 * g + q, r) for g in range(4) for r in (8, 9)]
        out_ref[:, 12 + q, :] = jnp.concatenate(chunk, axis=0).T
    target = lax.broadcasted_iota(jnp.int32, (SHARDS, 128), 0)
    lane = lax.broadcasted_iota(jnp.int32, (SHARDS, 128), 1)
    weights = jnp.zeros((SHARDS, 128), F32)
    for i in range(OWN):
        channel = OWN * shard + i
        here = target == lax.rem(channel, SHARDS)
        first = BASIS * lax.div(channel, SHARDS)
        for b in range(BASIS):
            weights = jnp.where(here & (lane == first + b), mixing_ref[b, i], weights)
    out_ref[:, 15, :] = weights


def pack_kernel(place_ref, mixing_ref, unit_ref, arrived_ref, block_ref):
    pack(unit_ref[...] + arrived_ref[...], mixing_ref, place_ref[0], block_ref)


def along_x(place_ref, m):
    return lax.rem(place_ref[4] + m, 4)


def along_y(place_ref, m):
    upper, right = place_ref[2], place_ref[3]
    return 2 * (1 - upper if m & 2 else upper) + (1 - right if m & 1 else right)


def low_high(rows):
    low = jnp.concatenate([rows[40 * z : 40 * z + 20] for z in range(4)], axis=0)
    high = jnp.concatenate([rows[40 * z + 20 : 40 * z + 40] for z in range(4)], axis=0)
    return low, high


def mlp_kernel(
    place_ref,
    act_ref,
    act_other_ref,
    cot_ref,
    cot_other_ref,
    in_ref,
    out_ref,
    own_ref,
    other_ref,
    *refs,
):
    outs, kept_ref = refs[:4], refs[4]
    core = place_ref[1]
    points = act_ref.shape[0]
    act = split(jnp.concatenate([act_ref[...], act_other_ref[...]], axis=0))
    cot = split(jnp.concatenate([cot_ref[...], cot_other_ref[...]], axis=0))
    w_in = split(in_ref[...].reshape(640, 640))
    w_out = split(out_ref[...].reshape(640, 640))
    preact = dot3(act, w_in, ((1,), (1,)))
    cdf = 0.5 * (1.0 + lax.erf(preact * (1.0 / math.sqrt(2.0))))
    density = jnp.exp(-0.5 * preact * preact) * (1.0 / math.sqrt(2.0 * math.pi))
    hidden = split(preact * cdf)
    slope = cdf + preact * density
    grad = split(dot3(cot, w_out, ((1,), (1,))) * slope)
    term = dot3(grad, w_in, ((1,), (0,)))
    own_ref[...] = cot_ref[...] + term[0:points]
    other_ref[...] = term[points:]
    contract = ((0,), (0,))
    first = dot3(grad, act, contract)
    second = dot3(hidden, cot, contract)

    @pl.when(core == 0)
    def _():
        for x in range(4):
            rows = slice(160 * x, 160 * x + 160)
            kept_ref[x, :, 0:640] = first[rows]
            kept_ref[x, :, 640:1280] = second[rows]

    @pl.when(core == 1)
    def _():
        for x in range(4):
            rows = slice(160 * x, 160 * x + 160)
            row, lane = 80 * (x % 2), 640 * (x // 2)
            parts = zip(low_high(first[rows]), low_high(second[rows]))
            for right, (a, b) in enumerate(parts):
                for upper in range(2):
                    cols = slice(320 * upper, 320 * upper + 320)
                    piece = jnp.concatenate([a[:, cols], b[:, cols]], axis=1)
                    kept_ref[2 * upper + right, row : row + 80, lane : lane + 640] = piece

    for m in range(4):
        index = jnp.where(core == 0, along_x(place_ref, m), along_y(place_ref, m))
        outs[m][...] = kept_ref[index]


def mlp(place, act, act_other, cot, cot_other, weight_in, weight_out):
    points, width = act.shape
    units = weight_in.shape[0]
    full = lambda shape: pl.BlockSpec(shape, lambda i, place: (0,) * len(shape))
    rows = pl.BlockSpec((4, None, 160, width), lambda i, place: (0, place[1], 0, 0))
    return pl.pallas_call(
        mlp_kernel,
        grid_spec=pltpu.PrefetchScalarGridSpec(
            num_scalar_prefetch=1,
            grid=(1,),
            in_specs=[full((points, width))] * 4 + [rows, rows],
            out_specs=[full((points, width))] * 2 + [full((160, 1280))] * 4,
            scratch_shapes=[pltpu.VMEM((4, 160, 1280), F32)],
        ),
        out_shape=[jax.ShapeDtypeStruct((points, width), F32)] * 2
        + [jax.ShapeDtypeStruct((160, 1280), F32)] * 4,
        compiler_params=params(57),
        cost_estimate=cost(30 * points * width * units, 12_000_000),
        name="mlp",
    )(
        place,
        act,
        act_other,
        cot,
        cot_other,
        weight_in.reshape(4, 2, 160, width),
        weight_out.reshape(4, 2, 160, width),
    )


def swap_kernel(place_ref, *refs):
    ins, outs, kept_ref = refs[:4], refs[4:8], refs[8]
    core = place_ref[1]
    total = (ins[0][...] + ins[1][...]) + (ins[2][...] + ins[3][...])

    @pl.when(core == 0)
    def _():
        for right, part in enumerate(low_high(total)):
            for upper in range(2):
                at = 320 * upper
                pair = [part[:, at : at + 320], part[:, 640 + at : 960 + at]]
                kept_ref[2 * upper + right] = jnp.concatenate(pair, axis=1)

    @pl.when(core == 1)
    def _():
        for x in range(4):
            row, col = 80 * (x % 2), 640 * (x // 2)
            kept_ref[x] = total[row : row + 80, col : col + 640]

    for m in range(4):
        index = jnp.where(core == 0, along_y(place_ref, m), along_x(place_ref, m))
        outs[m][...] = kept_ref[index]


def pair_kernel(place_ref, _, *refs):
    ins, (mine_ref, send_ref) = refs[:4], refs[4:]
    total = (ins[0][...] + ins[1][...]) + (ins[2][...] + ins[3][...])
    even = jnp.concatenate([total[:, 0:160], total[:, 320:480]], axis=1)
    odd = jnp.concatenate([total[:, 160:320], total[:, 480:640]], axis=1)
    first = place_ref[1] == 0
    mine_ref[...] = jnp.where(first, even, odd)
    send_ref[...] = jnp.where(first, odd, even)


def stack_kernel(place_ref, _, mine_ref, arrived_ref, *refs):
    outs, kept_ref = refs[:4], refs[4]
    first = place_ref[1] == 0
    mine, arrived = mine_ref[...], arrived_ref[...]
    below, above = jnp.where(first, mine, arrived), jnp.where(first, arrived, mine)
    for r in range(4):
        rows = slice(20 * r, 20 * r + 20)
        kept_ref[r] = jnp.concatenate([below[rows], above[rows]], axis=0)
    for m in range(4):
        outs[m][...] = kept_ref[lax.rem(place_ref[5] + m, 4)]


def half_kernel(place_ref, *refs):
    ins, (mine_ref, send_ref) = refs[:4], refs[4:]
    total = (ins[0][...] + ins[1][...]) + (ins[2][...] + ins[3][...])
    below = place_ref[5] < 4
    mine_ref[...] = jnp.where(below, total[0:20], total[20:40])
    send_ref[...] = jnp.where(below, total[20:40], total[0:20])


def last_kernel(mine_ref, arrived_ref, first_ref, second_ref):
    total = mine_ref[...] + arrived_ref[...]
    first_ref[...] = total[:, 0:160]
    second_ref[...] = total[:, 160:320]


def small(kernel, operands, shapes, scalars=0, scratch=(), earlier=(), name=None, flops=0):
    return pl.pallas_call(
        kernel,
        in_specs=[pl.BlockSpec(memory_space=pltpu.SMEM)] * scalars
        + EARLIER * len(earlier)
        + whole(len(operands) - scalars),
        out_specs=whole(len(shapes)),
        out_shape=[jax.ShapeDtypeStruct(shape, F32) for shape in shapes],
        scratch_shapes=scratch,
        compiler_params=params(32),
        cost_estimate=cost(flops, 4_000_000) if flops else None,
        name=name,
    )(*operands[:scalars], *earlier, *operands[scalars:])


def permute(value, target):
    sizes = (2, 2, 4, 8, 2)
    order = lambda at: int(np.ravel_multi_index(at, sizes))
    pairs = [(order(at), order(target(*at))) for at in np.ndindex(*sizes)]
    return lax.ppermute(value, AXES, pairs)


def exchange(pieces, cores):
    def target(m, yl, co, x, z, yh):
        if cores[co] == "x":
            x = (x + m) % 4
        else:
            yl, yh = yl ^ (m >> 1), yh ^ (m & 1)
        return yl, co, x, z, yh

    return [pieces[0]] + [permute(pieces[m], functools.partial(target, m)) for m in (1, 2, 3)]


def exchange_z(pieces):
    def pairs(m):
        return [(z, 4 * (z // 4) + (z + m) % 4) for z in range(8)]

    return [pieces[0]] + [lax.ppermute(pieces[m], "z", pairs(m)) for m in (1, 2, 3)]


def to_core(value):
    return lax.ppermute(value, "co", [(0, 1), (1, 0)])


def spectrum_kernel(
    block_ref, top_ref, low_ref, _, out_ref, first_ref, final_ref, mixing_ref, flat_ref
):
    for p in range(COLS // 2):
        pair = jnp.concatenate([block_ref[:, 2 * p, :], block_ref[:, 2 * p + 1, :]], axis=0)
        flat_ref[0:128, 128 * p : 128 * (p + 1)] = pair.T
    rest = [block_ref[:, 12 + q, :].T for q in range(3)]
    pieces = [rest[q][32 * g : 32 * (g + 1), :] for g in range(4) for q in range(3)]
    flat_ref[128:160, :] = jnp.concatenate(pieces, axis=1)
    result = dot3(split(flat_ref[...]), (top_ref[...], low_ref[...]), ((1,), (0,)))
    out_ref[...] = result
    mixing_ref[...] = jnp.sum(block_ref[:, 15, :], axis=0, keepdims=True)
    for r in range(OWN):
        first_ref[3 * r : 3 * r + 3, :] = result[ROWS * r : ROWS * r + 3, :]
        final_ref[3 * r : 3 * r + 3, :] = result[ROWS * r + 13 : ROWS * r + 16, :]


def spectrum(block, earlier):
    top, low = forward_table(shard_order())
    rows = OWN * ROWS
    return pl.pallas_call(
        spectrum_kernel,
        in_specs=whole(3) + EARLIER,
        out_specs=whole(4),
        out_shape=[
            jax.ShapeDtypeStruct((rows, CIRCLE), F32),
            jax.ShapeDtypeStruct((3 * OWN, CIRCLE), F32),
            jax.ShapeDtypeStruct((3 * OWN, CIRCLE), F32),
            jax.ShapeDtypeStruct((1, 128), F32),
        ],
        scratch_shapes=[pltpu.VMEM((rows, CIRCLE), F32)],
        compiler_params=params(24),
        cost_estimate=cost(6 * rows * CIRCLE * CIRCLE, 4_000_000),
        name="spectrum",
    )(block, jnp.asarray(top), jnp.asarray(low), earlier)


def kernel_spectrum_kernel(kernel_ref, top_ref, low_ref, _, out_ref):
    out_ref[...] = dot3(split(kernel_ref[...]), (top_ref[...], low_ref[...]), ((1,), (0,)))


def kernel_spectrum(kernels, earlier):
    top, low = forward_table(np.arange(CIRCLE))
    rows = BASIS * TAPS * ROWS
    flat = kernels.transpose(0, 2, 1, 3).reshape(rows, CIRCLE)
    return pl.pallas_call(
        kernel_spectrum_kernel,
        in_specs=whole(3) + EARLIER,
        out_specs=whole(1)[0],
        out_shape=jax.ShapeDtypeStruct((rows, CIRCLE), F32),
        compiler_params=params(24),
        cost_estimate=cost(6 * rows * CIRCLE * CIRCLE, 5_000_000),
        name="kernel_spectrum",
    )(flat, jnp.asarray(top), jnp.asarray(low), earlier)


def filter_kernel(
    mixing_ref, data_ref, before_ref, after_ref, kernel_ref, top_ref, low_ref, *refs
):
    out_ref, rows_ref, sum_ref = refs[-3:]
    for r in range(OWN):
        rows_ref[r, 0:3, :] = before_ref[3 * r : 3 * r + 3, :]
        rows_ref[r, 3 : 3 + ROWS, :] = data_ref[ROWS * r : ROWS * (r + 1), :]
        rows_ref[r, 3 + ROWS : 6 + ROWS, :] = after_ref[3 * r : 3 * r + 3, :]
    lane = lax.broadcasted_iota(jnp.int32, (ROWS, HALF), 1)
    ends = lane == 0

    def channel(r, carry):
        real = jnp.zeros((ROWS, HALF), F32)
        imag = jnp.zeros((ROWS, HALF), F32)
        for k in range(TAPS):
            mixed_real = jnp.zeros((ROWS, HALF), F32)
            mixed_imag = jnp.zeros((ROWS, HALF), F32)
            for b in range(BASIS):
                weight = mixing_ref[0, BASIS * r + b]
                at = ROWS * (TAPS * b + k)
                mixed_real += weight * kernel_ref[at : at + ROWS, 0:HALF]
                mixed_imag += weight * kernel_ref[at : at + ROWS, HALF:CIRCLE]
            own = jnp.where(ends, mixed_imag, mixed_real)
            cross = jnp.where(ends, 0.0, mixed_imag)
            data_real = rows_ref[r, 6 - k : 6 - k + ROWS, 0:HALF]
            data_imag = rows_ref[r, 6 - k : 6 - k + ROWS, HALF:CIRCLE]
            real += mixed_real * data_real + cross * data_imag
            imag += own * data_imag - cross * data_real
        sum_ref[r, :, 0:HALF] = real
        sum_ref[r, :, HALF:CIRCLE] = imag
        return carry

    lax.fori_loop(0, OWN, channel, 0)
    total = split(sum_ref[...].reshape(OWN * ROWS, CIRCLE))
    field = dot3((top_ref[...], low_ref[...]), total, ((1,), (1,)))
    for l in range(COLS):
        out_ref[:, l, :] = field[SHARDS * l : SHARDS * (l + 1), 0:128]
    for q in range(3):
        pieces = [
            field[SHARDS * (3 * g + q) : SHARDS * (3 * g + q + 1), 128:160] for g in range(4)
        ]
        out_ref[:, 12 + q, :] = jnp.concatenate(pieces, axis=1)
    out_ref[:, 15, :] = jnp.zeros((SHARDS, 128), F32)


def filtered(mixing, data, before, beyond, kernel, earlier):
    top, low = backward_table(shard_order())
    return pl.pallas_call(
        filter_kernel,
        in_specs=[pl.BlockSpec(memory_space=pltpu.SMEM)] + whole(6) + EARLIER * len(earlier),
        out_specs=whole(1)[0],
        out_shape=jax.ShapeDtypeStruct((SHARDS, 16, 128), F32),
        scratch_shapes=[
            pltpu.VMEM((OWN, 24, CIRCLE), F32),
            pltpu.VMEM((OWN, ROWS, CIRCLE), F32),
        ],
        compiler_params=params(32),
        cost_estimate=cost(6 * OWN * ROWS * CIRCLE * CIRCLE, 5_000_000),
        name="filter",
    )(mixing, data, before, beyond, kernel, jnp.asarray(top), jnp.asarray(low), *earlier)


def unpack_kernel(block_ref, out_ref):
    def put(l, r, pair):
        out_ref[ROWS * l : ROWS * (l + 1), SHARDS * r : SHARDS * (r + 2)] = jnp.concatenate(
            pair, axis=1
        )

    for l in range(COLS):
        turned = block_ref[:, l, :].T
        for r in range(0, 8, 2):
            put(l, r, [turned[ROWS * r : ROWS * (r + 1)], turned[ROWS * (r + 1) : ROWS * (r + 2)]])
    for q in range(3):
        turned = block_ref[:, 12 + q, :].T
        for g in range(4):
            at = 32 * g
            put(3 * g + q, 8, [turned[at : at + ROWS], turned[at + ROWS : at + 2 * ROWS]])


def unpack(block):
    return pl.pallas_call(
        unpack_kernel,
        in_specs=whole(1),
        out_specs=whole(1)[0],
        out_shape=jax.ShapeDtypeStruct((ROWS * COLS, SHARDS * OWN), F32),
        compiler_params=params(16),
        name="unpack",
    )(block)


def across(block):
    return lax.all_to_all(block, LON, split_axis=0, concat_axis=0, tiled=True)


def per_device(activation, cotangent, weight_in, weight_out, kernels, mixing):
    points = ROWS * COLS
    width = activation.shape[2]
    act = activation.transpose(1, 0, 2).reshape(points, width)
    cot = cotangent.transpose(1, 0, 2).reshape(points, width)
    place = jnp.stack([lax.axis_index(axis) for axis in (LON, "co", "yl", "yh", "x", "z")])
    unit, other, *pieces = mlp(place, act, to_core(act), cot, to_core(cot), weight_in, weight_out)
    operands = (place, mixing.T, unit, to_core(other))
    (block,) = small(pack_kernel, operands, [(SHARDS, 16, 128)], 2, name="pack")
    moved = exchange(pieces, "xy")
    spread = across(block)
    kept = (pltpu.VMEM((4, 80, 640), F32),)
    swapped = small(swap_kernel, (place, *moved), [(80, 640)] * 4, 1, kept, (), "swap", 10**10)
    kernel = kernel_spectrum(kernels, swapped[0])
    moved = exchange(swapped, "yx")
    mine, send = small(
        pair_kernel, (place, *moved), [(80, 320)] * 2, 1, (), (kernel,), "pair"
    )
    data, first, final, own_mixing = spectrum(spread, mine)
    forward = [(i, i + 1) for i in range(3)]
    backward = [(target, source) for source, target in forward]
    before = lax.ppermute(final, LAT, forward)
    beyond = lax.ppermute(first, LAT, backward)
    paired = to_core(send)
    sent = filtered(own_mixing, data, before, beyond, kernel, (paired,))
    result = across(sent)
    kept = (pltpu.VMEM((4, 40, 320), F32),)
    operands = (place, mine, paired)
    stacked = small(stack_kernel, operands, [(40, 320)] * 4, 1, kept, (sent,), "stack")
    moved = exchange_z(stacked)
    mine, send = small(half_kernel, (place, *moved), [(20, 320)] * 2, 1, name="half")
    arrived = lax.ppermute(send, "z", [(z, z ^ 4) for z in range(8)])
    grad_in, grad_out = small(last_kernel, (mine, arrived), [(20, 160)] * 2, name="last")
    field = unpack(result).reshape(COLS, ROWS, width).transpose(1, 0, 2)
    return (field, grad_in, grad_out)


def solution(mesh):
    fine = Mesh(mesh.devices.reshape(2, 2, 4, 8, 2), AXES)
    placed = (
        P(LAT, LON, None),
        P(LAT, LON, None),
        P(),
        P(),
        P(None, LAT, None, None),
        P(LON, None),
    )
    return jax.shard_map(
        per_device,
        mesh=fine,
        in_specs=placed,
        out_specs=(P(LAT, LON, None), P(LON, LAT), P(LON, LAT)),
        check_vma=False,
    )
```

```python
import functools
import math

import jax
import jax.numpy as jnp
import ml_dtypes
import numpy as np
from jax import lax
from jax.experimental import pallas as pl
from jax.experimental.pallas import tpu as pltpu
from jax.sharding import Mesh
from jax.sharding import PartitionSpec as P

AXES = ("yl", "co", "x", "z", "yh")
LAT = ("yl", "co")
LON = ("x", "z", "yh")
F32 = jnp.float32
BF16 = jnp.bfloat16
SHARDS = 64
COLS = 12
ROWS = 16
OWN = 10
CIRCLE = 768
HALF = 384
TAPS = 7
BASIS = 3
MIB = 1 << 20


def split(value):
    top = value.astype(BF16)
    return top, (value - top.astype(F32)).astype(BF16)


def dot3(left, right, dims):
    (a, b), (c, d) = left, right
    (at,), (to,) = dims
    return lax.dot_general(
        jnp.concatenate([a, b, a], axis=at),
        jnp.concatenate([c, c, d], axis=to),
        dimension_numbers=(dims, ((), ())),
        preferred_element_type=F32,
    )


def whole(n):
    return [pl.BlockSpec(memory_space=pltpu.VMEM)] * n


EARLIER = [pl.BlockSpec(memory_space=pl.ANY)]


def params(mib):
    return pltpu.CompilerParams(vmem_limit_bytes=mib * MIB)


def cost(flops, moved):
    return pl.CostEstimate(flops=flops, bytes_accessed=moved, transcendentals=0)


def table(order):
    angle = 2.0 * np.pi / CIRCLE * (order[:, None] * np.arange(HALF)[None, :] % CIRCLE)
    nyquist = np.where(order % 2 == 0, 1.0, -1.0)
    real, imag = np.cos(angle), -np.sin(angle)
    imag[:, 0] = nyquist
    return np.concatenate([real, imag], axis=1)


def parts(matrix):
    exact = matrix.astype(np.float32)
    top = exact.astype(ml_dtypes.bfloat16)
    return top, (exact - top.astype(np.float32)).astype(ml_dtypes.bfloat16)


def forward_table(order):
    return parts(table(order))


def backward_table(order):
    weight = np.full((2, HALF), 2.0 / CIRCLE)
    weight[:, 0] = 1.0 / CIRCLE
    return parts(table(order) * weight.reshape(1, -1))


def shard_order():
    return (np.arange(COLS)[:, None] + COLS * np.arange(SHARDS)[None, :]).reshape(-1)


def pack(unit, mixing_ref, shard, out_ref):
    def piece(l, r):
        return unit[ROWS * l : ROWS * (l + 1), SHARDS * r : SHARDS * (r + 1)]

    for l in range(COLS):
        out_ref[:, l, :] = jnp.concatenate([piece(l, r) for r in range(8)], axis=0).T
    for q in range(3):
        chunk = [piece(3 * g + q, r) for g in range(4) for r in (8, 9)]
        out_ref[:, 12 + q, :] = jnp.concatenate(chunk, axis=0).T
    target = lax.broadcasted_iota(jnp.int32, (SHARDS, 128), 0)
    lane = lax.broadcasted_iota(jnp.int32, (SHARDS, 128), 1)
    weights = jnp.zeros((SHARDS, 128), F32)
    for i in range(OWN):
        channel = OWN * shard + i
        here = target == lax.rem(channel, SHARDS)
        first = BASIS * lax.div(channel, SHARDS)
        for b in range(BASIS):
            weights = jnp.where(here & (lane == first + b), mixing_ref[b, i], weights)
    out_ref[:, 15, :] = weights


def pack_kernel(place_ref, mixing_ref, unit_ref, arrived_ref, block_ref):
    pack(unit_ref[...] + arrived_ref[...], mixing_ref, place_ref[0], block_ref)


def along_x(place_ref, m):
    return lax.rem(place_ref[4] + m, 4)


def along_y(place_ref, m):
    upper, right = place_ref[2], place_ref[3]
    return 2 * (1 - upper if m & 2 else upper) + (1 - right if m & 1 else right)


def low_high(rows):
    low = jnp.concatenate([rows[40 * z : 40 * z + 20] for z in range(4)], axis=0)
    high = jnp.concatenate([rows[40 * z + 20 : 40 * z + 40] for z in range(4)], axis=0)
    return low, high


def mlp_kernel(
    place_ref,
    act_ref,
    act_other_ref,
    cot_ref,
    cot_other_ref,
    in_ref,
    out_ref,
    own_ref,
    other_ref,
    *refs,
):
    outs, kept_ref = refs[:4], refs[4]
    core = place_ref[1]
    points = act_ref.shape[0]
    act = split(jnp.concatenate([act_ref[...], act_other_ref[...]], axis=0))
    cot = split(jnp.concatenate([cot_ref[...], cot_other_ref[...]], axis=0))
    w_in = split(in_ref[...].reshape(640, 640))
    w_out = split(out_ref[...].reshape(640, 640))
    preact = dot3(act, w_in, ((1,), (1,)))
    cdf = 0.5 * (1.0 + lax.erf(preact * (1.0 / math.sqrt(2.0))))
    density = jnp.exp(-0.5 * preact * preact) * (1.0 / math.sqrt(2.0 * math.pi))
    hidden = split(preact * cdf)
    slope = cdf + preact * density
    grad = split(dot3(cot, w_out, ((1,), (1,))) * slope)
    term = dot3(grad, w_in, ((1,), (0,)))
    own_ref[...] = cot_ref[...] + term[0:points]
    other_ref[...] = term[points:]
    contract = ((0,), (0,))
    first = dot3(grad, act, contract)
    second = dot3(hidden, cot, contract)

    @pl.when(core == 0)
    def _():
        for x in range(4):
            rows = slice(160 * x, 160 * x + 160)
            kept_ref[x, :, 0:640] = first[rows]
            kept_ref[x, :, 640:1280] = second[rows]

    @pl.when(core == 1)
    def _():
        for x in range(4):
            rows = slice(160 * x, 160 * x + 160)
            row, lane = 80 * (x % 2), 640 * (x // 2)
            parts = zip(low_high(first[rows]), low_high(second[rows]))
            for right, (a, b) in enumerate(parts):
                for upper in range(2):
                    cols = slice(320 * upper, 320 * upper + 320)
                    piece = jnp.concatenate([a[:, cols], b[:, cols]], axis=1)
                    kept_ref[2 * upper + right, row : row + 80, lane : lane + 640] = piece

    for m in range(4):
        index = jnp.where(core == 0, along_x(place_ref, m), along_y(place_ref, m))
        outs[m][...] = kept_ref[index]


def mlp(place, act, act_other, cot, cot_other, weight_in, weight_out):
    points, width = act.shape
    units = weight_in.shape[0]
    full = lambda shape: pl.BlockSpec(shape, lambda i, place: (0,) * len(shape))
    rows = pl.BlockSpec((4, None, 160, width), lambda i, place: (0, place[1], 0, 0))
    return pl.pallas_call(
        mlp_kernel,
        grid_spec=pltpu.PrefetchScalarGridSpec(
            num_scalar_prefetch=1,
            grid=(1,),
            in_specs=[full((points, width))] * 4 + [rows, rows],
            out_specs=[full((points, width))] * 2 + [full((160, 1280))] * 4,
            scratch_shapes=[pltpu.VMEM((4, 160, 1280), F32)],
        ),
        out_shape=[jax.ShapeDtypeStruct((points, width), F32)] * 2
        + [jax.ShapeDtypeStruct((160, 1280), F32)] * 4,
        compiler_params=params(57),
        cost_estimate=cost(30 * points * width * units, 12_000_000),
        name="mlp",
    )(
        place,
        act,
        act_other,
        cot,
        cot_other,
        weight_in.reshape(4, 2, 160, width),
        weight_out.reshape(4, 2, 160, width),
    )


def swap_kernel(place_ref, *refs):
    ins, outs, kept_ref = refs[:4], refs[4:8], refs[8]
    core = place_ref[1]
    total = (ins[0][...] + ins[1][...]) + (ins[2][...] + ins[3][...])

    @pl.when(core == 0)
    def _():
        for right, part in enumerate(low_high(total)):
            for upper in range(2):
                at = 320 * upper
                pair = [part[:, at : at + 320], part[:, 640 + at : 960 + at]]
                kept_ref[2 * upper + right] = jnp.concatenate(pair, axis=1)

    @pl.when(core == 1)
    def _():
        for x in range(4):
            row, col = 80 * (x % 2), 640 * (x // 2)
            kept_ref[x] = total[row : row + 80, col : col + 640]

    for m in range(4):
        index = jnp.where(core == 0, along_y(place_ref, m), along_x(place_ref, m))
        outs[m][...] = kept_ref[index]


def pair_kernel(place_ref, _, *refs):
    ins, outs = refs[:4], refs[4:]
    total = (ins[0][...] + ins[1][...]) + (ins[2][...] + ins[3][...])
    even = jnp.concatenate([total[:, 0:160], total[:, 320:480]], axis=1)
    odd = jnp.concatenate([total[:, 160:320], total[:, 480:640]], axis=1)
    below = place_ref[5] < 4
    outs[0][...] = jnp.where(below, even, odd)
    outs[1][...] = jnp.where(below, odd, even)


def stack_kernel(place_ref, _, first_ref, second_ref, *refs):
    outs, kept_ref = refs[:4], refs[4]
    total = first_ref[...] + second_ref[...]
    for r in range(4):
        kept_ref[r, 0:20, :] = total[20 * r : 20 * r + 20]
    for m in range(4):
        outs[m][...] = kept_ref[lax.rem(place_ref[5] + m, 4), 0:20, :]


def last_kernel(*refs):
    ins, (first_ref, second_ref) = refs[:4], refs[4:]
    total = (ins[0][...] + ins[1][...]) + (ins[2][...] + ins[3][...])
    first_ref[...] = total[:, 0:160]
    second_ref[...] = total[:, 160:320]


def small(kernel, operands, shapes, scalars=0, scratch=(), earlier=(), name=None, flops=0):
    return pl.pallas_call(
        kernel,
        in_specs=[pl.BlockSpec(memory_space=pltpu.SMEM)] * scalars
        + EARLIER * len(earlier)
        + whole(len(operands) - scalars),
        out_specs=whole(len(shapes)),
        out_shape=[jax.ShapeDtypeStruct(shape, F32) for shape in shapes],
        scratch_shapes=scratch,
        compiler_params=params(16),
        cost_estimate=cost(flops, 4_000_000) if flops else None,
        name=name,
    )(*operands[:scalars], *earlier, *operands[scalars:])


def permute(value, target):
    sizes = (2, 2, 4, 8, 2)
    order = lambda at: int(np.ravel_multi_index(at, sizes))
    pairs = [(order(at), order(target(*at))) for at in np.ndindex(*sizes)]
    return lax.ppermute(value, AXES, pairs)


def exchange(pieces, cores):
    def target(m, yl, co, x, z, yh):
        if cores[co] == "x":
            x = (x + m) % 4
        else:
            yl, yh = yl ^ (m >> 1), yh ^ (m & 1)
        return yl, co, x, z, yh

    return [pieces[0]] + [permute(pieces[m], functools.partial(target, m)) for m in (1, 2, 3)]


def exchange_pair(pieces):
    def target(b, yl, co, x, z, yh):
        return yl, (z // 4) ^ b, x, 4 * co + z % 4, yh

    return [permute(pieces[b], functools.partial(target, b)) for b in range(2)]


def exchange_z(pieces):
    def pairs(m):
        return [(z, 4 * (z // 4) + (z + m) % 4) for z in range(8)]

    return [pieces[0]] + [lax.ppermute(pieces[m], "z", pairs(m)) for m in (1, 2, 3)]


def to_core(value):
    return lax.ppermute(value, "co", [(0, 1), (1, 0)])


def spectrum_kernel(
    block_ref, top_ref, low_ref, _, out_ref, first_ref, final_ref, mixing_ref, flat_ref
):
    for p in range(COLS // 2):
        pair = jnp.concatenate([block_ref[:, 2 * p, :], block_ref[:, 2 * p + 1, :]], axis=0)
        flat_ref[0:128, 128 * p : 128 * (p + 1)] = pair.T
    rest = [block_ref[:, 12 + q, :].T for q in range(3)]
    pieces = [rest[q][32 * g : 32 * (g + 1), :] for g in range(4) for q in range(3)]
    flat_ref[128:160, :] = jnp.concatenate(pieces, axis=1)
    result = dot3(split(flat_ref[...]), (top_ref[...], low_ref[...]), ((1,), (0,)))
    out_ref[...] = result
    mixing_ref[...] = jnp.sum(block_ref[:, 15, :], axis=0, keepdims=True)
    for r in range(OWN):
        first_ref[3 * r : 3 * r + 3, :] = result[ROWS * r : ROWS * r + 3, :]
        final_ref[3 * r : 3 * r + 3, :] = result[ROWS * r + 13 : ROWS * r + 16, :]


def spectrum(block, earlier):
    top, low = forward_table(shard_order())
    rows = OWN * ROWS
    return pl.pallas_call(
        spectrum_kernel,
        in_specs=whole(3) + EARLIER,
        out_specs=whole(4),
        out_shape=[
            jax.ShapeDtypeStruct((rows, CIRCLE), F32),
            jax.ShapeDtypeStruct((3 * OWN, CIRCLE), F32),
            jax.ShapeDtypeStruct((3 * OWN, CIRCLE), F32),
            jax.ShapeDtypeStruct((1, 128), F32),
        ],
        scratch_shapes=[pltpu.VMEM((rows, CIRCLE), F32)],
        compiler_params=params(24),
        cost_estimate=cost(6 * rows * CIRCLE * CIRCLE, 4_000_000),
        name="spectrum",
    )(block, jnp.asarray(top), jnp.asarray(low), earlier)


def kernel_spectrum_kernel(kernel_ref, top_ref, low_ref, _, out_ref):
    out_ref[...] = dot3(split(kernel_ref[...]), (top_ref[...], low_ref[...]), ((1,), (0,)))


def kernel_spectrum(kernels, earlier):
    top, low = forward_table(np.arange(CIRCLE))
    rows = BASIS * TAPS * ROWS
    flat = kernels.transpose(0, 2, 1, 3).reshape(rows, CIRCLE)
    return pl.pallas_call(
        kernel_spectrum_kernel,
        in_specs=whole(3) + EARLIER,
        out_specs=whole(1)[0],
        out_shape=jax.ShapeDtypeStruct((rows, CIRCLE), F32),
        compiler_params=params(24),
        cost_estimate=cost(6 * rows * CIRCLE * CIRCLE, 5_000_000),
        name="kernel_spectrum",
    )(flat, jnp.asarray(top), jnp.asarray(low), earlier)


def filter_kernel(
    mixing_ref, data_ref, before_ref, after_ref, kernel_ref, top_ref, low_ref, *refs
):
    out_ref, rows_ref, sum_ref = refs[-3:]
    for r in range(OWN):
        rows_ref[r, 0:3, :] = before_ref[3 * r : 3 * r + 3, :]
        rows_ref[r, 3 : 3 + ROWS, :] = data_ref[ROWS * r : ROWS * (r + 1), :]
        rows_ref[r, 3 + ROWS : 6 + ROWS, :] = after_ref[3 * r : 3 * r + 3, :]
    lane = lax.broadcasted_iota(jnp.int32, (ROWS, HALF), 1)
    ends = lane == 0

    def channel(r, carry):
        real = jnp.zeros((ROWS, HALF), F32)
        imag = jnp.zeros((ROWS, HALF), F32)
        for k in range(TAPS):
            mixed_real = jnp.zeros((ROWS, HALF), F32)
            mixed_imag = jnp.zeros((ROWS, HALF), F32)
            for b in range(BASIS):
                weight = mixing_ref[0, BASIS * r + b]
                at = ROWS * (TAPS * b + k)
                mixed_real += weight * kernel_ref[at : at + ROWS, 0:HALF]
                mixed_imag += weight * kernel_ref[at : at + ROWS, HALF:CIRCLE]
            own = jnp.where(ends, mixed_imag, mixed_real)
            cross = jnp.where(ends, 0.0, mixed_imag)
            data_real = rows_ref[r, 6 - k : 6 - k + ROWS, 0:HALF]
            data_imag = rows_ref[r, 6 - k : 6 - k + ROWS, HALF:CIRCLE]
            real += mixed_real * data_real + cross * data_imag
            imag += own * data_imag - cross * data_real
        sum_ref[r, :, 0:HALF] = real
        sum_ref[r, :, HALF:CIRCLE] = imag
        return carry

    lax.fori_loop(0, OWN, channel, 0)
    total = split(sum_ref[...].reshape(OWN * ROWS, CIRCLE))
    field = dot3((top_ref[...], low_ref[...]), total, ((1,), (1,)))
    for l in range(COLS):
        out_ref[:, l, :] = field[SHARDS * l : SHARDS * (l + 1), 0:128]
    for q in range(3):
        pieces = [
            field[SHARDS * (3 * g + q) : SHARDS * (3 * g + q + 1), 128:160] for g in range(4)
        ]
        out_ref[:, 12 + q, :] = jnp.concatenate(pieces, axis=1)
    out_ref[:, 15, :] = jnp.zeros((SHARDS, 128), F32)


def filtered(mixing, data, before, beyond, kernel, earlier):
    top, low = backward_table(shard_order())
    return pl.pallas_call(
        filter_kernel,
        in_specs=[pl.BlockSpec(memory_space=pltpu.SMEM)] + whole(6) + EARLIER * len(earlier),
        out_specs=whole(1)[0],
        out_shape=jax.ShapeDtypeStruct((SHARDS, 16, 128), F32),
        scratch_shapes=[
            pltpu.VMEM((OWN, 24, CIRCLE), F32),
            pltpu.VMEM((OWN, ROWS, CIRCLE), F32),
        ],
        compiler_params=params(32),
        cost_estimate=cost(6 * OWN * ROWS * CIRCLE * CIRCLE, 5_000_000),
        name="filter",
    )(mixing, data, before, beyond, kernel, jnp.asarray(top), jnp.asarray(low), *earlier)


def unpack_kernel(block_ref, out_ref):
    def put(l, r, pair):
        out_ref[ROWS * l : ROWS * (l + 1), SHARDS * r : SHARDS * (r + 2)] = jnp.concatenate(
            pair, axis=1
        )

    for l in range(COLS):
        turned = block_ref[:, l, :].T
        for r in range(0, 8, 2):
            put(l, r, [turned[ROWS * r : ROWS * (r + 1)], turned[ROWS * (r + 1) : ROWS * (r + 2)]])
    for q in range(3):
        turned = block_ref[:, 12 + q, :].T
        for g in range(4):
            at = 32 * g
            put(3 * g + q, 8, [turned[at : at + ROWS], turned[at + ROWS : at + 2 * ROWS]])


def unpack(block):
    return pl.pallas_call(
        unpack_kernel,
        in_specs=whole(1),
        out_specs=whole(1)[0],
        out_shape=jax.ShapeDtypeStruct((ROWS * COLS, SHARDS * OWN), F32),
        compiler_params=params(16),
        name="unpack",
    )(block)


def across(block):
    return lax.all_to_all(block, LON, split_axis=0, concat_axis=0, tiled=True)


def per_device(activation, cotangent, weight_in, weight_out, kernels, mixing):
    points = ROWS * COLS
    width = activation.shape[2]
    act = activation.transpose(1, 0, 2).reshape(points, width)
    cot = cotangent.transpose(1, 0, 2).reshape(points, width)
    place = jnp.stack([lax.axis_index(axis) for axis in (LON, "co", "yl", "yh", "x", "z")])
    unit, other, *pieces = mlp(place, act, to_core(act), cot, to_core(cot), weight_in, weight_out)
    operands = (place, mixing.T, unit, to_core(other))
    (block,) = small(pack_kernel, operands, [(SHARDS, 16, 128)], 2, name="pack")
    moved = exchange(pieces, "xy")
    spread = across(block)
    kept = (pltpu.VMEM((4, 80, 640), F32),)
    swapped = small(swap_kernel, (place, *moved), [(80, 640)] * 4, 1, kept, (), "swap", 10**10)
    kernel = kernel_spectrum(kernels, swapped[0])
    moved = exchange(swapped, "yx")
    pair = small(pair_kernel, (place, *moved), [(80, 320)] * 2, 1, (), (kernel,), "pair")
    paired = exchange_pair(pair)
    data, first, final, own_mixing = spectrum(spread, pair[0])
    forward = [(i, i + 1) for i in range(3)]
    backward = [(target, source) for source, target in forward]
    before = lax.ppermute(final, LAT, forward)
    beyond = lax.ppermute(first, LAT, backward)
    sent = filtered(own_mixing, data, before, beyond, kernel, paired)
    result = across(sent)
    kept = (pltpu.VMEM((4, 24, 320), F32),)
    stacked = small(stack_kernel, (place, *paired), [(20, 320)] * 4, 1, kept, (sent,), "stack")
    grad_in, grad_out = small(last_kernel, exchange_z(stacked), [(20, 160)] * 2, name="last")
    field = unpack(result).reshape(COLS, ROWS, width).transpose(1, 0, 2)
    return (field, grad_in, grad_out)


def solution(mesh):
    fine = Mesh(mesh.devices.reshape(2, 2, 4, 8, 2), AXES)
    placed = (
        P(LAT, LON, None),
        P(LAT, LON, None),
        P(),
        P(),
        P(None, LAT, None, None),
        P(LON, None),
    )
    return jax.shard_map(
        per_device,
        mesh=fine,
        in_specs=placed,
        out_specs=(P(LAT, LON, None), P(LON, LAT), P(LON, LAT)),
        check_vma=False,
    )
```

```python
import functools
import math

import jax
import jax.numpy as jnp
import ml_dtypes
import numpy as np
from jax import lax
from jax.experimental import pallas as pl
from jax.experimental.pallas import tpu as pltpu
from jax.sharding import Mesh
from jax.sharding import PartitionSpec as P

AXES = ("yl", "co", "x", "z", "yh")
LAT = ("yl", "co")
LON = ("x", "z", "yh")
F32 = jnp.float32
BF16 = jnp.bfloat16
SHARDS = 64
COLS = 12
ROWS = 16
OWN = 10
CIRCLE = 768
HALF = 384
TAPS = 7
BASIS = 3
MIB = 1 << 20


def split(value):
    top = value.astype(BF16)
    return top, (value - top.astype(F32)).astype(BF16)


def dot3(left, right, dims):
    (a, b), (c, d) = left, right
    (at,), (to,) = dims
    return lax.dot_general(
        jnp.concatenate([a, b, a], axis=at),
        jnp.concatenate([c, c, d], axis=to),
        dimension_numbers=(dims, ((), ())),
        preferred_element_type=F32,
    )


def whole(n):
    return [pl.BlockSpec(memory_space=pltpu.VMEM)] * n


EARLIER = [pl.BlockSpec(memory_space=pl.ANY)]


def params(mib):
    return pltpu.CompilerParams(vmem_limit_bytes=mib * MIB)


def cost(flops, moved):
    return pl.CostEstimate(flops=flops, bytes_accessed=moved, transcendentals=0)


def table(order):
    angle = 2.0 * np.pi / CIRCLE * (order[:, None] * np.arange(HALF)[None, :] % CIRCLE)
    nyquist = np.where(order % 2 == 0, 1.0, -1.0)
    real, imag = np.cos(angle), -np.sin(angle)
    imag[:, 0] = nyquist
    return np.concatenate([real, imag], axis=1)


def parts(matrix):
    exact = matrix.astype(np.float32)
    top = exact.astype(ml_dtypes.bfloat16)
    return top, (exact - top.astype(np.float32)).astype(ml_dtypes.bfloat16)


def forward_table(order):
    return parts(table(order))


def backward_table(order):
    weight = np.full((2, HALF), 2.0 / CIRCLE)
    weight[:, 0] = 1.0 / CIRCLE
    return parts(table(order) * weight.reshape(1, -1))


def shard_order():
    return (np.arange(COLS)[:, None] + COLS * np.arange(SHARDS)[None, :]).reshape(-1)


def pack(unit, mixing_ref, shard, out_ref):
    def piece(l, r):
        return unit[ROWS * l : ROWS * (l + 1), SHARDS * r : SHARDS * (r + 1)]

    for l in range(COLS):
        out_ref[:, l, :] = jnp.concatenate([piece(l, r) for r in range(8)], axis=0).T
    for q in range(3):
        chunk = [piece(3 * g + q, r) for g in range(4) for r in (8, 9)]
        out_ref[:, 12 + q, :] = jnp.concatenate(chunk, axis=0).T
    target = lax.broadcasted_iota(jnp.int32, (SHARDS, 128), 0)
    lane = lax.broadcasted_iota(jnp.int32, (SHARDS, 128), 1)
    weights = jnp.zeros((SHARDS, 128), F32)
    for i in range(OWN):
        channel = OWN * shard + i
        here = target == lax.rem(channel, SHARDS)
        first = BASIS * lax.div(channel, SHARDS)
        for b in range(BASIS):
            weights = jnp.where(here & (lane == first + b), mixing_ref[b, i], weights)
    out_ref[:, 15, :] = weights


def pack_kernel(place_ref, mixing_ref, unit_ref, arrived_ref, block_ref):
    pack(unit_ref[...] + arrived_ref[...], mixing_ref, place_ref[0], block_ref)


def along_x(place_ref, m):
    return lax.rem(place_ref[4] + m, 4)


def along_y(place_ref, m):
    upper, right = place_ref[2], place_ref[3]
    return 2 * (1 - upper if m & 2 else upper) + (1 - right if m & 1 else right)


def low_high(rows):
    low = jnp.concatenate([rows[40 * z : 40 * z + 20] for z in range(4)], axis=0)
    high = jnp.concatenate([rows[40 * z + 20 : 40 * z + 40] for z in range(4)], axis=0)
    return low, high


def mlp_kernel(
    place_ref,
    act_ref,
    act_other_ref,
    cot_ref,
    cot_other_ref,
    in_ref,
    out_ref,
    own_ref,
    other_ref,
    *refs,
):
    outs, kept_ref = refs[:4], refs[4]
    core = place_ref[1]
    points = act_ref.shape[0]
    act = split(jnp.concatenate([act_ref[...], act_other_ref[...]], axis=0))
    cot = split(jnp.concatenate([cot_ref[...], cot_other_ref[...]], axis=0))
    w_in = split(in_ref[...].reshape(640, 640))
    w_out = split(out_ref[...].reshape(640, 640))
    preact = dot3(act, w_in, ((1,), (1,)))
    cdf = 0.5 * (1.0 + lax.erf(preact * (1.0 / math.sqrt(2.0))))
    density = jnp.exp(-0.5 * preact * preact) * (1.0 / math.sqrt(2.0 * math.pi))
    hidden = split(preact * cdf)
    slope = cdf + preact * density
    grad = split(dot3(cot, w_out, ((1,), (1,))) * slope)
    term = dot3(grad, w_in, ((1,), (0,)))
    own_ref[...] = cot_ref[...] + term[0:points]
    other_ref[...] = term[points:]
    contract = ((0,), (0,))
    first = dot3(grad, act, contract)
    second = dot3(hidden, cot, contract)

    @pl.when(core == 0)
    def _():
        for x in range(4):
            rows = slice(160 * x, 160 * x + 160)
            kept_ref[x, :, 0:640] = first[rows]
            kept_ref[x, :, 640:1280] = second[rows]

    @pl.when(core == 1)
    def _():
        for x in range(4):
            rows = slice(160 * x, 160 * x + 160)
            row, lane = 80 * (x % 2), 640 * (x // 2)
            parts = zip(low_high(first[rows]), low_high(second[rows]))
            for right, (a, b) in enumerate(parts):
                for upper in range(2):
                    cols = slice(320 * upper, 320 * upper + 320)
                    piece = jnp.concatenate([a[:, cols], b[:, cols]], axis=1)
                    kept_ref[2 * upper + right, row : row + 80, lane : lane + 640] = piece

    for m in range(4):
        index = jnp.where(core == 0, along_x(place_ref, m), along_y(place_ref, m))
        outs[m][...] = kept_ref[index]


def mlp(place, act, act_other, cot, cot_other, weight_in, weight_out):
    points, width = act.shape
    units = weight_in.shape[0]
    full = lambda shape: pl.BlockSpec(shape, lambda i, place: (0,) * len(shape))
    rows = pl.BlockSpec((4, None, 160, width), lambda i, place: (0, place[1], 0, 0))
    return pl.pallas_call(
        mlp_kernel,
        grid_spec=pltpu.PrefetchScalarGridSpec(
            num_scalar_prefetch=1,
            grid=(1,),
            in_specs=[full((points, width))] * 4 + [rows, rows],
            out_specs=[full((points, width))] * 2 + [full((160, 1280))] * 4,
            scratch_shapes=[pltpu.VMEM((4, 160, 1280), F32)],
        ),
        out_shape=[jax.ShapeDtypeStruct((points, width), F32)] * 2
        + [jax.ShapeDtypeStruct((160, 1280), F32)] * 4,
        compiler_params=params(57),
        cost_estimate=cost(30 * points * width * units, 12_000_000),
        name="mlp",
    )(
        place,
        act,
        act_other,
        cot,
        cot_other,
        weight_in.reshape(4, 2, 160, width),
        weight_out.reshape(4, 2, 160, width),
    )


def swap_kernel(place_ref, *refs):
    ins, outs, kept_ref = refs[:4], refs[4:8], refs[8]
    core = place_ref[1]
    total = (ins[0][...] + ins[1][...]) + (ins[2][...] + ins[3][...])

    @pl.when(core == 0)
    def _():
        for right, part in enumerate(low_high(total)):
            for upper in range(2):
                at = 320 * upper
                pair = [part[:, at : at + 320], part[:, 640 + at : 960 + at]]
                kept_ref[2 * upper + right] = jnp.concatenate(pair, axis=1)

    @pl.when(core == 1)
    def _():
        for x in range(4):
            row, col = 80 * (x % 2), 640 * (x // 2)
            kept_ref[x] = total[row : row + 80, col : col + 640]

    for m in range(4):
        index = jnp.where(core == 0, along_y(place_ref, m), along_x(place_ref, m))
        outs[m][...] = kept_ref[index]


def pair_kernel(place_ref, _, *refs):
    ins, (mine_ref, send_ref) = refs[:4], refs[4:]
    total = (ins[0][...] + ins[1][...]) + (ins[2][...] + ins[3][...])
    even = jnp.concatenate([total[:, 0:160], total[:, 320:480]], axis=1)
    odd = jnp.concatenate([total[:, 160:320], total[:, 480:640]], axis=1)
    first = place_ref[1] == 0
    mine_ref[...] = jnp.where(first, even, odd)
    send_ref[...] = jnp.where(first, odd, even)


def stack_kernel(place_ref, _, mine_ref, arrived_ref, *refs):
    outs, kept_ref = refs[:8], refs[8]
    first = place_ref[1] == 0
    mine, arrived = mine_ref[...], arrived_ref[...]
    below, above = jnp.where(first, mine, arrived), jnp.where(first, arrived, mine)
    for z in range(4):
        kept_ref[z, 0:20, :] = below[20 * z : 20 * z + 20]
        kept_ref[4 + z, 0:20, :] = above[20 * z : 20 * z + 20]
    for m in range(8):
        outs[m][...] = kept_ref[lax.rem(place_ref[5] + m, 8), 0:20, :]


def last_kernel(*refs):
    first_ref, second_ref = refs[8:]
    a, b, c, d = (refs[m][...] + refs[m + 4][...] for m in range(4))
    total = (a + b) + (c + d)
    first_ref[...] = total[:, 0:160]
    second_ref[...] = total[:, 160:320]


def small(kernel, operands, shapes, scalars=0, scratch=(), earlier=(), name=None, flops=0):
    return pl.pallas_call(
        kernel,
        in_specs=[pl.BlockSpec(memory_space=pltpu.SMEM)] * scalars
        + EARLIER * len(earlier)
        + whole(len(operands) - scalars),
        out_specs=whole(len(shapes)),
        out_shape=[jax.ShapeDtypeStruct(shape, F32) for shape in shapes],
        scratch_shapes=scratch,
        compiler_params=params(32),
        cost_estimate=cost(flops, 4_000_000) if flops else None,
        name=name,
    )(*operands[:scalars], *earlier, *operands[scalars:])


def permute(value, target):
    sizes = (2, 2, 4, 8, 2)
    order = lambda at: int(np.ravel_multi_index(at, sizes))
    pairs = [(order(at), order(target(*at))) for at in np.ndindex(*sizes)]
    return lax.ppermute(value, AXES, pairs)


def exchange(pieces, cores):
    def target(m, yl, co, x, z, yh):
        if cores[co] == "x":
            x = (x + m) % 4
        else:
            yl, yh = yl ^ (m >> 1), yh ^ (m & 1)
        return yl, co, x, z, yh

    return [pieces[0]] + [permute(pieces[m], functools.partial(target, m)) for m in (1, 2, 3)]


def exchange_z(pieces):
    far = (1, 7, 4, 3, 5, 2, 6)
    return [pieces[0]] + [
        lax.ppermute(pieces[m], "z", [(z, (z + m) % 8) for z in range(8)]) for m in far
    ]


def to_core(value):
    return lax.ppermute(value, "co", [(0, 1), (1, 0)])


def spectrum_kernel(
    block_ref, top_ref, low_ref, _, out_ref, first_ref, final_ref, mixing_ref, flat_ref
):
    for p in range(COLS // 2):
        pair = jnp.concatenate([block_ref[:, 2 * p, :], block_ref[:, 2 * p + 1, :]], axis=0)
        flat_ref[0:128, 128 * p : 128 * (p + 1)] = pair.T
    rest = [block_ref[:, 12 + q, :].T for q in range(3)]
    pieces = [rest[q][32 * g : 32 * (g + 1), :] for g in range(4) for q in range(3)]
    flat_ref[128:160, :] = jnp.concatenate(pieces, axis=1)
    result = dot3(split(flat_ref[...]), (top_ref[...], low_ref[...]), ((1,), (0,)))
    out_ref[...] = result
    mixing_ref[...] = jnp.sum(block_ref[:, 15, :], axis=0, keepdims=True)
    for r in range(OWN):
        first_ref[3 * r : 3 * r + 3, :] = result[ROWS * r : ROWS * r + 3, :]
        final_ref[3 * r : 3 * r + 3, :] = result[ROWS * r + 13 : ROWS * r + 16, :]


def spectrum(block, earlier):
    top, low = forward_table(shard_order())
    rows = OWN * ROWS
    return pl.pallas_call(
        spectrum_kernel,
        in_specs=whole(3) + EARLIER,
        out_specs=whole(4),
        out_shape=[
            jax.ShapeDtypeStruct((rows, CIRCLE), F32),
            jax.ShapeDtypeStruct((3 * OWN, CIRCLE), F32),
            jax.ShapeDtypeStruct((3 * OWN, CIRCLE), F32),
            jax.ShapeDtypeStruct((1, 128), F32),
        ],
        scratch_shapes=[pltpu.VMEM((rows, CIRCLE), F32)],
        compiler_params=params(24),
        cost_estimate=cost(6 * rows * CIRCLE * CIRCLE, 4_000_000),
        name="spectrum",
    )(block, jnp.asarray(top), jnp.asarray(low), earlier)


def kernel_spectrum_kernel(kernel_ref, top_ref, low_ref, _, out_ref):
    out_ref[...] = dot3(split(kernel_ref[...]), (top_ref[...], low_ref[...]), ((1,), (0,)))


def kernel_spectrum(kernels, earlier):
    top, low = forward_table(np.arange(CIRCLE))
    rows = BASIS * TAPS * ROWS
    flat = kernels.transpose(0, 2, 1, 3).reshape(rows, CIRCLE)
    return pl.pallas_call(
        kernel_spectrum_kernel,
        in_specs=whole(3) + EARLIER,
        out_specs=whole(1)[0],
        out_shape=jax.ShapeDtypeStruct((rows, CIRCLE), F32),
        compiler_params=params(24),
        cost_estimate=cost(6 * rows * CIRCLE * CIRCLE, 5_000_000),
        name="kernel_spectrum",
    )(flat, jnp.asarray(top), jnp.asarray(low), earlier)


def filter_kernel(
    mixing_ref, data_ref, before_ref, after_ref, kernel_ref, top_ref, low_ref, *refs
):
    out_ref, rows_ref, sum_ref = refs[-3:]
    for r in range(OWN):
        rows_ref[r, 0:3, :] = before_ref[3 * r : 3 * r + 3, :]
        rows_ref[r, 3 : 3 + ROWS, :] = data_ref[ROWS * r : ROWS * (r + 1), :]
        rows_ref[r, 3 + ROWS : 6 + ROWS, :] = after_ref[3 * r : 3 * r + 3, :]
    lane = lax.broadcasted_iota(jnp.int32, (ROWS, HALF), 1)
    ends = lane == 0

    def channel(r, carry):
        real = jnp.zeros((ROWS, HALF), F32)
        imag = jnp.zeros((ROWS, HALF), F32)
        for k in range(TAPS):
            mixed_real = jnp.zeros((ROWS, HALF), F32)
            mixed_imag = jnp.zeros((ROWS, HALF), F32)
            for b in range(BASIS):
                weight = mixing_ref[0, BASIS * r + b]
                at = ROWS * (TAPS * b + k)
                mixed_real += weight * kernel_ref[at : at + ROWS, 0:HALF]
                mixed_imag += weight * kernel_ref[at : at + ROWS, HALF:CIRCLE]
            own = jnp.where(ends, mixed_imag, mixed_real)
            cross = jnp.where(ends, 0.0, mixed_imag)
            data_real = rows_ref[r, 6 - k : 6 - k + ROWS, 0:HALF]
            data_imag = rows_ref[r, 6 - k : 6 - k + ROWS, HALF:CIRCLE]
            real += mixed_real * data_real + cross * data_imag
            imag += own * data_imag - cross * data_real
        sum_ref[r, :, 0:HALF] = real
        sum_ref[r, :, HALF:CIRCLE] = imag
        return carry

    lax.fori_loop(0, OWN, channel, 0)
    total = split(sum_ref[...].reshape(OWN * ROWS, CIRCLE))
    field = dot3((top_ref[...], low_ref[...]), total, ((1,), (1,)))
    for l in range(COLS):
        out_ref[:, l, :] = field[SHARDS * l : SHARDS * (l + 1), 0:128]
    for q in range(3):
        pieces = [
            field[SHARDS * (3 * g + q) : SHARDS * (3 * g + q + 1), 128:160] for g in range(4)
        ]
        out_ref[:, 12 + q, :] = jnp.concatenate(pieces, axis=1)
    out_ref[:, 15, :] = jnp.zeros((SHARDS, 128), F32)


def filtered(mixing, data, before, beyond, kernel, earlier):
    top, low = backward_table(shard_order())
    return pl.pallas_call(
        filter_kernel,
        in_specs=[pl.BlockSpec(memory_space=pltpu.SMEM)] + whole(6) + EARLIER * len(earlier),
        out_specs=whole(1)[0],
        out_shape=jax.ShapeDtypeStruct((SHARDS, 16, 128), F32),
        scratch_shapes=[
            pltpu.VMEM((OWN, 24, CIRCLE), F32),
            pltpu.VMEM((OWN, ROWS, CIRCLE), F32),
        ],
        compiler_params=params(32),
        cost_estimate=cost(6 * OWN * ROWS * CIRCLE * CIRCLE, 5_000_000),
        name="filter",
    )(mixing, data, before, beyond, kernel, jnp.asarray(top), jnp.asarray(low), *earlier)


def unpack_kernel(block_ref, out_ref):
    def put(l, r, pair):
        out_ref[ROWS * l : ROWS * (l + 1), SHARDS * r : SHARDS * (r + 2)] = jnp.concatenate(
            pair, axis=1
        )

    for l in range(COLS):
        turned = block_ref[:, l, :].T
        for r in range(0, 8, 2):
            put(l, r, [turned[ROWS * r : ROWS * (r + 1)], turned[ROWS * (r + 1) : ROWS * (r + 2)]])
    for q in range(3):
        turned = block_ref[:, 12 + q, :].T
        for g in range(4):
            at = 32 * g
            put(3 * g + q, 8, [turned[at : at + ROWS], turned[at + ROWS : at + 2 * ROWS]])


def unpack(block):
    return pl.pallas_call(
        unpack_kernel,
        in_specs=whole(1),
        out_specs=whole(1)[0],
        out_shape=jax.ShapeDtypeStruct((ROWS * COLS, SHARDS * OWN), F32),
        compiler_params=params(16),
        name="unpack",
    )(block)


def across(block):
    return lax.all_to_all(block, LON, split_axis=0, concat_axis=0, tiled=True)


def per_device(activation, cotangent, weight_in, weight_out, kernels, mixing):
    points = ROWS * COLS
    width = activation.shape[2]
    act = activation.transpose(1, 0, 2).reshape(points, width)
    cot = cotangent.transpose(1, 0, 2).reshape(points, width)
    place = jnp.stack([lax.axis_index(axis) for axis in (LON, "co", "yl", "yh", "x", "z")])
    unit, other, *pieces = mlp(place, act, to_core(act), cot, to_core(cot), weight_in, weight_out)
    operands = (place, mixing.T, unit, to_core(other))
    (block,) = small(pack_kernel, operands, [(SHARDS, 16, 128)], 2, name="pack")
    moved = exchange(pieces, "xy")
    spread = across(block)
    kept = (pltpu.VMEM((4, 80, 640), F32),)
    swapped = small(swap_kernel, (place, *moved), [(80, 640)] * 4, 1, kept, (), "swap", 10**10)
    kernel = kernel_spectrum(kernels, swapped[0])
    moved = exchange(swapped, "yx")
    mine, send = small(
        pair_kernel, (place, *moved), [(80, 320)] * 2, 1, (), (kernel,), "pair"
    )
    data, first, final, own_mixing = spectrum(spread, mine)
    forward = [(i, i + 1) for i in range(3)]
    backward = [(target, source) for source, target in forward]
    before = lax.ppermute(final, LAT, forward)
    beyond = lax.ppermute(first, LAT, backward)
    paired = to_core(send)
    sent = filtered(own_mixing, data, before, beyond, kernel, (paired,))
    result = across(sent)
    kept = (pltpu.VMEM((8, 24, 320), F32),)
    operands = (place, mine, paired)
    stacked = small(stack_kernel, operands, [(20, 320)] * 8, 1, kept, (sent,), "stack")
    grad_in, grad_out = small(last_kernel, exchange_z(stacked), [(20, 160)] * 2, name="last")
    field = unpack(result).reshape(COLS, ROWS, width).transpose(1, 0, 2)
    return (field, grad_in, grad_out)


def solution(mesh):
    fine = Mesh(mesh.devices.reshape(2, 2, 4, 8, 2), AXES)
    placed = (
        P(LAT, LON, None),
        P(LAT, LON, None),
        P(),
        P(),
        P(None, LAT, None, None),
        P(LON, None),
    )
    return jax.shard_map(
        per_device,
        mesh=fine,
        in_specs=placed,
        out_specs=(P(LAT, LON, None), P(LON, LAT), P(LON, LAT)),
        check_vma=False,
    )
```

```python
import functools
import math

import jax
import jax.numpy as jnp
import ml_dtypes
import numpy as np
from jax import lax
from jax.experimental import pallas as pl
from jax.experimental.pallas import tpu as pltpu
from jax.sharding import Mesh
from jax.sharding import PartitionSpec as P

AXES = ("yl", "co", "x", "z", "yh")
LAT = ("yl", "co")
LON = ("x", "z", "yh")
F32 = jnp.float32
BF16 = jnp.bfloat16
SHARDS = 64
COLS = 12
ROWS = 16
OWN = 10
CIRCLE = 768
HALF = 384
TAPS = 7
BASIS = 3
MIB = 1 << 20


def split(value):
    top = value.astype(BF16)
    return top, (value - top.astype(F32)).astype(BF16)


def dot3(left, right, dims):
    (a, b), (c, d) = left, right
    (at,), (to,) = dims
    return lax.dot_general(
        jnp.concatenate([a, b, a], axis=at),
        jnp.concatenate([c, c, d], axis=to),
        dimension_numbers=(dims, ((), ())),
        preferred_element_type=F32,
    )


def whole(n):
    return [pl.BlockSpec(memory_space=pltpu.VMEM)] * n


EARLIER = [pl.BlockSpec(memory_space=pl.ANY)]


def params(mib):
    return pltpu.CompilerParams(vmem_limit_bytes=mib * MIB)


def cost(flops, moved):
    return pl.CostEstimate(flops=flops, bytes_accessed=moved, transcendentals=0)


def table(order):
    angle = 2.0 * np.pi / CIRCLE * (order[:, None] * np.arange(HALF)[None, :] % CIRCLE)
    nyquist = np.where(order % 2 == 0, 1.0, -1.0)
    real, imag = np.cos(angle), -np.sin(angle)
    imag[:, 0] = nyquist
    return np.concatenate([real, imag], axis=1)


def parts(matrix):
    exact = matrix.astype(np.float32)
    top = exact.astype(ml_dtypes.bfloat16)
    return top, (exact - top.astype(np.float32)).astype(ml_dtypes.bfloat16)


def forward_table(order):
    return parts(table(order))


def backward_table(order):
    weight = np.full((2, HALF), 2.0 / CIRCLE)
    weight[:, 0] = 1.0 / CIRCLE
    return parts(table(order) * weight.reshape(1, -1))


def shard_order():
    return (np.arange(COLS)[:, None] + COLS * np.arange(SHARDS)[None, :]).reshape(-1)


def pack(unit, mixing_ref, shard, out_ref):
    def piece(l, r):
        return unit[ROWS * l : ROWS * (l + 1), SHARDS * r : SHARDS * (r + 1)]

    for l in range(COLS):
        out_ref[:, l, :] = jnp.concatenate([piece(l, r) for r in range(8)], axis=0).T
    for q in range(3):
        chunk = [piece(3 * g + q, r) for g in range(4) for r in (8, 9)]
        out_ref[:, 12 + q, :] = jnp.concatenate(chunk, axis=0).T
    target = lax.broadcasted_iota(jnp.int32, (SHARDS, 128), 0)
    lane = lax.broadcasted_iota(jnp.int32, (SHARDS, 128), 1)
    weights = jnp.zeros((SHARDS, 128), F32)
    for i in range(OWN):
        channel = OWN * shard + i
        here = target == lax.rem(channel, SHARDS)
        first = BASIS * lax.div(channel, SHARDS)
        for b in range(BASIS):
            weights = jnp.where(here & (lane == first + b), mixing_ref[b, i], weights)
    out_ref[:, 15, :] = weights


def pack_kernel(place_ref, mixing_ref, unit_ref, arrived_ref, block_ref):
    pack(unit_ref[...] + arrived_ref[...], mixing_ref, place_ref[0], block_ref)


def along_x(place_ref, m):
    return lax.rem(place_ref[4] + m, 4)


def along_y(place_ref, m):
    upper, right = place_ref[2], place_ref[3]
    return 2 * (1 - upper if m & 2 else upper) + (1 - right if m & 1 else right)


def low_high(rows):
    low = jnp.concatenate([rows[40 * z : 40 * z + 20] for z in range(4)], axis=0)
    high = jnp.concatenate([rows[40 * z + 20 : 40 * z + 40] for z in range(4)], axis=0)
    return low, high


def mlp_kernel(
    place_ref,
    act_ref,
    act_other_ref,
    cot_ref,
    cot_other_ref,
    in_ref,
    out_ref,
    own_ref,
    other_ref,
    *refs,
):
    outs, kept_ref = refs[:4], refs[4]
    core = place_ref[1]
    points = act_ref.shape[0]
    act = split(jnp.concatenate([act_ref[...], act_other_ref[...]], axis=0))
    cot = split(jnp.concatenate([cot_ref[...], cot_other_ref[...]], axis=0))
    w_in = split(in_ref[...].reshape(640, 640))
    w_out = split(out_ref[...].reshape(640, 640))
    preact = dot3(act, w_in, ((1,), (1,)))
    cdf = 0.5 * (1.0 + lax.erf(preact * (1.0 / math.sqrt(2.0))))
    density = jnp.exp(-0.5 * preact * preact) * (1.0 / math.sqrt(2.0 * math.pi))
    hidden = split(preact * cdf)
    slope = cdf + preact * density
    grad = split(dot3(cot, w_out, ((1,), (1,))) * slope)
    term = dot3(grad, w_in, ((1,), (0,)))
    own_ref[...] = cot_ref[...] + term[0:points]
    other_ref[...] = term[points:]
    contract = ((0,), (0,))
    first = dot3(grad, act, contract)
    second = dot3(hidden, cot, contract)

    @pl.when(core == 0)
    def _():
        for x in range(4):
            rows = slice(160 * x, 160 * x + 160)
            kept_ref[x, :, 0:640] = first[rows]
            kept_ref[x, :, 640:1280] = second[rows]

    @pl.when(core == 1)
    def _():
        for x in range(4):
            rows = slice(160 * x, 160 * x + 160)
            row, lane = 80 * (x % 2), 640 * (x // 2)
            parts = zip(low_high(first[rows]), low_high(second[rows]))
            for right, (a, b) in enumerate(parts):
                for upper in range(2):
                    cols = slice(320 * upper, 320 * upper + 320)
                    piece = jnp.concatenate([a[:, cols], b[:, cols]], axis=1)
                    kept_ref[2 * upper + right, row : row + 80, lane : lane + 640] = piece

    for m in range(4):
        index = jnp.where(core == 0, along_x(place_ref, m), along_y(place_ref, m))
        outs[m][...] = kept_ref[index]


def mlp(place, act, act_other, cot, cot_other, weight_in, weight_out):
    points, width = act.shape
    units = weight_in.shape[0]
    full = lambda shape: pl.BlockSpec(shape, lambda i, place: (0,) * len(shape))
    rows = pl.BlockSpec((4, None, 160, width), lambda i, place: (0, place[1], 0, 0))
    return pl.pallas_call(
        mlp_kernel,
        grid_spec=pltpu.PrefetchScalarGridSpec(
            num_scalar_prefetch=1,
            grid=(1,),
            in_specs=[full((points, width))] * 4 + [rows, rows],
            out_specs=[full((points, width))] * 2 + [full((160, 1280))] * 4,
            scratch_shapes=[pltpu.VMEM((4, 160, 1280), F32)],
        ),
        out_shape=[jax.ShapeDtypeStruct((points, width), F32)] * 2
        + [jax.ShapeDtypeStruct((160, 1280), F32)] * 4,
        compiler_params=params(57),
        cost_estimate=cost(30 * points * width * units, 12_000_000),
        name="mlp",
    )(
        place,
        act,
        act_other,
        cot,
        cot_other,
        weight_in.reshape(4, 2, 160, width),
        weight_out.reshape(4, 2, 160, width),
    )


def swap_kernel(place_ref, *refs):
    ins, outs, kept_ref = refs[:4], refs[4:8], refs[8]
    core = place_ref[1]
    total = (ins[0][...] + ins[1][...]) + (ins[2][...] + ins[3][...])

    @pl.when(core == 0)
    def _():
        for right, part in enumerate(low_high(total)):
            for upper in range(2):
                at = 320 * upper
                pair = [part[:, at : at + 320], part[:, 640 + at : 960 + at]]
                kept_ref[2 * upper + right] = jnp.concatenate(pair, axis=1)

    @pl.when(core == 1)
    def _():
        for x in range(4):
            row, col = 80 * (x % 2), 640 * (x // 2)
            kept_ref[x] = total[row : row + 80, col : col + 640]

    for m in range(4):
        index = jnp.where(core == 0, along_y(place_ref, m), along_x(place_ref, m))
        outs[m][...] = kept_ref[index]


def pair_kernel(place_ref, _, *refs):
    ins, (mine_ref, send_ref) = refs[:4], refs[4:]
    total = (ins[0][...] + ins[1][...]) + (ins[2][...] + ins[3][...])
    even = jnp.concatenate([total[:, 0:160], total[:, 320:480]], axis=1)
    odd = jnp.concatenate([total[:, 160:320], total[:, 480:640]], axis=1)
    first = place_ref[1] == 0
    mine_ref[...] = jnp.where(first, even, odd)
    send_ref[...] = jnp.where(first, odd, even)


def stack_kernel(place_ref, mine_ref, arrived_ref, *refs):
    outs, kept_ref = refs[:8], refs[8]
    first = place_ref[1] == 0
    mine, arrived = mine_ref[...], arrived_ref[...]
    below, above = jnp.where(first, mine, arrived), jnp.where(first, arrived, mine)
    for z in range(4):
        kept_ref[z, 0:20, :] = below[20 * z : 20 * z + 20]
        kept_ref[4 + z, 0:20, :] = above[20 * z : 20 * z + 20]
    for m in range(8):
        outs[m][...] = kept_ref[lax.rem(place_ref[5] + m, 8), 0:20, :]


def last_kernel(*refs):
    first_ref, second_ref = refs[8:]
    a, b, c, d = (refs[m][...] + refs[m + 4][...] for m in range(4))
    total = (a + b) + (c + d)
    first_ref[...] = total[:, 0:160]
    second_ref[...] = total[:, 160:320]


def small(kernel, operands, shapes, scalars=0, scratch=(), earlier=(), name=None, flops=0):
    return pl.pallas_call(
        kernel,
        in_specs=[pl.BlockSpec(memory_space=pltpu.SMEM)] * scalars
        + EARLIER * len(earlier)
        + whole(len(operands) - scalars),
        out_specs=whole(len(shapes)),
        out_shape=[jax.ShapeDtypeStruct(shape, F32) for shape in shapes],
        scratch_shapes=scratch,
        compiler_params=params(32),
        cost_estimate=cost(flops, 4_000_000) if flops else None,
        name=name,
    )(*operands[:scalars], *earlier, *operands[scalars:])


def permute(value, target):
    sizes = (2, 2, 4, 8, 2)
    order = lambda at: int(np.ravel_multi_index(at, sizes))
    pairs = [(order(at), order(target(*at))) for at in np.ndindex(*sizes)]
    return lax.ppermute(value, AXES, pairs)


def exchange(pieces, cores):
    def target(m, yl, co, x, z, yh):
        if cores[co] == "x":
            x = (x + m) % 4
        else:
            yl, yh = yl ^ (m >> 1), yh ^ (m & 1)
        return yl, co, x, z, yh

    return [pieces[0]] + [permute(pieces[m], functools.partial(target, m)) for m in (1, 2, 3)]


def exchange_z(pieces):
    order = (4, 1, 3, 5, 2, 6, 7)
    return [pieces[0]] + [
        lax.ppermute(pieces[m], "z", [(z, (z + m) % 8) for z in range(8)]) for m in order
    ]


def to_core(value):
    return lax.ppermute(value, "co", [(0, 1), (1, 0)])


def spectrum_kernel(
    block_ref, top_ref, low_ref, _, out_ref, first_ref, final_ref, mixing_ref, flat_ref
):
    for p in range(COLS // 2):
        pair = jnp.concatenate([block_ref[:, 2 * p, :], block_ref[:, 2 * p + 1, :]], axis=0)
        flat_ref[0:128, 128 * p : 128 * (p + 1)] = pair.T
    rest = [block_ref[:, 12 + q, :].T for q in range(3)]
    pieces = [rest[q][32 * g : 32 * (g + 1), :] for g in range(4) for q in range(3)]
    flat_ref[128:160, :] = jnp.concatenate(pieces, axis=1)
    result = dot3(split(flat_ref[...]), (top_ref[...], low_ref[...]), ((1,), (0,)))
    out_ref[...] = result
    mixing_ref[...] = jnp.sum(block_ref[:, 15, :], axis=0, keepdims=True)
    for r in range(OWN):
        first_ref[3 * r : 3 * r + 3, :] = result[ROWS * r : ROWS * r + 3, :]
        final_ref[3 * r : 3 * r + 3, :] = result[ROWS * r + 13 : ROWS * r + 16, :]


def spectrum(block, earlier):
    top, low = forward_table(shard_order())
    rows = OWN * ROWS
    return pl.pallas_call(
        spectrum_kernel,
        in_specs=whole(3) + EARLIER,
        out_specs=whole(4),
        out_shape=[
            jax.ShapeDtypeStruct((rows, CIRCLE), F32),
            jax.ShapeDtypeStruct((3 * OWN, CIRCLE), F32),
            jax.ShapeDtypeStruct((3 * OWN, CIRCLE), F32),
            jax.ShapeDtypeStruct((1, 128), F32),
        ],
        scratch_shapes=[pltpu.VMEM((rows, CIRCLE), F32)],
        compiler_params=params(24),
        cost_estimate=cost(6 * rows * CIRCLE * CIRCLE, 4_000_000),
        name="spectrum",
    )(block, jnp.asarray(top), jnp.asarray(low), earlier)


def kernel_spectrum_kernel(kernel_ref, top_ref, low_ref, _, out_ref):
    out_ref[...] = dot3(split(kernel_ref[...]), (top_ref[...], low_ref[...]), ((1,), (0,)))


def kernel_spectrum(kernels, earlier):
    top, low = forward_table(np.arange(CIRCLE))
    rows = BASIS * TAPS * ROWS
    flat = kernels.transpose(0, 2, 1, 3).reshape(rows, CIRCLE)
    return pl.pallas_call(
        kernel_spectrum_kernel,
        in_specs=whole(3) + EARLIER,
        out_specs=whole(1)[0],
        out_shape=jax.ShapeDtypeStruct((rows, CIRCLE), F32),
        compiler_params=params(24),
        cost_estimate=cost(6 * rows * CIRCLE * CIRCLE, 5_000_000),
        name="kernel_spectrum",
    )(flat, jnp.asarray(top), jnp.asarray(low), earlier)


def filter_kernel(
    mixing_ref, data_ref, before_ref, after_ref, kernel_ref, top_ref, low_ref, *refs
):
    out_ref, rows_ref, sum_ref = refs[-3:]
    for r in range(OWN):
        rows_ref[r, 0:3, :] = before_ref[3 * r : 3 * r + 3, :]
        rows_ref[r, 3 : 3 + ROWS, :] = data_ref[ROWS * r : ROWS * (r + 1), :]
        rows_ref[r, 3 + ROWS : 6 + ROWS, :] = after_ref[3 * r : 3 * r + 3, :]
    lane = lax.broadcasted_iota(jnp.int32, (ROWS, HALF), 1)
    ends = lane == 0

    def channel(r, carry):
        real = jnp.zeros((ROWS, HALF), F32)
        imag = jnp.zeros((ROWS, HALF), F32)
        for k in range(TAPS):
            mixed_real = jnp.zeros((ROWS, HALF), F32)
            mixed_imag = jnp.zeros((ROWS, HALF), F32)
            for b in range(BASIS):
                weight = mixing_ref[0, BASIS * r + b]
                at = ROWS * (TAPS * b + k)
                mixed_real += weight * kernel_ref[at : at + ROWS, 0:HALF]
                mixed_imag += weight * kernel_ref[at : at + ROWS, HALF:CIRCLE]
            own = jnp.where(ends, mixed_imag, mixed_real)
            cross = jnp.where(ends, 0.0, mixed_imag)
            data_real = rows_ref[r, 6 - k : 6 - k + ROWS, 0:HALF]
            data_imag = rows_ref[r, 6 - k : 6 - k + ROWS, HALF:CIRCLE]
            real += mixed_real * data_real + cross * data_imag
            imag += own * data_imag - cross * data_real
        sum_ref[r, :, 0:HALF] = real
        sum_ref[r, :, HALF:CIRCLE] = imag
        return carry

    lax.fori_loop(0, OWN, channel, 0)
    total = split(sum_ref[...].reshape(OWN * ROWS, CIRCLE))
    field = dot3((top_ref[...], low_ref[...]), total, ((1,), (1,)))
    for l in range(COLS):
        out_ref[:, l, :] = field[SHARDS * l : SHARDS * (l + 1), 0:128]
    for q in range(3):
        pieces = [
            field[SHARDS * (3 * g + q) : SHARDS * (3 * g + q + 1), 128:160] for g in range(4)
        ]
        out_ref[:, 12 + q, :] = jnp.concatenate(pieces, axis=1)
    out_ref[:, 15, :] = jnp.zeros((SHARDS, 128), F32)


def filtered(mixing, data, before, beyond, kernel, earlier):
    top, low = backward_table(shard_order())
    return pl.pallas_call(
        filter_kernel,
        in_specs=[pl.BlockSpec(memory_space=pltpu.SMEM)] + whole(6) + EARLIER * len(earlier),
        out_specs=whole(1)[0],
        out_shape=jax.ShapeDtypeStruct((SHARDS, 16, 128), F32),
        scratch_shapes=[
            pltpu.VMEM((OWN, 24, CIRCLE), F32),
            pltpu.VMEM((OWN, ROWS, CIRCLE), F32),
        ],
        compiler_params=params(32),
        cost_estimate=cost(6 * OWN * ROWS * CIRCLE * CIRCLE, 5_000_000),
        name="filter",
    )(mixing, data, before, beyond, kernel, jnp.asarray(top), jnp.asarray(low), *earlier)


def unpack_kernel(block_ref, out_ref):
    def put(l, r, pair):
        out_ref[ROWS * l : ROWS * (l + 1), SHARDS * r : SHARDS * (r + 2)] = jnp.concatenate(
            pair, axis=1
        )

    for l in range(COLS):
        turned = block_ref[:, l, :].T
        for r in range(0, 8, 2):
            put(l, r, [turned[ROWS * r : ROWS * (r + 1)], turned[ROWS * (r + 1) : ROWS * (r + 2)]])
    for q in range(3):
        turned = block_ref[:, 12 + q, :].T
        for g in range(4):
            at = 32 * g
            put(3 * g + q, 8, [turned[at : at + ROWS], turned[at + ROWS : at + 2 * ROWS]])


def unpack(block):
    return pl.pallas_call(
        unpack_kernel,
        in_specs=whole(1),
        out_specs=whole(1)[0],
        out_shape=jax.ShapeDtypeStruct((ROWS * COLS, SHARDS * OWN), F32),
        compiler_params=params(16),
        name="unpack",
    )(block)


def across(block):
    return lax.all_to_all(block, LON, split_axis=0, concat_axis=0, tiled=True)


def per_device(activation, cotangent, weight_in, weight_out, kernels, mixing):
    points = ROWS * COLS
    width = activation.shape[2]
    act = activation.transpose(1, 0, 2).reshape(points, width)
    cot = cotangent.transpose(1, 0, 2).reshape(points, width)
    place = jnp.stack([lax.axis_index(axis) for axis in (LON, "co", "yl", "yh", "x", "z")])
    unit, other, *pieces = mlp(place, act, to_core(act), cot, to_core(cot), weight_in, weight_out)
    operands = (place, mixing.T, unit, to_core(other))
    (block,) = small(pack_kernel, operands, [(SHARDS, 16, 128)], 2, name="pack")
    moved = exchange(pieces, "xy")
    spread = across(block)
    kept = (pltpu.VMEM((4, 80, 640), F32),)
    swapped = small(swap_kernel, (place, *moved), [(80, 640)] * 4, 1, kept, (), "swap", 10**10)
    kernel = kernel_spectrum(kernels, swapped[0])
    moved = exchange(swapped, "yx")
    mine, send = small(
        pair_kernel, (place, *moved), [(80, 320)] * 2, 1, (), (kernel,), "pair"
    )
    data, first, final, own_mixing = spectrum(spread, kernel)
    forward = [(i, i + 1) for i in range(3)]
    backward = [(target, source) for source, target in forward]
    before = lax.ppermute(final, LAT, forward)
    beyond = lax.ppermute(first, LAT, backward)
    paired = to_core(send)
    kept = (pltpu.VMEM((8, 24, 320), F32),)
    operands = (place, mine, paired)
    stacked = small(stack_kernel, operands, [(20, 320)] * 8, 1, kept, name="stack")
    moved = exchange_z(stacked)
    sent = filtered(own_mixing, data, before, beyond, kernel, moved[1:3])
    result = across(sent)
    grad_in, grad_out = small(last_kernel, moved, [(20, 160)] * 2, name="last")
    field = unpack(result).reshape(COLS, ROWS, width).transpose(1, 0, 2)
    return (field, grad_in, grad_out)


def solution(mesh):
    fine = Mesh(mesh.devices.reshape(2, 2, 4, 8, 2), AXES)
    placed = (
        P(LAT, LON, None),
        P(LAT, LON, None),
        P(),
        P(),
        P(None, LAT, None, None),
        P(LON, None),
    )
    return jax.shard_map(
        per_device,
        mesh=fine,
        in_specs=placed,
        out_specs=(P(LAT, LON, None), P(LON, LAT), P(LON, LAT)),
        check_vma=False,
    )
```

```python
import functools
import math

import jax
import jax.numpy as jnp
import ml_dtypes
import numpy as np
from jax import lax
from jax.experimental import pallas as pl
from jax.experimental.pallas import tpu as pltpu
from jax.sharding import Mesh
from jax.sharding import PartitionSpec as P

AXES = ("yl", "co", "x", "z", "yh")
LAT = ("yl", "co")
LON = ("x", "z", "yh")
F32 = jnp.float32
BF16 = jnp.bfloat16
SHARDS = 64
COLS = 12
ROWS = 16
OWN = 10
CIRCLE = 768
HALF = 384
TAPS = 7
BASIS = 3
MIB = 1 << 20


def split(value):
    top = value.astype(BF16)
    return top, (value - top.astype(F32)).astype(BF16)


def dot3(left, right, dims):
    (a, b), (c, d) = left, right
    (at,), (to,) = dims
    return lax.dot_general(
        jnp.concatenate([a, b, a], axis=at),
        jnp.concatenate([c, c, d], axis=to),
        dimension_numbers=(dims, ((), ())),
        preferred_element_type=F32,
    )


def whole(n):
    return [pl.BlockSpec(memory_space=pltpu.VMEM)] * n


EARLIER = [pl.BlockSpec(memory_space=pl.ANY)]


def params(mib):
    return pltpu.CompilerParams(vmem_limit_bytes=mib * MIB)


def cost(flops, moved):
    return pl.CostEstimate(flops=flops, bytes_accessed=moved, transcendentals=0)


def table(order):
    angle = 2.0 * np.pi / CIRCLE * (order[:, None] * np.arange(HALF)[None, :] % CIRCLE)
    nyquist = np.where(order % 2 == 0, 1.0, -1.0)
    real, imag = np.cos(angle), -np.sin(angle)
    imag[:, 0] = nyquist
    return np.concatenate([real, imag], axis=1)


def parts(matrix):
    exact = matrix.astype(np.float32)
    top = exact.astype(ml_dtypes.bfloat16)
    return top, (exact - top.astype(np.float32)).astype(ml_dtypes.bfloat16)


def forward_table(order):
    return parts(table(order))


def backward_table(order):
    weight = np.full((2, HALF), 2.0 / CIRCLE)
    weight[:, 0] = 1.0 / CIRCLE
    return parts(table(order) * weight.reshape(1, -1))


def shard_order():
    return (np.arange(COLS)[:, None] + COLS * np.arange(SHARDS)[None, :]).reshape(-1)


def pack(unit, mixing_ref, shard, out_ref):
    def piece(l, r):
        return unit[ROWS * l : ROWS * (l + 1), SHARDS * r : SHARDS * (r + 1)]

    for l in range(COLS):
        out_ref[:, l, :] = jnp.concatenate([piece(l, r) for r in range(8)], axis=0).T
    for q in range(3):
        chunk = [piece(3 * g + q, r) for g in range(4) for r in (8, 9)]
        out_ref[:, 12 + q, :] = jnp.concatenate(chunk, axis=0).T
    target = lax.broadcasted_iota(jnp.int32, (SHARDS, 128), 0)
    lane = lax.broadcasted_iota(jnp.int32, (SHARDS, 128), 1)
    weights = jnp.zeros((SHARDS, 128), F32)
    for i in range(OWN):
        channel = OWN * shard + i
        here = target == lax.rem(channel, SHARDS)
        first = BASIS * lax.div(channel, SHARDS)
        for b in range(BASIS):
            weights = jnp.where(here & (lane == first + b), mixing_ref[b, i], weights)
    out_ref[:, 15, :] = weights


def pack_kernel(place_ref, mixing_ref, unit_ref, arrived_ref, block_ref):
    pack(unit_ref[...] + arrived_ref[...], mixing_ref, place_ref[0], block_ref)


def along_x(place_ref, m):
    return lax.rem(place_ref[4] + m, 4)


def along_y(place_ref, m):
    upper, right = place_ref[2], place_ref[3]
    return 2 * (1 - upper if m & 2 else upper) + (1 - right if m & 1 else right)


def low_high(rows):
    low = jnp.concatenate([rows[40 * z : 40 * z + 20] for z in range(4)], axis=0)
    high = jnp.concatenate([rows[40 * z + 20 : 40 * z + 40] for z in range(4)], axis=0)
    return low, high


def mlp_kernel(
    place_ref,
    act_ref,
    act_other_ref,
    cot_ref,
    cot_other_ref,
    in_ref,
    out_ref,
    own_ref,
    other_ref,
    *refs,
):
    outs, kept_ref = refs[:4], refs[4]
    core = place_ref[1]
    points = act_ref.shape[0]
    act = split(jnp.concatenate([act_ref[...], act_other_ref[...]], axis=0))
    cot = split(jnp.concatenate([cot_ref[...], cot_other_ref[...]], axis=0))
    w_in = split(in_ref[...].reshape(640, 640))
    w_out = split(out_ref[...].reshape(640, 640))
    preact = dot3(act, w_in, ((1,), (1,)))
    cdf = 0.5 * (1.0 + lax.erf(preact * (1.0 / math.sqrt(2.0))))
    density = jnp.exp(-0.5 * preact * preact) * (1.0 / math.sqrt(2.0 * math.pi))
    hidden = split(preact * cdf)
    slope = cdf + preact * density
    grad = split(dot3(cot, w_out, ((1,), (1,))) * slope)
    term = dot3(grad, w_in, ((1,), (0,)))
    own_ref[...] = cot_ref[...] + term[0:points]
    other_ref[...] = term[points:]
    contract = ((0,), (0,))
    first = dot3(grad, act, contract)
    second = dot3(hidden, cot, contract)

    @pl.when(core == 0)
    def _():
        for x in range(4):
            rows = slice(160 * x, 160 * x + 160)
            kept_ref[x, :, 0:640] = first[rows]
            kept_ref[x, :, 640:1280] = second[rows]

    @pl.when(core == 1)
    def _():
        for x in range(4):
            rows = slice(160 * x, 160 * x + 160)
            row, lane = 80 * (x % 2), 640 * (x // 2)
            parts = zip(low_high(first[rows]), low_high(second[rows]))
            for right, (a, b) in enumerate(parts):
                for upper in range(2):
                    cols = slice(320 * upper, 320 * upper + 320)
                    piece = jnp.concatenate([a[:, cols], b[:, cols]], axis=1)
                    kept_ref[2 * upper + right, row : row + 80, lane : lane + 640] = piece

    for m in range(4):
        index = jnp.where(core == 0, along_x(place_ref, m), along_y(place_ref, m))
        outs[m][...] = kept_ref[index]


def mlp(place, act, act_other, cot, cot_other, weight_in, weight_out):
    points, width = act.shape
    units = weight_in.shape[0]
    full = lambda shape: pl.BlockSpec(shape, lambda i, place: (0,) * len(shape))
    rows = pl.BlockSpec((4, None, 160, width), lambda i, place: (0, place[1], 0, 0))
    return pl.pallas_call(
        mlp_kernel,
        grid_spec=pltpu.PrefetchScalarGridSpec(
            num_scalar_prefetch=1,
            grid=(1,),
            in_specs=[full((points, width))] * 4 + [rows, rows],
            out_specs=[full((points, width))] * 2 + [full((160, 1280))] * 4,
            scratch_shapes=[pltpu.VMEM((4, 160, 1280), F32)],
        ),
        out_shape=[jax.ShapeDtypeStruct((points, width), F32)] * 2
        + [jax.ShapeDtypeStruct((160, 1280), F32)] * 4,
        compiler_params=params(57),
        cost_estimate=cost(30 * points * width * units, 12_000_000),
        name="mlp",
    )(
        place,
        act,
        act_other,
        cot,
        cot_other,
        weight_in.reshape(4, 2, 160, width),
        weight_out.reshape(4, 2, 160, width),
    )


def swap_kernel(place_ref, *refs):
    ins, outs, kept_ref = refs[:4], refs[4:8], refs[8]
    core = place_ref[1]
    total = (ins[0][...] + ins[1][...]) + (ins[2][...] + ins[3][...])

    @pl.when(core == 0)
    def _():
        for right, part in enumerate(low_high(total)):
            for upper in range(2):
                at = 320 * upper
                pair = [part[:, at : at + 320], part[:, 640 + at : 960 + at]]
                kept_ref[2 * upper + right] = jnp.concatenate(pair, axis=1)

    @pl.when(core == 1)
    def _():
        for x in range(4):
            row, col = 80 * (x % 2), 640 * (x // 2)
            kept_ref[x] = total[row : row + 80, col : col + 640]

    for m in range(4):
        index = jnp.where(core == 0, along_y(place_ref, m), along_x(place_ref, m))
        outs[m][...] = kept_ref[index]


def pair_kernel(place_ref, _, *refs):
    ins, (mine_ref, send_ref) = refs[:4], refs[4:]
    total = (ins[0][...] + ins[1][...]) + (ins[2][...] + ins[3][...])
    even = jnp.concatenate([total[:, 0:160], total[:, 320:480]], axis=1)
    odd = jnp.concatenate([total[:, 160:320], total[:, 480:640]], axis=1)
    first = place_ref[1] == 0
    mine_ref[...] = jnp.where(first, even, odd)
    send_ref[...] = jnp.where(first, odd, even)


def stack_kernel(place_ref, _, mine_ref, arrived_ref, *refs):
    outs, kept_ref = refs[:8], refs[8]
    first = place_ref[1] == 0
    mine, arrived = mine_ref[...], arrived_ref[...]
    below, above = jnp.where(first, mine, arrived), jnp.where(first, arrived, mine)
    for z in range(4):
        kept_ref[z, 0:20, :] = below[20 * z : 20 * z + 20]
        kept_ref[4 + z, 0:20, :] = above[20 * z : 20 * z + 20]
    for m in range(8):
        outs[m][...] = kept_ref[lax.rem(place_ref[5] + m, 8), 0:20, :]


def last_kernel(*refs):
    first_ref, second_ref = refs[8:]
    a, b, c, d = (refs[m][...] + refs[m + 4][...] for m in range(4))
    total = (a + b) + (c + d)
    first_ref[...] = total[:, 0:160]
    second_ref[...] = total[:, 160:320]


def small(kernel, operands, shapes, scalars=0, scratch=(), earlier=(), name=None, flops=0):
    return pl.pallas_call(
        kernel,
        in_specs=[pl.BlockSpec(memory_space=pltpu.SMEM)] * scalars
        + EARLIER * len(earlier)
        + whole(len(operands) - scalars),
        out_specs=whole(len(shapes)),
        out_shape=[jax.ShapeDtypeStruct(shape, F32) for shape in shapes],
        scratch_shapes=scratch,
        compiler_params=params(32),
        cost_estimate=cost(flops, 4_000_000) if flops else None,
        name=name,
    )(*operands[:scalars], *earlier, *operands[scalars:])


def permute(value, target):
    sizes = (2, 2, 4, 8, 2)
    order = lambda at: int(np.ravel_multi_index(at, sizes))
    pairs = [(order(at), order(target(*at))) for at in np.ndindex(*sizes)]
    return lax.ppermute(value, AXES, pairs)


def exchange(pieces, cores):
    def target(m, yl, co, x, z, yh):
        if cores[co] == "x":
            x = (x + m) % 4
        else:
            yl, yh = yl ^ (m >> 1), yh ^ (m & 1)
        return yl, co, x, z, yh

    return [pieces[0]] + [permute(pieces[m], functools.partial(target, m)) for m in (1, 2, 3)]


def exchange_z(pieces):
    far = (1, 7, 4, 3, 5, 2, 6)
    return [pieces[0]] + [
        lax.ppermute(pieces[m], "z", [(z, (z + m) % 8) for z in range(8)]) for m in far
    ]


def to_core(value):
    return lax.ppermute(value, "co", [(0, 1), (1, 0)])


def spectrum_kernel(
    place_ref, block_ref, top_ref, low_ref, _, out_ref, near_ref, cross_ref, mixing_ref, flat_ref
):
    for p in range(COLS // 2):
        pair = jnp.concatenate([block_ref[:, 2 * p, :], block_ref[:, 2 * p + 1, :]], axis=0)
        flat_ref[0:128, 128 * p : 128 * (p + 1)] = pair.T
    rest = [block_ref[:, 12 + q, :].T for q in range(3)]
    pieces = [rest[q][32 * g : 32 * (g + 1), :] for g in range(4) for q in range(3)]
    flat_ref[128:160, :] = jnp.concatenate(pieces, axis=1)
    result = dot3(split(flat_ref[...]), (top_ref[...], low_ref[...]), ((1,), (0,)))
    out_ref[...] = result
    mixing_ref[...] = jnp.sum(block_ref[:, 15, :], axis=0, keepdims=True)
    even = place_ref[1] == 0
    for r in range(OWN):
        first = result[ROWS * r : ROWS * r + 3, :]
        final = result[ROWS * r + 13 : ROWS * r + 16, :]
        near_ref[3 * r : 3 * r + 3, :] = jnp.where(even, final, first)
        cross_ref[3 * r : 3 * r + 3, :] = jnp.where(even, first, final)


def spectrum(place, block, earlier):
    top, low = forward_table(shard_order())
    rows = OWN * ROWS
    return pl.pallas_call(
        spectrum_kernel,
        in_specs=[pl.BlockSpec(memory_space=pltpu.SMEM)] + whole(3) + EARLIER,
        out_specs=whole(4),
        out_shape=[
            jax.ShapeDtypeStruct((rows, CIRCLE), F32),
            jax.ShapeDtypeStruct((3 * OWN, CIRCLE), F32),
            jax.ShapeDtypeStruct((3 * OWN, CIRCLE), F32),
            jax.ShapeDtypeStruct((1, 128), F32),
        ],
        scratch_shapes=[pltpu.VMEM((rows, CIRCLE), F32)],
        compiler_params=params(24),
        cost_estimate=cost(6 * rows * CIRCLE * CIRCLE, 4_000_000),
        name="spectrum",
    )(place, block, jnp.asarray(top), jnp.asarray(low), earlier)


def kernel_spectrum_kernel(kernel_ref, top_ref, low_ref, _, out_ref):
    out_ref[...] = dot3(split(kernel_ref[...]), (top_ref[...], low_ref[...]), ((1,), (0,)))


def kernel_spectrum(kernels, earlier):
    top, low = forward_table(np.arange(CIRCLE))
    rows = BASIS * TAPS * ROWS
    flat = kernels.transpose(0, 2, 1, 3).reshape(rows, CIRCLE)
    return pl.pallas_call(
        kernel_spectrum_kernel,
        in_specs=whole(3) + EARLIER,
        out_specs=whole(1)[0],
        out_shape=jax.ShapeDtypeStruct((rows, CIRCLE), F32),
        compiler_params=params(24),
        cost_estimate=cost(6 * rows * CIRCLE * CIRCLE, 5_000_000),
        name="kernel_spectrum",
    )(flat, jnp.asarray(top), jnp.asarray(low), earlier)


def filter_kernel(
    place_ref, mixing_ref, data_ref, near_ref, cross_ref, kernel_ref, top_ref, low_ref, *refs
):
    out_ref, rows_ref, sum_ref = refs[-3:]
    even = place_ref[1] == 0
    for r in range(OWN):
        near, cross = near_ref[3 * r : 3 * r + 3, :], cross_ref[3 * r : 3 * r + 3, :]
        rows_ref[r, 0:3, :] = jnp.where(even, cross, near)
        rows_ref[r, 3 : 3 + ROWS, :] = data_ref[ROWS * r : ROWS * (r + 1), :]
        rows_ref[r, 3 + ROWS : 6 + ROWS, :] = jnp.where(even, near, cross)
    lane = lax.broadcasted_iota(jnp.int32, (ROWS, HALF), 1)
    ends = lane == 0

    def channel(r, carry):
        real = jnp.zeros((ROWS, HALF), F32)
        imag = jnp.zeros((ROWS, HALF), F32)
        for k in range(TAPS):
            mixed_real = jnp.zeros((ROWS, HALF), F32)
            mixed_imag = jnp.zeros((ROWS, HALF), F32)
            for b in range(BASIS):
                weight = mixing_ref[0, BASIS * r + b]
                at = ROWS * (TAPS * b + k)
                mixed_real += weight * kernel_ref[at : at + ROWS, 0:HALF]
                mixed_imag += weight * kernel_ref[at : at + ROWS, HALF:CIRCLE]
            own = jnp.where(ends, mixed_imag, mixed_real)
            cross = jnp.where(ends, 0.0, mixed_imag)
            data_real = rows_ref[r, 6 - k : 6 - k + ROWS, 0:HALF]
            data_imag = rows_ref[r, 6 - k : 6 - k + ROWS, HALF:CIRCLE]
            real += mixed_real * data_real + cross * data_imag
            imag += own * data_imag - cross * data_real
        sum_ref[r, :, 0:HALF] = real
        sum_ref[r, :, HALF:CIRCLE] = imag
        return carry

    lax.fori_loop(0, OWN, channel, 0)
    total = split(sum_ref[...].reshape(OWN * ROWS, CIRCLE))
    field = dot3((top_ref[...], low_ref[...]), total, ((1,), (1,)))
    for l in range(COLS):
        out_ref[:, l, :] = field[SHARDS * l : SHARDS * (l + 1), 0:128]
    for q in range(3):
        pieces = [
            field[SHARDS * (3 * g + q) : SHARDS * (3 * g + q + 1), 128:160] for g in range(4)
        ]
        out_ref[:, 12 + q, :] = jnp.concatenate(pieces, axis=1)
    out_ref[:, 15, :] = jnp.zeros((SHARDS, 128), F32)


def filtered(place, mixing, data, near, cross, kernel, earlier):
    top, low = backward_table(shard_order())
    return pl.pallas_call(
        filter_kernel,
        in_specs=[pl.BlockSpec(memory_space=pltpu.SMEM)] * 2 + whole(6) + EARLIER,
        out_specs=whole(1)[0],
        out_shape=jax.ShapeDtypeStruct((SHARDS, 16, 128), F32),
        scratch_shapes=[
            pltpu.VMEM((OWN, 24, CIRCLE), F32),
            pltpu.VMEM((OWN, ROWS, CIRCLE), F32),
        ],
        compiler_params=params(32),
        cost_estimate=cost(6 * OWN * ROWS * CIRCLE * CIRCLE, 5_000_000),
        name="filter",
    )(place, mixing, data, near, cross, kernel, jnp.asarray(top), jnp.asarray(low), earlier)


def unpack_kernel(block_ref, out_ref):
    def put(l, r, pair):
        out_ref[ROWS * l : ROWS * (l + 1), SHARDS * r : SHARDS * (r + 2)] = jnp.concatenate(
            pair, axis=1
        )

    for l in range(COLS):
        turned = block_ref[:, l, :].T
        for r in range(0, 8, 2):
            put(l, r, [turned[ROWS * r : ROWS * (r + 1)], turned[ROWS * (r + 1) : ROWS * (r + 2)]])
    for q in range(3):
        turned = block_ref[:, 12 + q, :].T
        for g in range(4):
            at = 32 * g
            put(3 * g + q, 8, [turned[at : at + ROWS], turned[at + ROWS : at + 2 * ROWS]])


def unpack(block):
    return pl.pallas_call(
        unpack_kernel,
        in_specs=whole(1),
        out_specs=whole(1)[0],
        out_shape=jax.ShapeDtypeStruct((ROWS * COLS, SHARDS * OWN), F32),
        compiler_params=params(16),
        name="unpack",
    )(block)


def across(block):
    return lax.all_to_all(block, LON, split_axis=0, concat_axis=0, tiled=True)


def per_device(activation, cotangent, weight_in, weight_out, kernels, mixing):
    points = ROWS * COLS
    width = activation.shape[2]
    act = activation.transpose(1, 0, 2).reshape(points, width)
    cot = cotangent.transpose(1, 0, 2).reshape(points, width)
    place = jnp.stack([lax.axis_index(axis) for axis in (LON, "co", "yl", "yh", "x", "z")])
    unit, other, *pieces = mlp(place, act, to_core(act), cot, to_core(cot), weight_in, weight_out)
    operands = (place, mixing.T, unit, to_core(other))
    (block,) = small(pack_kernel, operands, [(SHARDS, 16, 128)], 2, name="pack")
    moved = exchange(pieces, "xy")
    spread = across(block)
    kept = (pltpu.VMEM((4, 80, 640), F32),)
    swapped = small(swap_kernel, (place, *moved), [(80, 640)] * 4, 1, kept, (), "swap", 10**10)
    kernel = kernel_spectrum(kernels, swapped[0])
    moved = exchange(swapped, "yx")
    data, near, cross, own_mixing = spectrum(place, spread, kernel)
    near = to_core(near)
    cross = lax.ppermute(cross, LAT, [(1, 2), (2, 1)])
    mine, send = small(pair_kernel, (place, *moved), [(80, 320)] * 2, 1, (), (data,), "pair")
    paired = to_core(send)
    sent = filtered(place, own_mixing, data, near, cross, kernel, paired)
    result = across(sent)
    kept = (pltpu.VMEM((8, 24, 320), F32),)
    operands = (place, mine, paired)
    stacked = small(stack_kernel, operands, [(20, 320)] * 8, 1, kept, (sent,), "stack")
    grad_in, grad_out = small(last_kernel, exchange_z(stacked), [(20, 160)] * 2, name="last")
    field = unpack(result).reshape(COLS, ROWS, width).transpose(1, 0, 2)
    return (field, grad_in, grad_out)


def solution(mesh):
    fine = Mesh(mesh.devices.reshape(2, 2, 4, 8, 2), AXES)
    placed = (
        P(LAT, LON, None),
        P(LAT, LON, None),
        P(),
        P(),
        P(None, LAT, None, None),
        P(LON, None),
    )
    return jax.shard_map(
        per_device,
        mesh=fine,
        in_specs=placed,
        out_specs=(P(LAT, LON, None), P(LON, LAT), P(LON, LAT)),
        check_vma=False,
    )
```

```python
import functools
import math

import jax
import jax.numpy as jnp
import ml_dtypes
import numpy as np
from jax import lax
from jax.experimental import pallas as pl
from jax.experimental.pallas import tpu as pltpu
from jax.sharding import Mesh
from jax.sharding import PartitionSpec as P

AXES = ("yl", "co", "x", "z", "yh")
LAT = ("yl", "co")
LON = ("x", "z", "yh")
F32 = jnp.float32
BF16 = jnp.bfloat16
SHARDS = 64
COLS = 12
ROWS = 16
OWN = 10
CIRCLE = 768
HALF = 384
TAPS = 7
BASIS = 3
MIB = 1 << 20


def split(value):
    top = value.astype(BF16)
    return top, (value - top.astype(F32)).astype(BF16)


def dot3(left, right, dims):
    (a, b), (c, d) = left, right
    (at,), (to,) = dims
    return lax.dot_general(
        jnp.concatenate([a, b, a], axis=at),
        jnp.concatenate([c, c, d], axis=to),
        dimension_numbers=(dims, ((), ())),
        preferred_element_type=F32,
    )


def whole(n):
    return [pl.BlockSpec(memory_space=pltpu.VMEM)] * n


EARLIER = [pl.BlockSpec(memory_space=pl.ANY)]


def params(mib):
    return pltpu.CompilerParams(vmem_limit_bytes=mib * MIB)


def cost(flops, moved):
    return pl.CostEstimate(flops=flops, bytes_accessed=moved, transcendentals=0)


def table(order):
    angle = 2.0 * np.pi / CIRCLE * (order[:, None] * np.arange(HALF)[None, :] % CIRCLE)
    nyquist = np.where(order % 2 == 0, 1.0, -1.0)
    real, imag = np.cos(angle), -np.sin(angle)
    imag[:, 0] = nyquist
    return np.concatenate([real, imag], axis=1)


def parts(matrix):
    exact = matrix.astype(np.float32)
    top = exact.astype(ml_dtypes.bfloat16)
    return top, (exact - top.astype(np.float32)).astype(ml_dtypes.bfloat16)


def forward_table(order):
    return parts(table(order))


def backward_table(order):
    weight = np.full((2, HALF), 2.0 / CIRCLE)
    weight[:, 0] = 1.0 / CIRCLE
    return parts(table(order) * weight.reshape(1, -1))


def shard_order():
    return (np.arange(COLS)[:, None] + COLS * np.arange(SHARDS)[None, :]).reshape(-1)


def pack(unit, mixing_ref, shard, out_ref):
    def piece(l, r):
        return unit[ROWS * l : ROWS * (l + 1), SHARDS * r : SHARDS * (r + 1)]

    for l in range(COLS):
        out_ref[:, l, :] = jnp.concatenate([piece(l, r) for r in range(8)], axis=0).T
    for q in range(3):
        chunk = [piece(3 * g + q, r) for g in range(4) for r in (8, 9)]
        out_ref[:, 12 + q, :] = jnp.concatenate(chunk, axis=0).T
    target = lax.broadcasted_iota(jnp.int32, (SHARDS, 128), 0)
    lane = lax.broadcasted_iota(jnp.int32, (SHARDS, 128), 1)
    weights = jnp.zeros((SHARDS, 128), F32)
    for i in range(OWN):
        channel = OWN * shard + i
        here = target == lax.rem(channel, SHARDS)
        first = BASIS * lax.div(channel, SHARDS)
        for b in range(BASIS):
            weights = jnp.where(here & (lane == first + b), mixing_ref[b, i], weights)
    out_ref[:, 15, :] = weights


def pack_kernel(place_ref, mixing_ref, unit_ref, arrived_ref, block_ref):
    pack(unit_ref[...] + arrived_ref[...], mixing_ref, place_ref[0], block_ref)


def along_x(place_ref, m):
    return lax.rem(place_ref[4] + m, 4)


def along_y(place_ref, m):
    upper, right = place_ref[2], place_ref[3]
    return 2 * (1 - upper if m & 2 else upper) + (1 - right if m & 1 else right)


def low_high(rows):
    low = jnp.concatenate([rows[40 * z : 40 * z + 20] for z in range(4)], axis=0)
    high = jnp.concatenate([rows[40 * z + 20 : 40 * z + 40] for z in range(4)], axis=0)
    return low, high


def mlp_kernel(
    place_ref,
    act_ref,
    act_other_ref,
    cot_ref,
    cot_other_ref,
    in_ref,
    out_ref,
    own_ref,
    other_ref,
    *refs,
):
    outs, kept_ref = refs[:4], refs[4]
    core = place_ref[1]
    points = act_ref.shape[0]
    act = split(jnp.concatenate([act_ref[...], act_other_ref[...]], axis=0))
    cot = split(jnp.concatenate([cot_ref[...], cot_other_ref[...]], axis=0))
    w_in = split(in_ref[...].reshape(640, 640))
    w_out = split(out_ref[...].reshape(640, 640))
    preact = dot3(act, w_in, ((1,), (1,)))
    cdf = 0.5 * (1.0 + lax.erf(preact * (1.0 / math.sqrt(2.0))))
    density = jnp.exp(-0.5 * preact * preact) * (1.0 / math.sqrt(2.0 * math.pi))
    hidden = split(preact * cdf)
    slope = cdf + preact * density
    grad = split(dot3(cot, w_out, ((1,), (1,))) * slope)
    term = dot3(grad, w_in, ((1,), (0,)))
    own_ref[...] = cot_ref[...] + term[0:points]
    other_ref[...] = term[points:]
    contract = ((0,), (0,))
    first = dot3(grad, act, contract)
    second = dot3(hidden, cot, contract)

    @pl.when(core == 0)
    def _():
        for x in range(4):
            rows = slice(160 * x, 160 * x + 160)
            kept_ref[x, :, 0:640] = first[rows]
            kept_ref[x, :, 640:1280] = second[rows]

    @pl.when(core == 1)
    def _():
        for x in range(4):
            rows = slice(160 * x, 160 * x + 160)
            row, lane = 80 * (x % 2), 640 * (x // 2)
            parts = zip(low_high(first[rows]), low_high(second[rows]))
            for right, (a, b) in enumerate(parts):
                for upper in range(2):
                    cols = slice(320 * upper, 320 * upper + 320)
                    piece = jnp.concatenate([a[:, cols], b[:, cols]], axis=1)
                    kept_ref[2 * upper + right, row : row + 80, lane : lane + 640] = piece

    for m in range(4):
        index = jnp.where(core == 0, along_x(place_ref, m), along_y(place_ref, m))
        outs[m][...] = kept_ref[index]


def mlp(place, act, act_other, cot, cot_other, weight_in, weight_out):
    points, width = act.shape
    units = weight_in.shape[0]
    full = lambda shape: pl.BlockSpec(shape, lambda i, place: (0,) * len(shape))
    rows = pl.BlockSpec((4, None, 160, width), lambda i, place: (0, place[1], 0, 0))
    return pl.pallas_call(
        mlp_kernel,
        grid_spec=pltpu.PrefetchScalarGridSpec(
            num_scalar_prefetch=1,
            grid=(1,),
            in_specs=[full((points, width))] * 4 + [rows, rows],
            out_specs=[full((points, width))] * 2 + [full((160, 1280))] * 4,
            scratch_shapes=[pltpu.VMEM((4, 160, 1280), F32)],
        ),
        out_shape=[jax.ShapeDtypeStruct((points, width), F32)] * 2
        + [jax.ShapeDtypeStruct((160, 1280), F32)] * 4,
        compiler_params=params(57),
        cost_estimate=cost(30 * points * width * units, 12_000_000),
        name="mlp",
    )(
        place,
        act,
        act_other,
        cot,
        cot_other,
        weight_in.reshape(4, 2, 160, width),
        weight_out.reshape(4, 2, 160, width),
    )


def swap_kernel(place_ref, *refs):
    ins, outs, kept_ref = refs[:4], refs[4:8], refs[8]
    core = place_ref[1]
    total = (ins[0][...] + ins[1][...]) + (ins[2][...] + ins[3][...])

    @pl.when(core == 0)
    def _():
        for right, part in enumerate(low_high(total)):
            for upper in range(2):
                at = 320 * upper
                pair = [part[:, at : at + 320], part[:, 640 + at : 960 + at]]
                kept_ref[2 * upper + right] = jnp.concatenate(pair, axis=1)

    @pl.when(core == 1)
    def _():
        for x in range(4):
            row, col = 80 * (x % 2), 640 * (x // 2)
            kept_ref[x] = total[row : row + 80, col : col + 640]

    for m in range(4):
        index = jnp.where(core == 0, along_y(place_ref, m), along_x(place_ref, m))
        outs[m][...] = kept_ref[index]


def pair_kernel(place_ref, _, *refs):
    ins, (mine_ref, send_ref) = refs[:4], refs[4:]
    total = (ins[0][...] + ins[1][...]) + (ins[2][...] + ins[3][...])
    even = jnp.concatenate([total[:, 0:160], total[:, 320:480]], axis=1)
    odd = jnp.concatenate([total[:, 160:320], total[:, 480:640]], axis=1)
    first = place_ref[1] == 0
    mine_ref[...] = jnp.where(first, even, odd)
    send_ref[...] = jnp.where(first, odd, even)


def stack_kernel(place_ref, _, mine_ref, arrived_ref, *refs):
    outs, kept_ref = refs[:8], refs[8]
    first = place_ref[1] == 0
    mine, arrived = mine_ref[...], arrived_ref[...]
    below, above = jnp.where(first, mine, arrived), jnp.where(first, arrived, mine)
    for z in range(4):
        kept_ref[z, 0:20, :] = below[20 * z : 20 * z + 20]
        kept_ref[4 + z, 0:20, :] = above[20 * z : 20 * z + 20]
    for m in range(8):
        outs[m][...] = kept_ref[lax.rem(place_ref[5] + m, 8), 0:20, :]


def last_kernel(_, *refs):
    first_ref, second_ref = refs[8:]
    a, b, c, d = (refs[m][...] + refs[m + 4][...] for m in range(4))
    total = (a + b) + (c + d)
    first_ref[...] = total[:, 0:160]
    second_ref[...] = total[:, 160:320]


def small(
    kernel, operands, shapes, scalars=0, scratch=(), earlier=(), name=None, flops=0, piped=False
):
    def full(shape):
        return pl.BlockSpec(shape, lambda i: (0,) * len(shape))

    arrays = operands[scalars:]
    return pl.pallas_call(
        kernel,
        grid=(1,) if piped else (),
        in_specs=[pl.BlockSpec(memory_space=pltpu.SMEM)] * scalars
        + EARLIER * len(earlier)
        + ([full(array.shape) for array in arrays] if piped else whole(len(arrays))),
        out_specs=[full(shape) for shape in shapes] if piped else whole(len(shapes)),
        out_shape=[jax.ShapeDtypeStruct(shape, F32) for shape in shapes],
        scratch_shapes=scratch,
        compiler_params=params(57 if piped else 32),
        cost_estimate=cost(flops, 4_000_000) if flops else None,
        name=name,
    )(*operands[:scalars], *earlier, *arrays)


def permute(value, target):
    sizes = (2, 2, 4, 8, 2)
    order = lambda at: int(np.ravel_multi_index(at, sizes))
    pairs = [(order(at), order(target(*at))) for at in np.ndindex(*sizes)]
    return lax.ppermute(value, AXES, pairs)


def exchange(pieces, cores):
    def target(m, yl, co, x, z, yh):
        if cores[co] == "x":
            x = (x + m) % 4
        else:
            yl, yh = yl ^ (m >> 1), yh ^ (m & 1)
        return yl, co, x, z, yh

    return [pieces[0]] + [permute(pieces[m], functools.partial(target, m)) for m in (1, 2, 3)]


def exchange_z(pieces):
    far = (1, 7, 4, 3, 5, 2, 6)
    return [pieces[0]] + [
        lax.ppermute(pieces[m], "z", [(z, (z + m) % 8) for z in range(8)]) for m in far
    ]


def to_core(value):
    return lax.ppermute(value, "co", [(0, 1), (1, 0)])


def spectrum_kernel(
    place_ref, block_ref, top_ref, low_ref, _, out_ref, near_ref, cross_ref, mixing_ref, flat_ref
):
    for p in range(COLS // 2):
        pair = jnp.concatenate([block_ref[:, 2 * p, :], block_ref[:, 2 * p + 1, :]], axis=0)
        flat_ref[0:128, 128 * p : 128 * (p + 1)] = pair.T
    rest = [block_ref[:, 12 + q, :].T for q in range(3)]
    pieces = [rest[q][32 * g : 32 * (g + 1), :] for g in range(4) for q in range(3)]
    flat_ref[128:160, :] = jnp.concatenate(pieces, axis=1)
    result = dot3(split(flat_ref[...]), (top_ref[...], low_ref[...]), ((1,), (0,)))
    out_ref[...] = result
    mixing_ref[...] = jnp.sum(block_ref[:, 15, :], axis=0, keepdims=True)
    even = place_ref[1] == 0
    for r in range(OWN):
        first = result[ROWS * r : ROWS * r + 3, :]
        final = result[ROWS * r + 13 : ROWS * r + 16, :]
        near_ref[3 * r : 3 * r + 3, :] = jnp.where(even, final, first)
        cross_ref[3 * r : 3 * r + 3, :] = jnp.where(even, first, final)


def spectrum(place, block, earlier):
    top, low = forward_table(shard_order())
    rows = OWN * ROWS
    return pl.pallas_call(
        spectrum_kernel,
        in_specs=[pl.BlockSpec(memory_space=pltpu.SMEM)] + whole(3) + EARLIER,
        out_specs=whole(4),
        out_shape=[
            jax.ShapeDtypeStruct((rows, CIRCLE), F32),
            jax.ShapeDtypeStruct((3 * OWN, CIRCLE), F32),
            jax.ShapeDtypeStruct((3 * OWN, CIRCLE), F32),
            jax.ShapeDtypeStruct((1, 128), F32),
        ],
        scratch_shapes=[pltpu.VMEM((rows, CIRCLE), F32)],
        compiler_params=params(24),
        cost_estimate=cost(6 * rows * CIRCLE * CIRCLE, 4_000_000),
        name="spectrum",
    )(place, block, jnp.asarray(top), jnp.asarray(low), earlier)


def kernel_spectrum_kernel(kernel_ref, top_ref, low_ref, _, out_ref):
    out_ref[...] = dot3(split(kernel_ref[...]), (top_ref[...], low_ref[...]), ((1,), (0,)))


def kernel_spectrum(kernels, earlier):
    top, low = forward_table(np.arange(CIRCLE))
    rows = BASIS * TAPS * ROWS
    flat = kernels.transpose(0, 2, 1, 3).reshape(rows, CIRCLE)
    return pl.pallas_call(
        kernel_spectrum_kernel,
        in_specs=whole(3) + EARLIER,
        out_specs=whole(1)[0],
        out_shape=jax.ShapeDtypeStruct((rows, CIRCLE), F32),
        compiler_params=params(24),
        cost_estimate=cost(6 * rows * CIRCLE * CIRCLE, 5_000_000),
        name="kernel_spectrum",
    )(flat, jnp.asarray(top), jnp.asarray(low), earlier)


def filter_kernel(
    place_ref, mixing_ref, data_ref, near_ref, cross_ref, kernel_ref, top_ref, low_ref, *refs
):
    out_ref, rows_ref, sum_ref = refs[-3:]
    even = place_ref[1] == 0
    for r in range(OWN):
        near, cross = near_ref[3 * r : 3 * r + 3, :], cross_ref[3 * r : 3 * r + 3, :]
        rows_ref[r, 0:3, :] = jnp.where(even, cross, near)
        rows_ref[r, 3 : 3 + ROWS, :] = data_ref[ROWS * r : ROWS * (r + 1), :]
        rows_ref[r, 3 + ROWS : 6 + ROWS, :] = jnp.where(even, near, cross)
    lane = lax.broadcasted_iota(jnp.int32, (ROWS, HALF), 1)
    ends = lane == 0

    def channel(r, carry):
        real = jnp.zeros((ROWS, HALF), F32)
        imag = jnp.zeros((ROWS, HALF), F32)
        for k in range(TAPS):
            mixed_real = jnp.zeros((ROWS, HALF), F32)
            mixed_imag = jnp.zeros((ROWS, HALF), F32)
            for b in range(BASIS):
                weight = mixing_ref[0, BASIS * r + b]
                at = ROWS * (TAPS * b + k)
                mixed_real += weight * kernel_ref[at : at + ROWS, 0:HALF]
                mixed_imag += weight * kernel_ref[at : at + ROWS, HALF:CIRCLE]
            own = jnp.where(ends, mixed_imag, mixed_real)
            cross = jnp.where(ends, 0.0, mixed_imag)
            data_real = rows_ref[r, 6 - k : 6 - k + ROWS, 0:HALF]
            data_imag = rows_ref[r, 6 - k : 6 - k + ROWS, HALF:CIRCLE]
            real += mixed_real * data_real + cross * data_imag
            imag += own * data_imag - cross * data_real
        sum_ref[r, :, 0:HALF] = real
        sum_ref[r, :, HALF:CIRCLE] = imag
        return carry

    lax.fori_loop(0, OWN, channel, 0)
    total = split(sum_ref[...].reshape(OWN * ROWS, CIRCLE))
    field = dot3((top_ref[...], low_ref[...]), total, ((1,), (1,)))
    for l in range(COLS):
        out_ref[:, l, :] = field[SHARDS * l : SHARDS * (l + 1), 0:128]
    for q in range(3):
        pieces = [
            field[SHARDS * (3 * g + q) : SHARDS * (3 * g + q + 1), 128:160] for g in range(4)
        ]
        out_ref[:, 12 + q, :] = jnp.concatenate(pieces, axis=1)
    out_ref[:, 15, :] = jnp.zeros((SHARDS, 128), F32)


def filtered(place, mixing, data, near, cross, kernel, earlier):
    top, low = backward_table(shard_order())
    return pl.pallas_call(
        filter_kernel,
        in_specs=[pl.BlockSpec(memory_space=pltpu.SMEM)] * 2 + whole(6) + EARLIER,
        out_specs=whole(1)[0],
        out_shape=jax.ShapeDtypeStruct((SHARDS, 16, 128), F32),
        scratch_shapes=[
            pltpu.VMEM((OWN, 24, CIRCLE), F32),
            pltpu.VMEM((OWN, ROWS, CIRCLE), F32),
        ],
        compiler_params=params(32),
        cost_estimate=cost(6 * OWN * ROWS * CIRCLE * CIRCLE, 5_000_000),
        name="filter",
    )(place, mixing, data, near, cross, kernel, jnp.asarray(top), jnp.asarray(low), earlier)


def unpack_kernel(block_ref, out_ref, token_ref):
    token_ref[...] = jnp.zeros((8, 128), F32)

    def put(l, r, pair):
        out_ref[ROWS * l : ROWS * (l + 1), SHARDS * r : SHARDS * (r + 2)] = jnp.concatenate(
            pair, axis=1
        )

    for l in range(COLS):
        turned = block_ref[:, l, :].T
        for r in range(0, 8, 2):
            put(l, r, [turned[ROWS * r : ROWS * (r + 1)], turned[ROWS * (r + 1) : ROWS * (r + 2)]])
    for q in range(3):
        turned = block_ref[:, 12 + q, :].T
        for g in range(4):
            at = 32 * g
            put(3 * g + q, 8, [turned[at : at + ROWS], turned[at + ROWS : at + 2 * ROWS]])


def unpack(block):
    return pl.pallas_call(
        unpack_kernel,
        in_specs=whole(1),
        out_specs=whole(2),
        out_shape=[
            jax.ShapeDtypeStruct((ROWS * COLS, SHARDS * OWN), F32),
            jax.ShapeDtypeStruct((8, 128), F32),
        ],
        compiler_params=params(16),
        name="unpack",
    )(block)


def across(block):
    return lax.all_to_all(block, LON, split_axis=0, concat_axis=0, tiled=True)


def per_device(activation, cotangent, weight_in, weight_out, kernels, mixing):
    points = ROWS * COLS
    width = activation.shape[2]
    act = activation.transpose(1, 0, 2).reshape(points, width)
    cot = cotangent.transpose(1, 0, 2).reshape(points, width)
    place = jnp.stack([lax.axis_index(axis) for axis in (LON, "co", "yl", "yh", "x", "z")])
    unit, other, *pieces = mlp(place, act, to_core(act), cot, to_core(cot), weight_in, weight_out)
    operands = (place, mixing.T, unit, to_core(other))
    (block,) = small(pack_kernel, operands, [(SHARDS, 16, 128)], 2, name="pack", piped=True)
    moved = exchange(pieces, "xy")
    spread = across(block)
    kept = (pltpu.VMEM((4, 80, 640), F32),)
    swapped = small(swap_kernel, (place, *moved), [(80, 640)] * 4, 1, kept, (), "swap", 10**10, True)
    kernel = kernel_spectrum(kernels, swapped[0])
    moved = exchange(swapped, "yx")
    data, near, cross, own_mixing = spectrum(place, spread, kernel)
    near = to_core(near)
    cross = lax.ppermute(cross, LAT, [(1, 2), (2, 1)])
    mine, send = small(pair_kernel, (place, *moved), [(80, 320)] * 2, 1, (), (data,), "pair")
    paired = to_core(send)
    sent = filtered(place, own_mixing, data, near, cross, kernel, paired)
    result = across(sent)
    kept = (pltpu.VMEM((8, 24, 320), F32),)
    operands = (place, mine, paired)
    stacked = small(stack_kernel, operands, [(20, 320)] * 8, 1, kept, (sent,), "stack")
    flat, token = unpack(result)
    field = flat.reshape(COLS, ROWS, width).transpose(1, 0, 2)
    moved = exchange_z(stacked)
    grad_in, grad_out = small(last_kernel, moved, [(20, 160)] * 2, 0, (), (token,), "last")
    return (field, grad_in, grad_out)


def solution(mesh):
    fine = Mesh(mesh.devices.reshape(2, 2, 4, 8, 2), AXES)
    placed = (
        P(LAT, LON, None),
        P(LAT, LON, None),
        P(),
        P(),
        P(None, LAT, None, None),
        P(LON, None),
    )
    return jax.shard_map(
        per_device,
        mesh=fine,
        in_specs=placed,
        out_specs=(P(LAT, LON, None), P(LON, LAT), P(LON, LAT)),
        check_vma=False,
    )
```

```python
import functools
import math

import jax
import jax.numpy as jnp
import ml_dtypes
import numpy as np
from jax import lax
from jax.experimental import pallas as pl
from jax.experimental.pallas import tpu as pltpu
from jax.sharding import Mesh
from jax.sharding import PartitionSpec as P

AXES = ("yl", "co", "x", "z", "yh")
LAT = ("yl", "co")
LON = ("x", "z", "yh")
F32 = jnp.float32
BF16 = jnp.bfloat16
SHARDS = 64
COLS = 12
ROWS = 16
OWN = 10
CIRCLE = 768
HALF = 384
TAPS = 7
BASIS = 3
MIB = 1 << 20


def split(value):
    top = value.astype(BF16)
    return top, (value - top.astype(F32)).astype(BF16)


def dot3(left, right, dims):
    (a, b), (c, d) = left, right
    (at,), (to,) = dims
    return lax.dot_general(
        jnp.concatenate([a, b, a], axis=at),
        jnp.concatenate([c, c, d], axis=to),
        dimension_numbers=(dims, ((), ())),
        preferred_element_type=F32,
    )


def whole(n):
    return [pl.BlockSpec(memory_space=pltpu.VMEM)] * n


EARLIER = [pl.BlockSpec(memory_space=pl.ANY)]


def params(mib):
    return pltpu.CompilerParams(vmem_limit_bytes=mib * MIB)


def cost(flops, moved):
    return pl.CostEstimate(flops=flops, bytes_accessed=moved, transcendentals=0)


def table(order):
    angle = 2.0 * np.pi / CIRCLE * (order[:, None] * np.arange(HALF)[None, :] % CIRCLE)
    nyquist = np.where(order % 2 == 0, 1.0, -1.0)
    real, imag = np.cos(angle), -np.sin(angle)
    imag[:, 0] = nyquist
    return np.concatenate([real, imag], axis=1)


def parts(matrix):
    exact = matrix.astype(np.float32)
    top = exact.astype(ml_dtypes.bfloat16)
    return top, (exact - top.astype(np.float32)).astype(ml_dtypes.bfloat16)


def forward_table(order):
    return parts(table(order))


def backward_table(order):
    weight = np.full((2, HALF), 2.0 / CIRCLE)
    weight[:, 0] = 1.0 / CIRCLE
    return parts(table(order) * weight.reshape(1, -1))


def shard_order():
    return (np.arange(COLS)[:, None] + COLS * np.arange(SHARDS)[None, :]).reshape(-1)


def pack(unit, mixing_ref, shard, out_ref):
    def piece(l, r):
        return unit[ROWS * l : ROWS * (l + 1), SHARDS * r : SHARDS * (r + 1)]

    for l in range(COLS):
        out_ref[:, l, :] = jnp.concatenate([piece(l, r) for r in range(8)], axis=0).T
    for q in range(3):
        chunk = [piece(3 * g + q, r) for g in range(4) for r in (8, 9)]
        out_ref[:, 12 + q, :] = jnp.concatenate(chunk, axis=0).T
    target = lax.broadcasted_iota(jnp.int32, (SHARDS, 128), 0)
    lane = lax.broadcasted_iota(jnp.int32, (SHARDS, 128), 1)
    weights = jnp.zeros((SHARDS, 128), F32)
    for i in range(OWN):
        channel = OWN * shard + i
        here = target == lax.rem(channel, SHARDS)
        first = BASIS * lax.div(channel, SHARDS)
        for b in range(BASIS):
            weights = jnp.where(here & (lane == first + b), mixing_ref[b, i], weights)
    out_ref[:, 15, :] = weights


def pack_kernel(place_ref, mixing_ref, unit_ref, arrived_ref, block_ref):
    pack(unit_ref[...] + arrived_ref[...], mixing_ref, place_ref[0], block_ref)


def along_x(place_ref, m):
    return lax.rem(place_ref[4] + m, 4)


def along_y(place_ref, m):
    upper, right = place_ref[2], place_ref[3]
    return 2 * (1 - upper if m & 2 else upper) + (1 - right if m & 1 else right)


def low_high(rows):
    low = jnp.concatenate([rows[40 * z : 40 * z + 20] for z in range(4)], axis=0)
    high = jnp.concatenate([rows[40 * z + 20 : 40 * z + 40] for z in range(4)], axis=0)
    return low, high


def mlp_kernel(
    place_ref,
    act_ref,
    act_other_ref,
    cot_ref,
    cot_other_ref,
    in_ref,
    out_ref,
    own_ref,
    other_ref,
    *refs,
):
    outs, kept_ref = refs[:4], refs[4]
    core = place_ref[1]
    points = act_ref.shape[0]
    act = split(jnp.concatenate([act_ref[...], act_other_ref[...]], axis=0))
    cot = split(jnp.concatenate([cot_ref[...], cot_other_ref[...]], axis=0))
    w_in = split(in_ref[...].reshape(640, 640))
    w_out = split(out_ref[...].reshape(640, 640))
    preact = dot3(act, w_in, ((1,), (1,)))
    cdf = 0.5 * (1.0 + lax.erf(preact * (1.0 / math.sqrt(2.0))))
    density = jnp.exp(-0.5 * preact * preact) * (1.0 / math.sqrt(2.0 * math.pi))
    hidden = split(preact * cdf)
    slope = cdf + preact * density
    grad = split(dot3(cot, w_out, ((1,), (1,))) * slope)
    term = dot3(grad, w_in, ((1,), (0,)))
    own_ref[...] = cot_ref[...] + term[0:points]
    other_ref[...] = term[points:]
    contract = ((0,), (0,))
    first = dot3(grad, act, contract)
    second = dot3(hidden, cot, contract)

    @pl.when(core == 0)
    def _():
        for x in range(4):
            rows = slice(160 * x, 160 * x + 160)
            kept_ref[x, :, 0:640] = first[rows]
            kept_ref[x, :, 640:1280] = second[rows]

    @pl.when(core == 1)
    def _():
        for x in range(4):
            rows = slice(160 * x, 160 * x + 160)
            row, lane = 80 * (x % 2), 640 * (x // 2)
            parts = zip(low_high(first[rows]), low_high(second[rows]))
            for right, (a, b) in enumerate(parts):
                for upper in range(2):
                    cols = slice(320 * upper, 320 * upper + 320)
                    piece = jnp.concatenate([a[:, cols], b[:, cols]], axis=1)
                    kept_ref[2 * upper + right, row : row + 80, lane : lane + 640] = piece

    for m in range(4):
        index = jnp.where(core == 0, along_x(place_ref, m), along_y(place_ref, m))
        outs[m][...] = kept_ref[index]


def mlp(place, act, act_other, cot, cot_other, weight_in, weight_out):
    points, width = act.shape
    units = weight_in.shape[0]
    full = lambda shape: pl.BlockSpec(shape, lambda i, place: (0,) * len(shape))
    rows = pl.BlockSpec((4, None, 160, width), lambda i, place: (0, place[1], 0, 0))
    return pl.pallas_call(
        mlp_kernel,
        grid_spec=pltpu.PrefetchScalarGridSpec(
            num_scalar_prefetch=1,
            grid=(1,),
            in_specs=[full((points, width))] * 4 + [rows, rows],
            out_specs=[full((points, width))] * 2 + [full((160, 1280))] * 4,
            scratch_shapes=[pltpu.VMEM((4, 160, 1280), F32)],
        ),
        out_shape=[jax.ShapeDtypeStruct((points, width), F32)] * 2
        + [jax.ShapeDtypeStruct((160, 1280), F32)] * 4,
        compiler_params=params(57),
        cost_estimate=cost(30 * points * width * units, 12_000_000),
        name="mlp",
    )(
        place,
        act,
        act_other,
        cot,
        cot_other,
        weight_in.reshape(4, 2, 160, width),
        weight_out.reshape(4, 2, 160, width),
    )


def swap_kernel(place_ref, *refs):
    ins, outs, kept_ref = refs[:4], refs[4:8], refs[8]
    core = place_ref[1]
    total = (ins[0][...] + ins[1][...]) + (ins[2][...] + ins[3][...])

    @pl.when(core == 0)
    def _():
        for right, part in enumerate(low_high(total)):
            for upper in range(2):
                at = 320 * upper
                pair = [part[:, at : at + 320], part[:, 640 + at : 960 + at]]
                kept_ref[2 * upper + right] = jnp.concatenate(pair, axis=1)

    @pl.when(core == 1)
    def _():
        for x in range(4):
            row, col = 80 * (x % 2), 640 * (x // 2)
            kept_ref[x] = total[row : row + 80, col : col + 640]

    for m in range(4):
        index = jnp.where(core == 0, along_y(place_ref, m), along_x(place_ref, m))
        outs[m][...] = kept_ref[index]


def pair_kernel(place_ref, _, *refs):
    ins, (mine_ref, send_ref) = refs[:4], refs[4:]
    total = (ins[0][...] + ins[1][...]) + (ins[2][...] + ins[3][...])
    even = jnp.concatenate([total[:, 0:160], total[:, 320:480]], axis=1)
    odd = jnp.concatenate([total[:, 160:320], total[:, 480:640]], axis=1)
    first = place_ref[1] == 0
    mine_ref[...] = jnp.where(first, even, odd)
    send_ref[...] = jnp.where(first, odd, even)


def stack_kernel(place_ref, _, mine_ref, arrived_ref, *refs):
    outs, kept_ref = refs[:8], refs[8]
    first = place_ref[1] == 0
    mine, arrived = mine_ref[...], arrived_ref[...]
    below, above = jnp.where(first, mine, arrived), jnp.where(first, arrived, mine)
    for z in range(4):
        kept_ref[z, 0:20, :] = below[20 * z : 20 * z + 20]
        kept_ref[4 + z, 0:20, :] = above[20 * z : 20 * z + 20]
    for m in range(8):
        outs[m][...] = kept_ref[lax.rem(place_ref[5] + m, 8), 0:20, :]


def last_kernel(_, *refs):
    first_ref, second_ref = refs[8:]
    a, b, c, d = (refs[m][...] + refs[m + 4][...] for m in range(4))
    total = (a + b) + (c + d)
    first_ref[...] = total[:, 0:160]
    second_ref[...] = total[:, 160:320]


def small(
    kernel, operands, shapes, scalars=0, scratch=(), earlier=(), name=None, flops=0, piped=False
):
    def full(shape):
        return pl.BlockSpec(shape, lambda i: (0,) * len(shape))

    arrays = operands[scalars:]
    return pl.pallas_call(
        kernel,
        grid=(1,) if piped else (),
        in_specs=[pl.BlockSpec(memory_space=pltpu.SMEM)] * scalars
        + EARLIER * len(earlier)
        + ([full(array.shape) for array in arrays] if piped else whole(len(arrays))),
        out_specs=[full(shape) for shape in shapes] if piped else whole(len(shapes)),
        out_shape=[jax.ShapeDtypeStruct(shape, F32) for shape in shapes],
        scratch_shapes=scratch,
        compiler_params=params(57 if piped else 32),
        cost_estimate=cost(flops, 4_000_000) if flops else None,
        name=name,
    )(*operands[:scalars], *earlier, *arrays)


def permute(value, target):
    sizes = (2, 2, 4, 8, 2)
    order = lambda at: int(np.ravel_multi_index(at, sizes))
    pairs = [(order(at), order(target(*at))) for at in np.ndindex(*sizes)]
    return lax.ppermute(value, AXES, pairs)


def exchange(pieces, cores):
    def target(m, yl, co, x, z, yh):
        if cores[co] == "x":
            x = (x + m) % 4
        else:
            yl, yh = yl ^ (m >> 1), yh ^ (m & 1)
        return yl, co, x, z, yh

    return [pieces[0]] + [permute(pieces[m], functools.partial(target, m)) for m in (1, 2, 3)]


def exchange_z(pieces):
    far = (4, 3, 5, 1, 7, 2, 6)
    return [pieces[0]] + [
        lax.ppermute(pieces[m], "z", [(z, (z + m) % 8) for z in range(8)]) for m in far
    ]


def to_core(value):
    return lax.ppermute(value, "co", [(0, 1), (1, 0)])


def spectrum_kernel(
    place_ref, block_ref, top_ref, low_ref, _, out_ref, near_ref, cross_ref, mixing_ref, flat_ref
):
    for p in range(COLS // 2):
        pair = jnp.concatenate([block_ref[:, 2 * p, :], block_ref[:, 2 * p + 1, :]], axis=0)
        flat_ref[0:128, 128 * p : 128 * (p + 1)] = pair.T
    rest = [block_ref[:, 12 + q, :].T for q in range(3)]
    pieces = [rest[q][32 * g : 32 * (g + 1), :] for g in range(4) for q in range(3)]
    flat_ref[128:160, :] = jnp.concatenate(pieces, axis=1)
    result = dot3(split(flat_ref[...]), (top_ref[...], low_ref[...]), ((1,), (0,)))
    out_ref[...] = result
    mixing_ref[...] = jnp.sum(block_ref[:, 15, :], axis=0, keepdims=True)
    even = place_ref[1] == 0
    for r in range(OWN):
        first = result[ROWS * r : ROWS * r + 3, :]
        final = result[ROWS * r + 13 : ROWS * r + 16, :]
        near_ref[3 * r : 3 * r + 3, :] = jnp.where(even, final, first)
        cross_ref[3 * r : 3 * r + 3, :] = jnp.where(even, first, final)


def spectrum(place, block, earlier):
    top, low = forward_table(shard_order())
    rows = OWN * ROWS
    return pl.pallas_call(
        spectrum_kernel,
        in_specs=[pl.BlockSpec(memory_space=pltpu.SMEM)] + whole(3) + EARLIER,
        out_specs=whole(4),
        out_shape=[
            jax.ShapeDtypeStruct((rows, CIRCLE), F32),
            jax.ShapeDtypeStruct((3 * OWN, CIRCLE), F32),
            jax.ShapeDtypeStruct((3 * OWN, CIRCLE), F32),
            jax.ShapeDtypeStruct((1, 128), F32),
        ],
        scratch_shapes=[pltpu.VMEM((rows, CIRCLE), F32)],
        compiler_params=params(24),
        cost_estimate=cost(6 * rows * CIRCLE * CIRCLE, 4_000_000),
        name="spectrum",
    )(place, block, jnp.asarray(top), jnp.asarray(low), earlier)


def kernel_spectrum_kernel(kernel_ref, top_ref, low_ref, _, out_ref):
    out_ref[...] = dot3(split(kernel_ref[...]), (top_ref[...], low_ref[...]), ((1,), (0,)))


def kernel_spectrum(kernels, earlier):
    top, low = forward_table(np.arange(CIRCLE))
    rows = BASIS * TAPS * ROWS
    flat = kernels.transpose(0, 2, 1, 3).reshape(rows, CIRCLE)
    return pl.pallas_call(
        kernel_spectrum_kernel,
        in_specs=whole(3) + EARLIER,
        out_specs=whole(1)[0],
        out_shape=jax.ShapeDtypeStruct((rows, CIRCLE), F32),
        compiler_params=params(24),
        cost_estimate=cost(6 * rows * CIRCLE * CIRCLE, 5_000_000),
        name="kernel_spectrum",
    )(flat, jnp.asarray(top), jnp.asarray(low), earlier)


def filter_kernel(
    place_ref, mixing_ref, data_ref, near_ref, cross_ref, kernel_ref, top_ref, low_ref, *refs
):
    out_ref, rows_ref, sum_ref = refs[-3:]
    even = place_ref[1] == 0
    for r in range(OWN):
        near, cross = near_ref[3 * r : 3 * r + 3, :], cross_ref[3 * r : 3 * r + 3, :]
        rows_ref[r, 0:3, :] = jnp.where(even, cross, near)
        rows_ref[r, 3 : 3 + ROWS, :] = data_ref[ROWS * r : ROWS * (r + 1), :]
        rows_ref[r, 3 + ROWS : 6 + ROWS, :] = jnp.where(even, near, cross)
    lane = lax.broadcasted_iota(jnp.int32, (ROWS, HALF), 1)
    ends = lane == 0

    def channel(r, carry):
        real = jnp.zeros((ROWS, HALF), F32)
        imag = jnp.zeros((ROWS, HALF), F32)
        for k in range(TAPS):
            mixed_real = jnp.zeros((ROWS, HALF), F32)
            mixed_imag = jnp.zeros((ROWS, HALF), F32)
            for b in range(BASIS):
                weight = mixing_ref[0, BASIS * r + b]
                at = ROWS * (TAPS * b + k)
                mixed_real += weight * kernel_ref[at : at + ROWS, 0:HALF]
                mixed_imag += weight * kernel_ref[at : at + ROWS, HALF:CIRCLE]
            own = jnp.where(ends, mixed_imag, mixed_real)
            cross = jnp.where(ends, 0.0, mixed_imag)
            data_real = rows_ref[r, 6 - k : 6 - k + ROWS, 0:HALF]
            data_imag = rows_ref[r, 6 - k : 6 - k + ROWS, HALF:CIRCLE]
            real += mixed_real * data_real + cross * data_imag
            imag += own * data_imag - cross * data_real
        sum_ref[r, :, 0:HALF] = real
        sum_ref[r, :, HALF:CIRCLE] = imag
        return carry

    lax.fori_loop(0, OWN, channel, 0)
    total = split(sum_ref[...].reshape(OWN * ROWS, CIRCLE))
    field = dot3((top_ref[...], low_ref[...]), total, ((1,), (1,)))
    for l in range(COLS):
        out_ref[:, l, :] = field[SHARDS * l : SHARDS * (l + 1), 0:128]
    for q in range(3):
        pieces = [
            field[SHARDS * (3 * g + q) : SHARDS * (3 * g + q + 1), 128:160] for g in range(4)
        ]
        out_ref[:, 12 + q, :] = jnp.concatenate(pieces, axis=1)
    out_ref[:, 15, :] = jnp.zeros((SHARDS, 128), F32)


def filtered(place, mixing, data, near, cross, kernel, earlier):
    top, low = backward_table(shard_order())
    return pl.pallas_call(
        filter_kernel,
        in_specs=[pl.BlockSpec(memory_space=pltpu.SMEM)] * 2 + whole(6) + EARLIER,
        out_specs=whole(1)[0],
        out_shape=jax.ShapeDtypeStruct((SHARDS, 16, 128), F32),
        scratch_shapes=[
            pltpu.VMEM((OWN, 24, CIRCLE), F32),
            pltpu.VMEM((OWN, ROWS, CIRCLE), F32),
        ],
        compiler_params=params(32),
        cost_estimate=cost(6 * OWN * ROWS * CIRCLE * CIRCLE, 5_000_000),
        name="filter",
    )(place, mixing, data, near, cross, kernel, jnp.asarray(top), jnp.asarray(low), earlier)


def unpack_kernel(block_ref, out_ref, token_ref):
    token_ref[...] = jnp.zeros((8, 128), F32)

    def put(l, r, pair):
        out_ref[ROWS * l : ROWS * (l + 1), SHARDS * r : SHARDS * (r + 2)] = jnp.concatenate(
            pair, axis=1
        )

    for l in range(COLS):
        turned = block_ref[:, l, :].T
        for r in range(0, 8, 2):
            put(l, r, [turned[ROWS * r : ROWS * (r + 1)], turned[ROWS * (r + 1) : ROWS * (r + 2)]])
    for q in range(3):
        turned = block_ref[:, 12 + q, :].T
        for g in range(4):
            at = 32 * g
            put(3 * g + q, 8, [turned[at : at + ROWS], turned[at + ROWS : at + 2 * ROWS]])


def unpack(block):
    return pl.pallas_call(
        unpack_kernel,
        in_specs=whole(1),
        out_specs=whole(2),
        out_shape=[
            jax.ShapeDtypeStruct((ROWS * COLS, SHARDS * OWN), F32),
            jax.ShapeDtypeStruct((8, 128), F32),
        ],
        compiler_params=params(16),
        name="unpack",
    )(block)


def across(block):
    return lax.all_to_all(block, LON, split_axis=0, concat_axis=0, tiled=True)


def per_device(activation, cotangent, weight_in, weight_out, kernels, mixing):
    points = ROWS * COLS
    width = activation.shape[2]
    act = activation.transpose(1, 0, 2).reshape(points, width)
    cot = cotangent.transpose(1, 0, 2).reshape(points, width)
    place = jnp.stack([lax.axis_index(axis) for axis in (LON, "co", "yl", "yh", "x", "z")])
    unit, other, *pieces = mlp(place, act, to_core(act), cot, to_core(cot), weight_in, weight_out)
    operands = (place, mixing.T, unit, to_core(other))
    (block,) = small(pack_kernel, operands, [(SHARDS, 16, 128)], 2, name="pack", piped=True)
    moved = exchange(pieces, "xy")
    spread = across(block)
    kept = (pltpu.VMEM((4, 80, 640), F32),)
    swapped = small(swap_kernel, (place, *moved), [(80, 640)] * 4, 1, kept, (), "swap", 10**10, True)
    kernel = kernel_spectrum(kernels, swapped[0])
    moved = exchange(swapped, "yx")
    data, near, cross, own_mixing = spectrum(place, spread, kernel)
    near = to_core(near)
    cross = lax.ppermute(cross, LAT, [(1, 2), (2, 1)])
    mine, send = small(pair_kernel, (place, *moved), [(80, 320)] * 2, 1, (), (data,), "pair")
    paired = to_core(send)
    sent = filtered(place, own_mixing, data, near, cross, kernel, paired)
    result = across(sent)
    kept = (pltpu.VMEM((8, 24, 320), F32),)
    operands = (place, mine, paired)
    stacked = small(stack_kernel, operands, [(20, 320)] * 8, 1, kept, (sent,), "stack")
    flat, token = unpack(result)
    field = flat.reshape(COLS, ROWS, width).transpose(1, 0, 2)
    moved = exchange_z(stacked)
    grad_in, grad_out = small(last_kernel, moved, [(20, 160)] * 2, 0, (), (token,), "last")
    return (field, grad_in, grad_out)


def solution(mesh):
    fine = Mesh(mesh.devices.reshape(2, 2, 4, 8, 2), AXES)
    placed = (
        P(LAT, LON, None),
        P(LAT, LON, None),
        P(),
        P(),
        P(None, LAT, None, None),
        P(LON, None),
    )
    return jax.shard_map(
        per_device,
        mesh=fine,
        in_specs=placed,
        out_specs=(P(LAT, LON, None), P(LON, LAT), P(LON, LAT)),
        check_vma=False,
    )
```

```python
import functools
import math

import jax
import jax.numpy as jnp
import ml_dtypes
import numpy as np
from jax import lax
from jax.experimental import pallas as pl
from jax.experimental.pallas import tpu as pltpu
from jax.sharding import Mesh
from jax.sharding import PartitionSpec as P

AXES = ("yl", "co", "x", "z", "yh")
LAT = ("yl", "co")
LON = ("x", "z", "yh")
F32 = jnp.float32
BF16 = jnp.bfloat16
SHARDS = 64
COLS = 12
ROWS = 16
OWN = 10
CIRCLE = 768
HALF = 384
TAPS = 7
BASIS = 3
MIB = 1 << 20


def split(value):
    top = value.astype(BF16)
    return top, (value - top.astype(F32)).astype(BF16)


def dot3(left, right, dims):
    (a, b), (c, d) = left, right
    (at,), (to,) = dims
    return lax.dot_general(
        jnp.concatenate([a, b, a], axis=at),
        jnp.concatenate([c, c, d], axis=to),
        dimension_numbers=(dims, ((), ())),
        preferred_element_type=F32,
    )


def whole(n):
    return [pl.BlockSpec(memory_space=pltpu.VMEM)] * n


EARLIER = [pl.BlockSpec(memory_space=pl.ANY)]


def params(mib):
    return pltpu.CompilerParams(vmem_limit_bytes=mib * MIB)


def cost(flops, moved):
    return pl.CostEstimate(flops=flops, bytes_accessed=moved, transcendentals=0)


def table(order):
    angle = 2.0 * np.pi / CIRCLE * (order[:, None] * np.arange(HALF)[None, :] % CIRCLE)
    nyquist = np.where(order % 2 == 0, 1.0, -1.0)
    real, imag = np.cos(angle), -np.sin(angle)
    imag[:, 0] = nyquist
    return np.concatenate([real, imag], axis=1)


def parts(matrix):
    exact = matrix.astype(np.float32)
    top = exact.astype(ml_dtypes.bfloat16)
    return top, (exact - top.astype(np.float32)).astype(ml_dtypes.bfloat16)


def forward_table(order):
    return parts(table(order))


def backward_table(order):
    weight = np.full((2, HALF), 2.0 / CIRCLE)
    weight[:, 0] = 1.0 / CIRCLE
    return parts(table(order) * weight.reshape(1, -1))


def shard_order():
    return (np.arange(COLS)[:, None] + COLS * np.arange(SHARDS)[None, :]).reshape(-1)


def pack(unit, mixing_ref, shard, out_ref):
    def piece(l, r):
        return unit[ROWS * l : ROWS * (l + 1), SHARDS * r : SHARDS * (r + 1)]

    for l in range(COLS):
        out_ref[:, l, :] = jnp.concatenate([piece(l, r) for r in range(8)], axis=0).T
    for q in range(3):
        chunk = [piece(3 * g + q, r) for g in range(4) for r in (8, 9)]
        out_ref[:, 12 + q, :] = jnp.concatenate(chunk, axis=0).T
    target = lax.broadcasted_iota(jnp.int32, (SHARDS, 128), 0)
    lane = lax.broadcasted_iota(jnp.int32, (SHARDS, 128), 1)
    weights = jnp.zeros((SHARDS, 128), F32)
    for i in range(OWN):
        channel = OWN * shard + i
        here = target == lax.rem(channel, SHARDS)
        first = BASIS * lax.div(channel, SHARDS)
        for b in range(BASIS):
            weights = jnp.where(here & (lane == first + b), mixing_ref[b, i], weights)
    out_ref[:, 15, :] = weights


def pack_kernel(place_ref, mixing_ref, unit_ref, arrived_ref, block_ref):
    pack(unit_ref[...] + arrived_ref[...], mixing_ref, place_ref[0], block_ref)


def along_x(place_ref, m):
    return lax.rem(place_ref[4] + m, 4)


def along_y(place_ref, m):
    upper, right = place_ref[2], place_ref[3]
    return 2 * (1 - upper if m & 2 else upper) + (1 - right if m & 1 else right)


def low_high(rows):
    low = jnp.concatenate([rows[40 * z : 40 * z + 20] for z in range(4)], axis=0)
    high = jnp.concatenate([rows[40 * z + 20 : 40 * z + 40] for z in range(4)], axis=0)
    return low, high


def mlp_kernel(
    place_ref,
    act_ref,
    act_other_ref,
    cot_ref,
    cot_other_ref,
    in_ref,
    out_ref,
    own_ref,
    other_ref,
    *refs,
):
    outs, kept_ref = refs[:4], refs[4]
    core = place_ref[1]
    points = act_ref.shape[0]
    act = split(jnp.concatenate([act_ref[...], act_other_ref[...]], axis=0))
    cot = split(jnp.concatenate([cot_ref[...], cot_other_ref[...]], axis=0))
    w_in = split(in_ref[...].reshape(640, 640))
    w_out = split(out_ref[...].reshape(640, 640))
    preact = dot3(act, w_in, ((1,), (1,)))
    cdf = 0.5 * (1.0 + lax.erf(preact * (1.0 / math.sqrt(2.0))))
    density = jnp.exp(-0.5 * preact * preact) * (1.0 / math.sqrt(2.0 * math.pi))
    hidden = split(preact * cdf)
    slope = cdf + preact * density
    grad = split(dot3(cot, w_out, ((1,), (1,))) * slope)
    term = dot3(grad, w_in, ((1,), (0,)))
    own_ref[...] = cot_ref[...] + term[0:points]
    other_ref[...] = term[points:]
    contract = ((0,), (0,))
    first = dot3(grad, act, contract)
    second = dot3(hidden, cot, contract)

    @pl.when(core == 0)
    def _():
        for x in range(4):
            rows = slice(160 * x, 160 * x + 160)
            kept_ref[x, :, 0:640] = first[rows]
            kept_ref[x, :, 640:1280] = second[rows]

    @pl.when(core == 1)
    def _():
        for x in range(4):
            rows = slice(160 * x, 160 * x + 160)
            row, lane = 80 * (x % 2), 640 * (x // 2)
            parts = zip(low_high(first[rows]), low_high(second[rows]))
            for right, (a, b) in enumerate(parts):
                for upper in range(2):
                    cols = slice(320 * upper, 320 * upper + 320)
                    piece = jnp.concatenate([a[:, cols], b[:, cols]], axis=1)
                    kept_ref[2 * upper + right, row : row + 80, lane : lane + 640] = piece

    for m in range(4):
        index = jnp.where(core == 0, along_x(place_ref, m), along_y(place_ref, m))
        outs[m][...] = kept_ref[index]


def mlp(place, act, act_other, cot, cot_other, weight_in, weight_out):
    points, width = act.shape
    units = weight_in.shape[0]
    full = lambda shape: pl.BlockSpec(shape, lambda i, place: (0,) * len(shape))
    rows = pl.BlockSpec((4, None, 160, width), lambda i, place: (0, place[1], 0, 0))
    return pl.pallas_call(
        mlp_kernel,
        grid_spec=pltpu.PrefetchScalarGridSpec(
            num_scalar_prefetch=1,
            grid=(1,),
            in_specs=[full((points, width))] * 4 + [rows, rows],
            out_specs=[full((points, width))] * 2 + [full((160, 1280))] * 4,
            scratch_shapes=[pltpu.VMEM((4, 160, 1280), F32)],
        ),
        out_shape=[jax.ShapeDtypeStruct((points, width), F32)] * 2
        + [jax.ShapeDtypeStruct((160, 1280), F32)] * 4,
        compiler_params=params(57),
        cost_estimate=cost(30 * points * width * units, 12_000_000),
        name="mlp",
    )(
        place,
        act,
        act_other,
        cot,
        cot_other,
        weight_in.reshape(4, 2, 160, width),
        weight_out.reshape(4, 2, 160, width),
    )


def swap_kernel(place_ref, *refs):
    ins, outs, kept_ref = refs[:4], refs[4:8], refs[8]
    core = place_ref[1]
    total = (ins[0][...] + ins[1][...]) + (ins[2][...] + ins[3][...])

    @pl.when(core == 0)
    def _():
        for right, part in enumerate(low_high(total)):
            for upper in range(2):
                at = 320 * upper
                pair = [part[:, at : at + 320], part[:, 640 + at : 960 + at]]
                kept_ref[2 * upper + right] = jnp.concatenate(pair, axis=1)

    @pl.when(core == 1)
    def _():
        for x in range(4):
            row, col = 80 * (x % 2), 640 * (x // 2)
            kept_ref[x] = total[row : row + 80, col : col + 640]

    for m in range(4):
        index = jnp.where(core == 0, along_y(place_ref, m), along_x(place_ref, m))
        outs[m][...] = kept_ref[index]


def pair_kernel(place_ref, _, *refs):
    ins, (mine_ref, send_ref) = refs[:4], refs[4:]
    total = (ins[0][...] + ins[1][...]) + (ins[2][...] + ins[3][...])
    even = jnp.concatenate([total[:, 0:160], total[:, 320:480]], axis=1)
    odd = jnp.concatenate([total[:, 160:320], total[:, 480:640]], axis=1)
    first = place_ref[1] == 0
    mine_ref[...] = jnp.where(first, even, odd)
    send_ref[...] = jnp.where(first, odd, even)


def stack_kernel(place_ref, _, mine_ref, arrived_ref, *refs):
    outs, kept_ref = refs[:8], refs[8]
    first = place_ref[1] == 0
    mine, arrived = mine_ref[...], arrived_ref[...]
    below, above = jnp.where(first, mine, arrived), jnp.where(first, arrived, mine)
    for z in range(4):
        kept_ref[z, 0:20, :] = below[20 * z : 20 * z + 20]
        kept_ref[4 + z, 0:20, :] = above[20 * z : 20 * z + 20]
    for m in range(8):
        outs[m][...] = kept_ref[lax.rem(place_ref[5] + m, 8), 0:20, :]


def last_kernel(_, *refs):
    first_ref, second_ref = refs[8:]
    a, b, c, d = (refs[m][...] + refs[m + 4][...] for m in range(4))
    total = (a + b) + (c + d)
    first_ref[...] = total[:, 0:160]
    second_ref[...] = total[:, 160:320]


def small(
    kernel, operands, shapes, scalars=0, scratch=(), earlier=(), name=None, flops=0, piped=False
):
    def full(shape):
        return pl.BlockSpec(shape, lambda i: (0,) * len(shape))

    arrays = operands[scalars:]
    return pl.pallas_call(
        kernel,
        grid=(1,) if piped else (),
        in_specs=[pl.BlockSpec(memory_space=pltpu.SMEM)] * scalars
        + EARLIER * len(earlier)
        + ([full(array.shape) for array in arrays] if piped else whole(len(arrays))),
        out_specs=[full(shape) for shape in shapes] if piped else whole(len(shapes)),
        out_shape=[jax.ShapeDtypeStruct(shape, F32) for shape in shapes],
        scratch_shapes=scratch,
        compiler_params=params(57 if piped else 32),
        cost_estimate=cost(flops, 4_000_000) if flops else None,
        name=name,
    )(*operands[:scalars], *earlier, *arrays)


def permute(value, target):
    sizes = (2, 2, 4, 8, 2)
    order = lambda at: int(np.ravel_multi_index(at, sizes))
    pairs = [(order(at), order(target(*at))) for at in np.ndindex(*sizes)]
    return lax.ppermute(value, AXES, pairs)


def exchange(pieces, cores):
    def target(m, yl, co, x, z, yh):
        if cores[co] == "x":
            x = (x + m) % 4
        else:
            yl, yh = yl ^ (m >> 1), yh ^ (m & 1)
        return yl, co, x, z, yh

    return [pieces[0]] + [permute(pieces[m], functools.partial(target, m)) for m in (1, 2, 3)]


def exchange_z(pieces):
    far = (1, 7, 4, 3, 5, 2, 6)
    return [pieces[0]] + [
        lax.ppermute(pieces[m], "z", [(z, (z + m) % 8) for z in range(8)]) for m in far
    ]


def to_core(value):
    return lax.ppermute(value, "co", [(0, 1), (1, 0)])


def spectrum_kernel(
    place_ref, block_ref, top_ref, low_ref, _, out_ref, near_ref, cross_ref, mixing_ref, flat_ref
):
    for p in range(COLS // 2):
        pair = jnp.concatenate([block_ref[:, 2 * p, :], block_ref[:, 2 * p + 1, :]], axis=0)
        flat_ref[0:128, 128 * p : 128 * (p + 1)] = pair.T
    rest = [block_ref[:, 12 + q, :].T for q in range(3)]
    pieces = [rest[q][32 * g : 32 * (g + 1), :] for g in range(4) for q in range(3)]
    flat_ref[128:160, :] = jnp.concatenate(pieces, axis=1)
    result = dot3(split(flat_ref[...]), (top_ref[...], low_ref[...]), ((1,), (0,)))
    out_ref[...] = result
    mixing_ref[...] = jnp.sum(block_ref[:, 15, :], axis=0, keepdims=True)
    even = place_ref[1] == 0
    for r in range(OWN):
        first = result[ROWS * r : ROWS * r + 3, :]
        final = result[ROWS * r + 13 : ROWS * r + 16, :]
        near_ref[3 * r : 3 * r + 3, :] = jnp.where(even, final, first)
        cross_ref[3 * r : 3 * r + 3, :] = jnp.where(even, first, final)


def spectrum(place, block, earlier):
    top, low = forward_table(shard_order())
    rows = OWN * ROWS
    return pl.pallas_call(
        spectrum_kernel,
        in_specs=[pl.BlockSpec(memory_space=pltpu.SMEM)] + whole(3) + EARLIER,
        out_specs=whole(4),
        out_shape=[
            jax.ShapeDtypeStruct((rows, CIRCLE), F32),
            jax.ShapeDtypeStruct((3 * OWN, CIRCLE), F32),
            jax.ShapeDtypeStruct((3 * OWN, CIRCLE), F32),
            jax.ShapeDtypeStruct((1, 128), F32),
        ],
        scratch_shapes=[pltpu.VMEM((rows, CIRCLE), F32)],
        compiler_params=params(24),
        cost_estimate=cost(6 * rows * CIRCLE * CIRCLE, 4_000_000),
        name="spectrum",
    )(place, block, jnp.asarray(top), jnp.asarray(low), earlier)


def kernel_spectrum_kernel(kernel_ref, top_ref, low_ref, _, out_ref):
    out_ref[...] = dot3(split(kernel_ref[...]), (top_ref[...], low_ref[...]), ((1,), (0,)))


def kernel_spectrum(kernels, earlier):
    top, low = forward_table(np.arange(CIRCLE))
    rows = BASIS * TAPS * ROWS
    flat = kernels.transpose(0, 2, 1, 3).reshape(rows, CIRCLE)
    return pl.pallas_call(
        kernel_spectrum_kernel,
        in_specs=whole(3) + EARLIER,
        out_specs=whole(1)[0],
        out_shape=jax.ShapeDtypeStruct((rows, CIRCLE), F32),
        compiler_params=params(24),
        cost_estimate=cost(6 * rows * CIRCLE * CIRCLE, 5_000_000),
        name="kernel_spectrum",
    )(flat, jnp.asarray(top), jnp.asarray(low), earlier)


def filter_kernel(
    place_ref, mixing_ref, data_ref, near_ref, cross_ref, kernel_ref, top_ref, low_ref, *refs
):
    out_ref, rows_ref, sum_ref = refs[-3:]
    even = place_ref[1] == 0
    for r in range(OWN):
        near, cross = near_ref[3 * r : 3 * r + 3, :], cross_ref[3 * r : 3 * r + 3, :]
        rows_ref[r, 0:3, :] = jnp.where(even, cross, near)
        rows_ref[r, 3 : 3 + ROWS, :] = data_ref[ROWS * r : ROWS * (r + 1), :]
        rows_ref[r, 3 + ROWS : 6 + ROWS, :] = jnp.where(even, near, cross)
    lane = lax.broadcasted_iota(jnp.int32, (ROWS, HALF), 1)
    ends = lane == 0

    def channel(r, carry):
        real = jnp.zeros((ROWS, HALF), F32)
        imag = jnp.zeros((ROWS, HALF), F32)
        for k in range(TAPS):
            mixed_real = jnp.zeros((ROWS, HALF), F32)
            mixed_imag = jnp.zeros((ROWS, HALF), F32)
            for b in range(BASIS):
                weight = mixing_ref[0, BASIS * r + b]
                at = ROWS * (TAPS * b + k)
                mixed_real += weight * kernel_ref[at : at + ROWS, 0:HALF]
                mixed_imag += weight * kernel_ref[at : at + ROWS, HALF:CIRCLE]
            own = jnp.where(ends, mixed_imag, mixed_real)
            cross = jnp.where(ends, 0.0, mixed_imag)
            data_real = rows_ref[r, 6 - k : 6 - k + ROWS, 0:HALF]
            data_imag = rows_ref[r, 6 - k : 6 - k + ROWS, HALF:CIRCLE]
            real += mixed_real * data_real + cross * data_imag
            imag += own * data_imag - cross * data_real
        sum_ref[r, :, 0:HALF] = real
        sum_ref[r, :, HALF:CIRCLE] = imag
        return carry

    lax.fori_loop(0, OWN, channel, 0)
    total = split(sum_ref[...].reshape(OWN * ROWS, CIRCLE))
    field = dot3((top_ref[...], low_ref[...]), total, ((1,), (1,)))
    for l in range(COLS):
        out_ref[:, l, :] = field[SHARDS * l : SHARDS * (l + 1), 0:128]
    for q in range(3):
        pieces = [
            field[SHARDS * (3 * g + q) : SHARDS * (3 * g + q + 1), 128:160] for g in range(4)
        ]
        out_ref[:, 12 + q, :] = jnp.concatenate(pieces, axis=1)
    out_ref[:, 15, :] = jnp.zeros((SHARDS, 128), F32)


def filtered(place, mixing, data, near, cross, kernel, earlier):
    top, low = backward_table(shard_order())
    return pl.pallas_call(
        filter_kernel,
        in_specs=[pl.BlockSpec(memory_space=pltpu.SMEM)] * 2 + whole(6) + EARLIER,
        out_specs=whole(1)[0],
        out_shape=jax.ShapeDtypeStruct((SHARDS, 16, 128), F32),
        scratch_shapes=[
            pltpu.VMEM((OWN, 24, CIRCLE), F32),
            pltpu.VMEM((OWN, ROWS, CIRCLE), F32),
        ],
        compiler_params=params(32),
        cost_estimate=cost(6 * OWN * ROWS * CIRCLE * CIRCLE, 5_000_000),
        name="filter",
    )(place, mixing, data, near, cross, kernel, jnp.asarray(top), jnp.asarray(low), earlier)


def unpack_kernel(block_ref, out_ref, token_ref):
    token_ref[...] = jnp.zeros((8, 128), F32)

    def put(l, r, pair):
        out_ref[ROWS * l : ROWS * (l + 1), SHARDS * r : SHARDS * (r + 2)] = jnp.concatenate(
            pair, axis=1
        )

    for l in range(COLS):
        turned = block_ref[:, l, :].T
        for r in range(0, 8, 2):
            put(l, r, [turned[ROWS * r : ROWS * (r + 1)], turned[ROWS * (r + 1) : ROWS * (r + 2)]])
    for q in range(3):
        turned = block_ref[:, 12 + q, :].T
        for g in range(4):
            at = 32 * g
            put(3 * g + q, 8, [turned[at : at + ROWS], turned[at + ROWS : at + 2 * ROWS]])


def unpack(block):
    return pl.pallas_call(
        unpack_kernel,
        in_specs=whole(1),
        out_specs=whole(2),
        out_shape=[
            jax.ShapeDtypeStruct((ROWS * COLS, SHARDS * OWN), F32),
            jax.ShapeDtypeStruct((8, 128), F32),
        ],
        compiler_params=params(16),
        name="unpack",
    )(block)


def across(block):
    return lax.all_to_all(block, LON, split_axis=0, concat_axis=0, tiled=True)


def per_device(activation, cotangent, weight_in, weight_out, kernels, mixing):
    points = ROWS * COLS
    width = activation.shape[2]
    act = activation.transpose(1, 0, 2).reshape(points, width)
    cot = cotangent.transpose(1, 0, 2).reshape(points, width)
    place = jnp.stack([lax.axis_index(axis) for axis in (LON, "co", "yl", "yh", "x", "z")])
    unit, other, *pieces = mlp(place, act, to_core(act), cot, to_core(cot), weight_in, weight_out)
    operands = (place, mixing.T, unit, to_core(other))
    (block,) = small(pack_kernel, operands, [(SHARDS, 16, 128)], 2, name="pack")
    moved = exchange(pieces, "xy")
    spread = across(block)
    kept = (pltpu.VMEM((4, 80, 640), F32),)
    swapped = small(swap_kernel, (place, *moved), [(80, 640)] * 4, 1, kept, (), "swap", 10**10, True)
    kernel = kernel_spectrum(kernels, swapped[0])
    moved = exchange(swapped, "yx")
    data, near, cross, own_mixing = spectrum(place, spread, kernel)
    near = to_core(near)
    cross = lax.ppermute(cross, LAT, [(1, 2), (2, 1)])
    mine, send = small(pair_kernel, (place, *moved), [(80, 320)] * 2, 1, (), (data,), "pair")
    paired = to_core(send)
    sent = filtered(place, own_mixing, data, near, cross, kernel, paired)
    result = across(sent)
    kept = (pltpu.VMEM((8, 24, 320), F32),)
    operands = (place, mine, paired)
    stacked = small(stack_kernel, operands, [(20, 320)] * 8, 1, kept, (sent,), "stack")
    flat, token = unpack(result)
    field = flat.reshape(COLS, ROWS, width).transpose(1, 0, 2)
    moved = exchange_z(stacked)
    grad_in, grad_out = small(last_kernel, moved, [(20, 160)] * 2, 0, (), (token,), "last")
    return (field, grad_in, grad_out)


def solution(mesh):
    fine = Mesh(mesh.devices.reshape(2, 2, 4, 8, 2), AXES)
    placed = (
        P(LAT, LON, None),
        P(LAT, LON, None),
        P(),
        P(),
        P(None, LAT, None, None),
        P(LON, None),
    )
    return jax.shard_map(
        per_device,
        mesh=fine,
        in_specs=placed,
        out_specs=(P(LAT, LON, None), P(LON, LAT), P(LON, LAT)),
        check_vma=False,
    )
```
